32 devices in a mesh: gz: 4 (over y, core), gy: 8 (over z, x).
Axes of the slice: x: 2, y: 2, z: 4, core: 2. Of those that a mesh axis runs over, the one named last changes fastest.
Arguments:
- input_field: float32 [32, 16, 64, 256], P(None, 'gz', 'gy'), may hold values from -6 to 6
- pre_activation: float32 [32, 16, 64, 256], P(None, 'gz', 'gy'), may hold values from -8 to 8
- cotangent: float32 [32, 16, 64, 256], P(None, 'gz', 'gy'), may hold values from -6 to 6
- spectral_weights: float32 [2, 16, 32, 32, 32, 32], P(None, None, 'gz', 'gy'), may hold values from -4.2426405 to 4.2426405
- mix_weights: float32 [32, 32], replicated, may hold values from -1 to 1
- coefficients: float32 [5, 32], replicated, may hold values from -3 to 3
Outputs:
- grad_input: float32 [32, 16, 64, 256], P(None, 'gz', 'gy')
- grad_spectral: float32 [2, 16, 32, 32, 32, 32], P(None, None, 'gz', 'gy')
- grad_mix: float32 [32, 32], replicated
- grad_coef: float32 [5, 32], replicated
The draws below stay inside these ranges and needn't reach their ends.
All inputs are finite; a program needn't handle non-finite values.
Results may differ from the reference program's by a relative error of at most 0.00013.
Values sent between devices are 32-bit elements; how exact they have to be, the bound alone decides.
No kernel may reach another device: no remote copies, remote signals or barrier semaphores. Data moves between devices by JAX's collectives and lax.ppermute only.
A program may use at most 192 MiB of HBM per device.

```python
import math
import jax
import jax.numpy as jnp
from jax import lax

C = 32
X = 256
KX = 32
KY = 32
KZ = 16
Y = 64
Z = 16
CELLS = 262144


def block_scale(stream_key, dims, cuts, least, largest):
    factor_of, own = 1.0, jax.random.fold_in(stream_key, 6)
    for axis_at, parts in cuts:
        heights = jnp.exp(jax.random.uniform(jax.random.fold_in(own, axis_at), (parts,), jnp.float32, least / len(cuts), largest / len(cuts)))
        factor_of = factor_of * jnp.repeat(heights, dims[axis_at] // parts).reshape([-1 if axis == axis_at else 1 for axis in range(len(dims))])
    return factor_of


def scatter_about(own_key, dims, width, reach, split=(), kind=jnp.bfloat16):
    factor_of = block_scale(own_key, dims, split, -0.22, 0.18) if split else 1.0
    array = jax.random.normal(own_key, dims, jnp.float32) * width * factor_of
    return jnp.minimum(jnp.maximum(array, -reach), reach).astype(kind)


def setup_inputs(seed: int = 0) -> dict:
    streams_of = jax.random.split(jax.random.key(seed), 7)
    input_field = scatter_about(streams_of[0], (C, Z, Y, X), 1.0, 6.0, ((1, 4), (2, 8)), jnp.float32)
    pre_activation = scatter_about(streams_of[1], (C, Z, Y, X), 1.5, 8.0, ((1, 4), (2, 8)), jnp.float32)
    cotangent = scatter_about(streams_of[2], (C, Z, Y, X), 1.0, 6.0, ((1, 4), (2, 8)), jnp.float32)
    spectral_weights = scatter_about(streams_of[3], (2, KZ, KY, KX, C, C), (4.0 / C ** 0.5), 4.2426405, ((2, 4), (3, 8)), jnp.float32)
    mix_weights = scatter_about(streams_of[4], (C, C), C ** -0.5, 1.0, (), jnp.float32)
    coefficients = scatter_about(streams_of[5], (5, C), 0.5, 3.0, (), jnp.float32)
    return {"input_field": input_field, "pre_activation": pre_activation, "cotangent": cotangent, "spectral_weights": spectral_weights, "mix_weights": mix_weights, "coefficients": coefficients}


HIGHEST_PRECISION = lax.Precision.HIGHEST


def gelu_slope(values):
    normal_cdf = 0.5 * (1.0 + jax.scipy.special.erf(values * 0.7071067811865476))
    return normal_cdf + values * jnp.exp(-0.5 * values * values) * 0.3989422804014327


def mode_numbers(number):
    positions = jnp.arange(number, dtype=jnp.int32)
    return jnp.where(positions < number // 2, positions, positions - number).astype(jnp.int32)


def twiddle(cell_index, mode_index, period):
    product = jnp.remainder(cell_index[:, None] * mode_index[None, :], period).astype(jnp.float32)
    angles = product * (2.0 * math.pi / period)
    return jnp.cos(angles), jnp.sin(angles)


def rotate_pair(pair, cos_table, sin_table, formula, inverse):
    real_cos = jnp.einsum(formula, pair[0], cos_table, precision=HIGHEST_PRECISION)
    real_sin = jnp.einsum(formula, pair[0], sin_table, precision=HIGHEST_PRECISION)
    imag_cos = jnp.einsum(formula, pair[1], cos_table, precision=HIGHEST_PRECISION)
    imag_sin = jnp.einsum(formula, pair[1], sin_table, precision=HIGHEST_PRECISION)
    if inverse:
        return jnp.stack([real_cos - imag_sin, imag_cos + real_sin])
    return jnp.stack([real_cos + imag_sin, imag_cos - real_sin])


def mixing(hat_input, hat_slope, weights):
    outer = 'oljk,cljk->ljkoc'
    grad_re = jnp.einsum(outer, hat_slope[0], hat_input[0]) + jnp.einsum(outer, hat_slope[1], hat_input[1])
    grad_im = jnp.einsum(outer, hat_slope[1], hat_input[0]) - jnp.einsum(outer, hat_slope[0], hat_input[1])
    inner = 'ljkoc,oljk->cljk'
    dual_re = jnp.einsum(inner, weights[0], hat_slope[0], precision=HIGHEST_PRECISION) + jnp.einsum(inner, weights[1], hat_slope[1], precision=HIGHEST_PRECISION)
    dual_im = jnp.einsum(inner, weights[0], hat_slope[1], precision=HIGHEST_PRECISION) - jnp.einsum(inner, weights[1], hat_slope[0], precision=HIGHEST_PRECISION)
    return jnp.stack([grad_re, grad_im]), jnp.stack([dual_re, dual_im])


def neighbours(padded):
    return [padded[:, 1:-1, 1:-1], padded[:, 1:-1, 2:], padded[:, 1:-1, :-2], padded[:, 2:, 1:-1], padded[:, :-2, 1:-1]]


def adjoint_rims(padded):
    return [padded[:, 1:-1, 1:-1], padded[:, 1:-1, :-2], padded[:, 1:-1, 2:], padded[:, :-2, 1:-1], padded[:, 2:, 1:-1]]


def weighted(coefficients, pieces):
    total = coefficients[0][:, None, None, None] * pieces[0]
    for place in range(1, 5):
        total = total + coefficients[place][:, None, None, None] * pieces[place]
    return total


def tables():
    cos_x, sin_x = twiddle(jnp.arange(X, dtype=jnp.int32), mode_numbers(KX), X)
    cos_y, sin_y = twiddle(jnp.arange(Y, dtype=jnp.int32), mode_numbers(KY), Y)
    cos_z, sin_z = twiddle(jnp.arange(Z, dtype=jnp.int32), mode_numbers(KZ), Z)
    return cos_x, sin_x, cos_y, sin_y, cos_z, sin_z


def spectrum(values):
    cos_x, sin_x, cos_y, sin_y, cos_z, sin_z = tables()
    pair = jnp.stack([jnp.einsum('czyx,xk->czyk', values, cos_x, precision=HIGHEST_PRECISION),
                      -jnp.einsum('czyx,xk->czyk', values, sin_x, precision=HIGHEST_PRECISION)])
    pair = rotate_pair(pair, cos_y, sin_y, 'czyk,yj->czjk', False)
    return rotate_pair(pair, cos_z, sin_z, 'czjk,zl->cljk', False)


def reference(input_field, pre_activation, cotangent, spectral_weights, mix_weights, coefficients):
    slope_field = cotangent * gelu_slope(pre_activation)
    hat_input = spectrum(input_field)
    hat_slope = spectrum(slope_field) / CELLS
    grad_spectral, dual = mixing(hat_input, hat_slope, spectral_weights)
    cos_x, sin_x, cos_y, sin_y, cos_z, sin_z = tables()
    returned = rotate_pair(dual, cos_z, sin_z, 'cljk,zl->czjk', True)
    returned = rotate_pair(returned, cos_y, sin_y, 'czjk,yj->czyk', True)
    spectral_part = jnp.einsum('czyk,xk->czyx', returned[0], cos_x, precision=HIGHEST_PRECISION) - jnp.einsum('czyk,xk->czyx', returned[1], sin_x, precision=HIGHEST_PRECISION)
    pad_width = ((0, 0), (1, 1), (1, 1), (0, 0))
    pieces = neighbours(jnp.pad(input_field, pad_width))
    stencil = weighted(coefficients, pieces)
    hidden = jnp.einsum('oc,ozyx->czyx', mix_weights, slope_field, precision=HIGHEST_PRECISION)
    grad_mix = jnp.einsum('ozyx,czyx->oc', slope_field, stencil, precision=HIGHEST_PRECISION) / 1024.0
    grad_coef = jnp.stack([jnp.sum(hidden * piece, axis=(1, 2, 3)) for piece in pieces]) / 1024.0
    grad_input = weighted(coefficients, adjoint_rims(jnp.pad(hidden, pad_width))) + spectral_part
    return grad_input, grad_spectral, grad_mix, grad_coef
```

```python
import functools
import math

import jax
import jax.numpy as jnp
import numpy as np
from jax import lax
from jax.experimental import pallas as pl
from jax.experimental.pallas import tpu as pltpu
from jax.sharding import PartitionSpec as P

PRECISION = lax.Precision.HIGH
MIB = 1 << 20
SUB = 8
LANES = 128


def dot(left, right, dims=((1,), (0,)), precision=PRECISION):
    return lax.dot_general(
        left, right, (dims, ((), ())), precision=precision, preferred_element_type=jnp.float32
    )


def call(body, outs, operands, limit_mib, flops, bytes_accessed, scratch=(), **grid):
    return pl.pallas_call(
        body,
        out_shape=outs,
        scratch_shapes=list(scratch),
        compiler_params=pltpu.CompilerParams(vmem_limit_bytes=limit_mib * MIB),
        cost_estimate=pl.CostEstimate(
            flops=flops, bytes_accessed=bytes_accessed, transcendentals=0
        ),
        **grid,
    )(*operands)


def f32(*shape):
    return jax.ShapeDtypeStruct(shape, jnp.float32)


def mode_numbers(number):
    positions = np.arange(number)
    return np.where(positions < number // 2, positions, positions - number)


def angles(cells, modes):
    product = np.mod(np.arange(cells)[:, None] * mode_numbers(modes)[None, :], cells)
    return product * (2.0 * math.pi / cells)


def table_x(cells, modes):
    theta = angles(cells, modes)
    pair = np.stack([np.cos(theta), -np.sin(theta)], axis=2)
    return pair.reshape(cells, 2 * modes).astype(np.float32)


def wide_columns(table):
    spare = -table.shape[1] % LANES
    return np.pad(table, ((0, 0), (0, spare)))


def table_rows(cells, modes):
    theta = angles(cells, modes).T
    cos, sin = np.cos(theta), np.sin(theta)
    return np.block([[cos, sin], [-sin, cos]]).astype(np.float32)


def order_z(groups, depth):
    part, cell = np.meshgrid(np.arange(2), np.arange(groups * depth), indexing="ij")
    index = (part * groups * depth + cell).reshape(2, groups, depth)
    return index.transpose(1, 0, 2).reshape(-1)


def gelu_slope(values):
    normal_cdf = 0.5 * (1.0 + lax.erf(values * 0.7071067811865476))
    return normal_cdf + values * jnp.exp(-0.5 * values * values) * 0.3989422804014327


def x_kernel(sizes, in_ref, pre_ref, cot_ref, tab_ref, slope_ref, send_ref, ylast_ref, yfirst_ref,
             zlast_ref, zfirst_ref, work_ref, half_ref):
    C, zl, yl, dests, kr = sizes
    slope = cot_ref[...] * gelu_slope(pre_ref[...])
    slope_ref[...] = slope
    for f in range(2):
        field = in_ref[...] if f == 0 else slope
        work_ref[f] = dot(field, tab_ref[...])
        for y in range(yl):
            rows = [work_ref[f, pl.ds(z * yl + y, C, stride=zl * yl), :] for z in range(zl)]
            turned = jnp.concatenate(rows, axis=0).T
            for d in range(dests):
                send_ref[pl.ds(((d * 2 + f) * yl + y) * kr, kr), :] = turned[d * kr : (d + 1) * kr]
    for half in range(slope_ref.shape[1] // LANES):
        cut = pl.ds(half * LANES, LANES)
        half_ref[...] = slope[:, half * LANES : (half + 1) * LANES]
        for z in range(zl):
            to = pl.ds(z * C, C)
            ylast_ref[to, cut] = half_ref[pl.ds(z * yl + yl - 1, C, stride=zl * yl), :]
            yfirst_ref[to, cut] = half_ref[pl.ds(z * yl, C, stride=zl * yl), :]
    for c in range(C):
        zlast_ref[pl.ds(c * yl, yl), :] = slope_ref[pl.ds((c * zl + zl - 1) * yl, yl), :]
        zfirst_ref[pl.ds(c * yl, yl), :] = slope_ref[pl.ds(c * zl * yl, yl), :]


def widen(values, lanes):
    spare = lanes - values.shape[1]
    if spare == 0:
        return values
    return jnp.concatenate([values, jnp.zeros((values.shape[0], spare), jnp.float32)], axis=1)


def y_kernel(sizes, recv_ref, tab_ref, send_ref):
    C, zl, kxl, ky, kyl, yl, sources = sizes
    kr = 2 * kxl
    lanes = zl * C
    pieces = []
    for kx in range(kxl):
        for f in range(2):
            pieces.append(
                jnp.concatenate(
                    [
                        recv_ref[pl.ds((s * 2 + f) * yl * kr + kx * 2 + r, yl, stride=kr), :]
                        for r in range(2)
                        for s in range(sources)
                    ],
                    axis=0,
                )
            )
    out = dot(tab_ref[...], jnp.concatenate(pieces, axis=1))
    for f in range(2):
        for r in range(2):
            for z in range(zl):
                parts = []
                for kx in range(kxl):
                    base = (kx * 2 + f) * lanes + z * C
                    parts.append(out[r * ky : (r + 1) * ky, base : base + C])
                block = widen(jnp.concatenate(parts, axis=1), send_ref.shape[1])
                for g in range(ky // kyl):
                    start = (g * 2 + f) * kyl * 2 * zl + r * zl + z
                    send_ref[pl.ds(start, kyl, stride=2 * zl), :] = block[g * kyl : (g + 1) * kyl]


def spread(rows, C, kxl, eye, ones):
    n = rows.shape[0]
    high = rows.astype(jnp.bfloat16).astype(jnp.float32)
    both = jnp.concatenate([high, rows - high], axis=1)
    wide = jnp.broadcast_to(both[:, None, :], (n, C, both.shape[1]))
    wide = wide * eye[None]
    wide = wide.reshape(n * C, both.shape[1]).astype(jnp.bfloat16)
    return dot(wide, ones, precision=None)


def z_kernel(sizes, recv_ref, tab_ref, inv_ref, eye_ref, ones_ref, weights_ref, part_ref,
             send_ref, hat_ref):
    C, zl, kxl, kyl, kz, groups, part_rows, scale = sizes
    kc = kxl * C
    rows = 2 * zl
    chunk = kyl * rows
    wide = send_ref.shape[1]
    cols = []
    for k in range(kyl):
        for f in range(2):
            cols.append(
                jnp.concatenate(
                    [
                        recv_ref[pl.ds((s * 2 + f) * chunk + k * rows, rows), :]
                        for s in range(groups)
                    ],
                    axis=0,
                )
            )
    hat = dot(tab_ref[...], jnp.concatenate(cols, axis=1))
    eye, ones = eye_ref[...], ones_ref[...]
    for k in range(kyl):
        base = k * 2 * wide
        hat_ref[k, 0] = hat[:, base : base + kc]
        slope_hat = hat[:, base + wide : base + wide + kc] * scale
        hat_ref[k, 1] = slope_hat
        each = spread(slope_hat, C, kxl, eye, ones).reshape(2, kz, C, kc)
        w_re, w_im = weights_ref[0, :, k], weights_ref[1, :, k]
        re = w_re * each[0] + w_im * each[1]
        im = w_re * each[1] - w_im * each[0]
        dual = jnp.stack([re, im]).reshape(2, kz, C // SUB, SUB, kc)
        dual = jnp.sum(dual, axis=2).reshape(2 * kz * SUB, kc)
        back = widen(dot(inv_ref[...], dual), wide)
        for g in range(groups):
            send_ref[pl.ds(g * (chunk + part_rows) + k * rows, rows), :] = back[
                g * rows : (g + 1) * rows
            ]
    for g in range(groups):
        send_ref[pl.ds(g * (chunk + part_rows) + chunk, part_rows), :] = part_ref[...]


def grad_kernel(sizes, hat_ref, eye_ref, ones_ref, out_ref):
    C, kxl, kyl, kz = sizes
    kc = kxl * C
    step = pl.program_id(0)
    for k in range(kyl):
        in_re, in_im = hat_ref[k, 0, pl.ds(step, 1), :], hat_ref[k, 0, pl.ds(kz + step, 1), :]
        both = jnp.concatenate(
            [hat_ref[k, 1, pl.ds(step, 1), :], hat_ref[k, 1, pl.ds(kz + step, 1), :]], axis=0
        )
        wide = spread(both, C, kxl, eye_ref[...], ones_ref[...])
        re, im = wide[:C], wide[C:]
        grad_re = re * in_re + im * in_im
        grad_im = im * in_re - re * in_im
        for kx in range(kxl):
            out_ref[0, 0, k, kx] = grad_re[:, kx * C : (kx + 1) * C]
            out_ref[1, 0, k, kx] = grad_im[:, kx * C : (kx + 1) * C]


def pack_kernel(sizes, in_ref, out_ref):
    kxl, kyl = sizes
    for part in range(2):
        for k in range(kyl):
            out_ref[part, 0, k] = jnp.concatenate(
                [in_ref[part, 0, k, kx] for kx in range(kxl)], axis=1
            )


def y_back_kernel(sizes, recv_ref, tab_ref, send_ref):
    C, zl, kxl, ky, kyl, cells, yl, groups, dests, part_rows = sizes
    wide = recv_ref.shape[1]
    rows = 2 * zl
    kr = 2 * kxl
    chunk = kyl * rows + part_rows
    out_chunk = yl * kr + part_rows
    cols = []
    for z in range(zl):
        cols.append(
            jnp.concatenate(
                [
                    recv_ref[pl.ds(s * chunk + r * zl + z, kyl, stride=rows), :]
                    for r in range(2)
                    for s in range(groups)
                ],
                axis=0,
            )
        )
    out = dot(tab_ref[...], jnp.concatenate(cols, axis=1))
    total = recv_ref[pl.ds(kyl * rows, part_rows), :]
    for s in range(1, groups):
        total = total + recv_ref[pl.ds(s * chunk + kyl * rows, part_rows), :]
    for kx in range(kxl):
        for r in range(2):
            block = out[r * cells : (r + 1) * cells]
            piece = jnp.concatenate(
                [block[:, z * wide + kx * C : z * wide + (kx + 1) * C] for z in range(zl)], axis=1
            )
            for d in range(dests):
                send_ref[pl.ds(d * out_chunk + kx * 2 + r, yl, stride=kr), :] = piece[
                    d * yl : (d + 1) * yl
                ]
    for d in range(dests):
        send_ref[pl.ds(d * out_chunk + yl * kr, part_rows), :] = total


def x_back_kernel(sizes, recv_ref, tab_ref, local_ref, out_ref, mix_ref, coef_ref, work_ref):
    C, zl, yl, kxl, sources, part_rows = sizes
    kr = 2 * kxl
    chunk = yl * kr + part_rows
    for y in range(yl):
        column = jnp.concatenate(
            [recv_ref[pl.ds(s * chunk + y * kr, kr), :] for s in range(sources)], axis=0
        )
        value = dot(column.T, tab_ref[...])
        for z in range(zl):
            for half in range(value.shape[1] // LANES):
                work_ref[half, pl.ds(z * yl + y, C, stride=zl * yl), :] = value[
                    z * C : (z + 1) * C, half * LANES : (half + 1) * LANES
                ]
    for half in range(out_ref.shape[1] // LANES):
        cut = pl.ds(half * LANES, LANES)
        out_ref[:, cut] = work_ref[half] + local_ref[:, cut]
    total = recv_ref[pl.ds(yl * kr, part_rows), :]
    for s in range(1, sources):
        total = total + recv_ref[pl.ds(s * chunk + yl * kr, part_rows), :]
    total = total * (1.0 / 1024.0)
    high = C // kxl
    for b in range(kxl):
        mix_ref[pl.ds(b * high, high), :] = total[:high, b * C : (b + 1) * C]
    coef_ref[...] = total[high : high + 5, :C]


def local_kernel(sizes, in_ref, slope_ref, ybefore_ref, yafter_ref, zbefore_ref, zafter_ref,
                 kron_y_ref, kron_z_ref, coef_y_ref, coef_z_ref, sum_y_ref, sum_z_ref, same_y_ref,
                 same_z_ref, out_ref, part_ref):
    C, zl, yl, kxl = sizes
    length = in_ref.shape[1]

    def layer(ref, z):
        return jnp.concatenate(
            [ref[pl.ds((c * zl + z) * yl, yl), :] for c in range(C)], axis=0
        )

    def row_of(layers, y):
        return jnp.concatenate([each.reshape(C, yl, length)[:, y] for each in layers], axis=0)

    def up(values, edge):
        cube = values.reshape(C, yl, length)
        return jnp.concatenate([edge[:, None, :], cube[:, : yl - 1]], axis=1).reshape(
            C * yl, length
        )

    def down(values, edge):
        cube = values.reshape(C, yl, length)
        return jnp.concatenate([cube[:, 1:], edge[:, None, :]], axis=1).reshape(C * yl, length)

    coef = [coef_y_ref[:, j : j + 1] for j in range(5)]
    kron_y = kron_y_ref[...]
    slopes = [layer(slope_ref, z) for z in range(zl)]
    hidden = [dot(kron_y, zbefore_ref[...])]
    hidden += [dot(kron_y, slopes[z]) for z in range(zl)]
    hidden += [dot(kron_y, zafter_ref[...])]
    before = dot(kron_z_ref[...], ybefore_ref[...]).reshape(zl, C, length)
    after = dot(kron_z_ref[...], yafter_ref[...]).reshape(zl, C, length)
    inputs = [layer(in_ref, z) for z in range(zl)]
    nothing = jnp.zeros((C, length), jnp.float32)
    gram = None
    sums = [None] * 5
    for z in range(zl):
        shifted = [
            hidden[z + 1],
            up(hidden[z + 1], before[z]),
            down(hidden[z + 1], after[z]),
            hidden[z],
            hidden[z + 2],
        ]
        total = coef[0] * shifted[0]
        for j in range(1, 5):
            total = total + coef[j] * shifted[j]
        for c in range(C):
            out_ref[pl.ds((c * zl + z) * yl, yl), :] = total[c * yl : (c + 1) * yl]
        for j in range(5):
            term = inputs[z] * shifted[j]
            sums[j] = term if sums[j] is None else sums[j] + term
        stencil = (
            coef[0] * inputs[z]
            + coef[1] * down(inputs[z], nothing)
            + coef[2] * up(inputs[z], nothing)
        )
        if z + 1 < zl:
            stencil = stencil + coef[3] * inputs[z + 1]
        if z > 0:
            stencil = stencil + coef[4] * inputs[z - 1]
        term = dot(slopes[z], stencil, ((1,), (1,)))
        gram = term if gram is None else gram + term
    gram = gram + dot(zbefore_ref[...], coef[3] * inputs[0], ((1,), (1,)))
    gram = gram + dot(zafter_ref[...], coef[4] * inputs[zl - 1], ((1,), (1,)))
    edge = dot(ybefore_ref[...], coef_z_ref[:, 1:2] * row_of(inputs, 0), ((1,), (1,)))
    edge = edge + dot(yafter_ref[...], coef_z_ref[:, 2:3] * row_of(inputs, yl - 1), ((1,), (1,)))
    mix = dot(dot(sum_y_ref[...], gram * same_y_ref[...]), sum_y_ref[...], ((1,), (1,)))
    mix = mix + dot(dot(sum_z_ref[...], edge * same_z_ref[...]), sum_z_ref[...], ((1,), (1,)))
    columns = [jnp.sum(term, axis=1, keepdims=True) for term in sums]
    columns = jnp.concatenate(
        columns + [jnp.zeros((C * yl, SUB - 5), jnp.float32)], axis=1
    )
    eye = (
        lax.broadcasted_iota(jnp.int32, (SUB, SUB), 0)
        == lax.broadcasted_iota(jnp.int32, (SUB, SUB), 1)
    ).astype(jnp.float32)
    by_channel = dot(sum_y_ref[...], columns)
    coefs = dot(eye, by_channel, ((1,), (1,)))
    high = C // kxl
    packed = jnp.concatenate([mix[b * high : (b + 1) * high] for b in range(kxl)], axis=1)
    part_ref[pl.ds(0, high), :] = widen(packed, part_ref.shape[1])
    part_ref[pl.ds(high, SUB), :] = widen(coefs, part_ref.shape[1])


def per_device(input_field, pre_activation, cotangent, spectral_weights, mix_weights, coefficients):
    C, zl, yl, length = input_field.shape
    groups_y = lax.axis_size("gy")
    groups_z = lax.axis_size("gz")
    cells_y, cells_z = yl * groups_y, zl * groups_z
    kz, kyl, kxl = spectral_weights.shape[1:4]
    modes_y, modes_x = kyl * groups_z, kxl * groups_y
    scale = 1.0 / (length * cells_y * cells_z)
    rows = C * zl * yl
    kr = 2 * kxl
    kc = kxl * C
    lanes = zl * C
    wide = max(kc, LANES)
    part_rows = C // kxl + SUB

    tab_x = table_x(length, modes_x)
    tab_y = table_rows(cells_y, modes_y)
    z_rows = order_z(groups_z, zl)
    tab_z = table_rows(cells_z, kz)[:, z_rows]
    inv_z = np.repeat(table_rows(cells_z, kz).T[z_rows], SUB, axis=1)
    inv_y = np.ascontiguousarray(tab_y.T)
    inv_x = np.ascontiguousarray(tab_x.T)
    eye = np.tile(np.eye(C, dtype=np.float32), (1, 2 * kxl))
    ones = np.tile(np.kron(np.eye(kxl), np.ones((C, C))), (2, 1)).astype(jnp.bfloat16)

    flat = lambda values: values.reshape(rows, length)
    exchange = functools.partial(lax.all_to_all, split_axis=0, concat_axis=0, tiled=True)

    slope, send, ylast, yfirst, zlast, zfirst = call(
        functools.partial(x_kernel, (C, zl, yl, groups_y, kr)),
        (
            f32(rows, length),
            f32(groups_y * 2 * yl * kr, lanes),
            f32(C * zl, length),
            f32(C * zl, length),
            f32(C * yl, length),
            f32(C * yl, length),
        ),
        (flat(input_field), flat(pre_activation), flat(cotangent), jnp.asarray(wide_columns(tab_x))),
        24,
        flops=4 * rows * length * 2 * modes_x,
        bytes_accessed=6 * rows * length * 4,
        scratch=[
            pltpu.VMEM((2, rows, wide_columns(tab_x).shape[1]), jnp.float32),
            pltpu.VMEM((rows, LANES), jnp.float32),
        ],
    )
    lines = exchange(send, "gy")

    def from_below(values, axis):
        return lax.ppermute(values, axis, [(i, i + 1) for i in range(lax.axis_size(axis) - 1)])

    def from_above(values, axis):
        return lax.ppermute(values, axis, [(i + 1, i) for i in range(lax.axis_size(axis) - 1)])

    ybefore, yafter = from_below(ylast, "gy"), from_above(yfirst, "gy")
    zbefore, zafter = from_below(zlast, "gz"), from_above(zfirst, "gz")

    weights = call(
        functools.partial(pack_kernel, (kxl, kyl)),
        f32(2, kz, kyl, C, kc),
        (spectral_weights,),
        16,
        flops=2 * kz * kyl * C * kc,
        bytes_accessed=2 * kz * kyl * kxl * C * 128 * 4 * 2,
        grid=(kz,),
        in_specs=[pl.BlockSpec((2, 1, kyl, kxl, C, C), lambda i: (0, i, 0, 0, 0, 0))],
        out_specs=pl.BlockSpec((2, 1, kyl, C, kc), lambda i: (0, i, 0, 0, 0)),
    )

    send = call(
        functools.partial(y_kernel, (C, zl, kxl, modes_y, kyl, yl, groups_y)),
        f32(groups_z * 2 * kyl * 2 * zl, wide),
        (lines, jnp.asarray(tab_y)),
        16,
        flops=16 * modes_y * cells_y * kxl * lanes,
        bytes_accessed=4 * MIB,
    )
    owned = exchange(send, "gz")

    coef_rows = jnp.pad(coefficients.T, ((0, 0), (0, SUB - 5)))
    mixed = mix_weights.T
    local, part = call(
        functools.partial(local_kernel, (C, zl, yl, kxl)),
        (f32(rows, length), f32(part_rows, wide)),
        (
            flat(input_field),
            slope,
            ybefore,
            yafter,
            zbefore,
            zafter,
            jnp.kron(mixed, jnp.eye(yl, dtype=jnp.float32)),
            jnp.kron(jnp.eye(zl, dtype=jnp.float32), mixed),
            jnp.repeat(coef_rows, yl, axis=0),
            jnp.tile(coef_rows, (zl, 1)),
            jnp.asarray(np.repeat(np.eye(C, dtype=np.float32), yl, axis=1)),
            jnp.asarray(np.tile(np.eye(C, dtype=np.float32), (1, zl))),
            jnp.asarray(np.tile(np.eye(yl, dtype=np.float32), (C, C))),
            jnp.asarray(np.kron(np.eye(zl, dtype=np.float32), np.ones((C, C), np.float32))),
        ),
        32,
        flops=2 * 12 * (C * yl) ** 2 * length,
        bytes_accessed=6 * MIB,
    )

    chunk = kyl * 2 * zl + part_rows
    send, hats = call(
        functools.partial(z_kernel, (C, zl, kxl, kyl, kz, groups_z, part_rows, scale)),
        (f32(groups_z * chunk, wide), f32(kyl, 2, 2 * kz, kc)),
        (
            owned,
            jnp.asarray(tab_z),
            jnp.asarray(inv_z),
            jnp.asarray(eye),
            jnp.asarray(ones),
            weights,
            part,
        ),
        32,
        flops=16 * kz * kyl * C * kc,
        bytes_accessed=6 * MIB,
    )
    returned = exchange(send, "gz")

    grad_spectral = call(
        functools.partial(grad_kernel, (C, kxl, kyl, kz)),
        f32(2, kz, kyl, kxl, C, C),
        (hats, jnp.asarray(eye), jnp.asarray(ones)),
        16,
        flops=16 * kz * kyl * C * kc,
        bytes_accessed=2 * kz * kyl * kxl * C * 128 * 4,
        grid=(kz,),
        in_specs=[
            pl.BlockSpec((kyl, 2, 2 * kz, kc), lambda i: (0, 0, 0, 0)),
            pl.BlockSpec((C, 2 * kc), lambda i: (0, 0)),
            pl.BlockSpec((2 * kc, kc), lambda i: (0, 0)),
        ],
        out_specs=pl.BlockSpec((2, 1, kyl, kxl, C, C), lambda i: (0, i, 0, 0, 0, 0)),
    )

    send = call(
        functools.partial(
            y_back_kernel,
            (C, zl, kxl, modes_y, kyl, cells_y, yl, groups_z, groups_y, part_rows),
        ),
        f32(groups_y * (yl * kr + part_rows), lanes),
        (returned, jnp.asarray(inv_y)),
        16,
        flops=8 * modes_y * cells_y * kxl * lanes,
        bytes_accessed=2 * MIB,
    )
    arrived = exchange(send, "gy")

    grad_input, grad_mix, grad_coef = call(
        functools.partial(x_back_kernel, (C, zl, yl, kxl, groups_y, part_rows)),
        (f32(rows, length), f32(C, C), f32(5, C)),
        (arrived, jnp.asarray(inv_x), local),
        16,
        flops=2 * rows * length * 2 * modes_x,
        bytes_accessed=3 * MIB,
        scratch=[pltpu.VMEM((length // LANES, rows, LANES), jnp.float32)],
    )
    return (grad_input.reshape(input_field.shape), grad_spectral, grad_mix, grad_coef)


def solution(mesh):
    in_specs = (
        P(None, "gz", "gy", None),
        P(None, "gz", "gy", None),
        P(None, "gz", "gy", None),
        P(None, None, "gz", "gy", None, None),
        P(),
        P(),
    )
    out_specs = (P(None, "gz", "gy", None), P(None, None, "gz", "gy", None, None), P(), P())
    return jax.shard_map(
        per_device, mesh=mesh, in_specs=in_specs, out_specs=out_specs, check_vma=False
    )
```

```python
import functools
import math

import jax
import jax.numpy as jnp
import numpy as np
from jax import lax
from jax.experimental import pallas as pl
from jax.experimental.pallas import tpu as pltpu
from jax.sharding import PartitionSpec as P

PRECISION = lax.Precision.HIGH
MIB = 1 << 20
SUB = 8
LANES = 128


def dot(left, right, dims=((1,), (0,)), precision=PRECISION):
    return lax.dot_general(
        left, right, (dims, ((), ())), precision=precision, preferred_element_type=jnp.float32
    )


def call(body, outs, operands, limit_mib, flops, bytes_accessed, scratch=(), **grid):
    return pl.pallas_call(
        body,
        out_shape=outs,
        scratch_shapes=list(scratch),
        compiler_params=pltpu.CompilerParams(vmem_limit_bytes=limit_mib * MIB),
        cost_estimate=pl.CostEstimate(
            flops=flops, bytes_accessed=bytes_accessed, transcendentals=0
        ),
        **grid,
    )(*operands)


def f32(*shape):
    return jax.ShapeDtypeStruct(shape, jnp.float32)


def vmem(*shape):
    return pltpu.VMEM(shape, jnp.float32)


def far_out(*shape):
    return pltpu.HBM(shape, jnp.float32)


def hbm(values):
    return pltpu.with_memory_space_constraint(values, pltpu.HBM)


def held(values):
    return pltpu.with_memory_space_constraint(values, pltpu.VMEM)


def iota(shape, axis):
    return lax.broadcasted_iota(jnp.int32, shape, axis)


SERIES = [(-1.0) ** n * (2.0 * math.pi) ** (2 * n) / math.factorial(2 * n) for n in range(10)]


def cos_turns(turns):
    part = turns - jnp.floor(turns + 0.5)
    size = jnp.abs(part)
    flip = size > 0.25
    part = jnp.where(flip, 0.5 - size, size)
    square = part * part
    total = jnp.full_like(square, SERIES[-1])
    for factor in SERIES[-2::-1]:
        total = total * square + factor
    return jnp.where(flip, -total, total)


def mode_of(position, modes):
    return jnp.where(position < modes // 2, position, position - modes)


def turns_of(cell, mode, cells, quarter):
    return (cell * mode).astype(jnp.float32) * (1.0 / cells) - 0.25 * quarter.astype(jnp.float32)


def split(index, size):
    high = index // size
    return high, index - high * size


def table_x(cells, modes, mode_axis, columns=None):
    shape = [cells, cells]
    shape[mode_axis] = columns or 2 * modes
    mode, part = split(iota(tuple(shape), mode_axis), 2)
    value = cos_turns(turns_of(iota(tuple(shape), 1 - mode_axis), mode_of(mode, modes), cells, part))
    value = jnp.where(part == 1, -value, value)
    return jnp.where(mode < modes, value, 0.0)


def pair_table(mode, mode_part, cell, cell_part, modes, cells):
    value = cos_turns(turns_of(cell, mode_of(mode, modes), cells, mode_part ^ cell_part))
    return jnp.where((mode_part == 1) & (cell_part == 0), -value, value)


def table_y(cells, modes, mode_axis):
    shape = [2 * cells, 2 * cells]
    shape[mode_axis] = 2 * modes
    mode_part, mode = split(iota(tuple(shape), mode_axis), modes)
    cell_part, cell = split(iota(tuple(shape), 1 - mode_axis), cells)
    return pair_table(mode, mode_part, cell, cell_part, modes, cells)


def table_z(cells, modes, mode_axis, groups, times=1):
    shape = [2 * cells, 2 * cells]
    shape[mode_axis] = 2 * modes * times
    mode_part, mode = split(iota(tuple(shape), mode_axis) // times, modes)
    depth = cells // groups
    group, rest = split(iota(tuple(shape), 1 - mode_axis), 2 * depth)
    cell_part, cell = split(rest, depth)
    return pair_table(mode, mode_part, cell + group * depth, cell_part, modes, cells)


def gelu_slope(values):
    normal_cdf = 0.5 * (1.0 + lax.erf(values * 0.7071067811865476))
    return normal_cdf + values * jnp.exp(-0.5 * values * values) * 0.3989422804014327


def fetch(sources, targets, sems):
    copies = [
        pltpu.make_async_copy(source, target, sems.at[i])
        for i, (source, target) in enumerate(zip(sources, targets))
    ]
    for copy in copies:
        copy.start()
    return copies


def x_kernel(sizes, in_hbm, pre_hbm, cot_hbm, slope_ref, send_ref, ylast_ref, yfirst_ref,
             zlast_ref, zfirst_ref, in_ref, pre_ref, cot_ref, work_ref, half_ref, sems):
    C, zl, yl, dests, kr = sizes
    copies = fetch((in_hbm, pre_hbm, cot_hbm), (in_ref, pre_ref, cot_ref), sems)
    table = table_x(in_ref.shape[1], dests * kr // 2, 1, work_ref.shape[2])

    def transform(f, field):
        work_ref[f] = dot(field, table)
        for y in range(yl):
            rows = [work_ref[f, pl.ds(z * yl + y, C, stride=zl * yl), :] for z in range(zl)]
            turned = jnp.concatenate(rows, axis=0).T
            for d in range(dests):
                send_ref[pl.ds(((d * 2 + f) * yl + y) * kr, kr), :] = turned[d * kr : (d + 1) * kr]

    copies[0].wait()
    transform(0, in_ref[...])
    copies[1].wait()
    copies[2].wait()
    slope = cot_ref[...] * gelu_slope(pre_ref[...])
    slope_ref[...] = slope
    transform(1, slope)
    for half in range(slope_ref.shape[1] // LANES):
        cut = pl.ds(half * LANES, LANES)
        half_ref[...] = slope[:, half * LANES : (half + 1) * LANES]
        for z in range(zl):
            to = pl.ds(z * C, C)
            ylast_ref[to, cut] = half_ref[pl.ds(z * yl + yl - 1, C, stride=zl * yl), :]
            yfirst_ref[to, cut] = half_ref[pl.ds(z * yl, C, stride=zl * yl), :]
    for c in range(C):
        zlast_ref[pl.ds(c * yl, yl), :] = slope_ref[pl.ds((c * zl + zl - 1) * yl, yl), :]
        zfirst_ref[pl.ds(c * yl, yl), :] = slope_ref[pl.ds(c * zl * yl, yl), :]


def widen(values, lanes):
    spare = lanes - values.shape[1]
    if spare == 0:
        return values
    return jnp.concatenate([values, jnp.zeros((values.shape[0], spare), jnp.float32)], axis=1)


def y_kernel(sizes, recv_ref, *refs):
    send_ref = refs[-1]
    C, zl, kxl, ky, kyl, yl, sources = sizes
    kr = 2 * kxl
    lanes = zl * C
    pieces = []
    for kx in range(kxl):
        for f in range(2):
            pieces.append(
                jnp.concatenate(
                    [
                        recv_ref[pl.ds((s * 2 + f) * yl * kr + kx * 2 + r, yl, stride=kr), :]
                        for r in range(2)
                        for s in range(sources)
                    ],
                    axis=0,
                )
            )
    out = dot(table_y(yl * sources, ky, 0), jnp.concatenate(pieces, axis=1))
    for f in range(2):
        for r in range(2):
            for z in range(zl):
                parts = []
                for kx in range(kxl):
                    base = (kx * 2 + f) * lanes + z * C
                    parts.append(out[r * ky : (r + 1) * ky, base : base + C])
                block = widen(jnp.concatenate(parts, axis=1), send_ref.shape[1])
                for g in range(ky // kyl):
                    start = (g * 2 + f) * kyl * 2 * zl + r * zl + z
                    send_ref[pl.ds(start, kyl, stride=2 * zl), :] = block[g * kyl : (g + 1) * kyl]


def spread(rows, C):
    n, kc = rows.shape
    high = rows.astype(jnp.bfloat16).astype(jnp.float32)
    both = jnp.concatenate([high, rows - high], axis=1)
    own = jnp.remainder(iota((C, 2 * kc), 1), C) == iota((C, 2 * kc), 0)
    wide = jnp.where(own[None], jnp.broadcast_to(both[:, None, :], (n, C, 2 * kc)), 0.0)
    wide = wide.reshape(n * C, 2 * kc).astype(jnp.bfloat16)
    same = jnp.remainder(iota((2 * kc, kc), 0), kc) // C == iota((2 * kc, kc), 1) // C
    return dot(wide, same.astype(jnp.bfloat16), precision=None)


def z_kernel(sizes, recv_ref, weights_hbm, part_hbm, send_ref, hat_ref, weights_ref, part_ref,
             sems):
    C, zl, kxl, kyl, kz, groups, part_rows, scale = sizes
    copies = fetch(
        [weights_hbm.at[:, k] for k in range(kyl)] + [part_hbm],
        [weights_ref.at[:, k] for k in range(kyl)] + [part_ref],
        sems,
    )
    forward = table_z(zl * groups, kz, 1, groups).T
    back_table = table_z(zl * groups, kz, 1, groups, SUB)
    kc = kxl * C
    rows = 2 * zl
    chunk = kyl * rows
    wide = send_ref.shape[1]
    cols = []
    for k in range(kyl):
        for f in range(2):
            cols.append(
                jnp.concatenate(
                    [
                        recv_ref[pl.ds((s * 2 + f) * chunk + k * rows, rows), :]
                        for s in range(groups)
                    ],
                    axis=0,
                )
            )
    hat = dot(forward, jnp.concatenate(cols, axis=1))
    for k in range(kyl):
        slope_hat = None
        for f in range(2):
            base = (k * 2 + f) * wide
            value = hat[:, base : base + wide]
            if f == 1:
                value = value * scale
                slope_hat = value[:, :kc]
            for r in range(2):
                hat_ref[pl.ds((f * 2 + r) * kyl + k, kz, stride=4 * kyl), :] = value[
                    r * kz : (r + 1) * kz
                ]
        each = spread(slope_hat, C).reshape(2, kz, C, kc)
        copies[k].wait()
        w_re, w_im = weights_ref[0, k], weights_ref[1, k]
        re = w_re * each[0] + w_im * each[1]
        im = w_re * each[1] - w_im * each[0]
        dual = jnp.stack([re, im]).reshape(2, kz, C // SUB, SUB, kc)
        dual = jnp.sum(dual, axis=2).reshape(2 * kz * SUB, kc)
        back = widen(dot(back_table, dual), wide)
        for g in range(groups):
            send_ref[pl.ds(g * (chunk + part_rows) + k * rows, rows), :] = back[
                g * rows : (g + 1) * rows
            ]
    copies[kyl].wait()
    for g in range(groups):
        send_ref[pl.ds(g * (chunk + part_rows) + chunk, part_rows), :] = part_ref[...]


def grad_kernel(sizes, first, hat_ref, *refs):
    C, kxl, kyl, kz, steps = sizes
    out_hbm, out_ref, sems = refs[-3:]
    kc = kxl * C

    def copy(step):
        return pltpu.make_async_copy(
            out_ref.at[step], out_hbm.at[:, first + step], sems.at[step]
        )

    for step in range(steps):
        base = (first + step) * 4 * kyl
        in_re = hat_ref[pl.ds(base, kyl), :][:, :kc]
        in_im = hat_ref[pl.ds(base + kyl, kyl), :][:, :kc]
        wide = spread(hat_ref[pl.ds(base + 2 * kyl, 2 * kyl), :][:, :kc], C)
        wide = wide.reshape(2, kyl, C, kc)
        re, im = wide[0], wide[1]
        grad_re = re * in_re[:, None, :] + im * in_im[:, None, :]
        grad_im = im * in_re[:, None, :] - re * in_im[:, None, :]
        for kx in range(kxl):
            out_ref[step, 0, :, kx] = grad_re[:, :, kx * C : (kx + 1) * C]
            out_ref[step, 1, :, kx] = grad_im[:, :, kx * C : (kx + 1) * C]
        copy(step).start()
    for step in range(steps):
        copy(step).wait()


def y_back_kernel(sizes, recv_ref, *refs):
    send_ref = refs[-1]
    C, zl, kxl, ky, kyl, cells, yl, groups, dests, part_rows = sizes
    wide = recv_ref.shape[1]
    rows = 2 * zl
    kr = 2 * kxl
    chunk = kyl * rows + part_rows
    out_chunk = yl * kr + part_rows
    cols = []
    for z in range(zl):
        cols.append(
            jnp.concatenate(
                [
                    recv_ref[pl.ds(s * chunk + r * zl + z, kyl, stride=rows), :]
                    for r in range(2)
                    for s in range(groups)
                ],
                axis=0,
            )
        )
    out = dot(table_y(cells, ky, 1), jnp.concatenate(cols, axis=1))
    total = recv_ref[pl.ds(kyl * rows, part_rows), :]
    for s in range(1, groups):
        total = total + recv_ref[pl.ds(s * chunk + kyl * rows, part_rows), :]
    for kx in range(kxl):
        for r in range(2):
            block = out[r * cells : (r + 1) * cells]
            piece = jnp.concatenate(
                [block[:, z * wide + kx * C : z * wide + (kx + 1) * C] for z in range(zl)], axis=1
            )
            for d in range(dests):
                send_ref[pl.ds(d * out_chunk + kx * 2 + r, yl, stride=kr), :] = piece[
                    d * yl : (d + 1) * yl
                ]
    for d in range(dests):
        send_ref[pl.ds(d * out_chunk + yl * kr, part_rows), :] = total


def x_back_kernel(sizes, recv_ref, local_ref, fix_ref, out_ref, mix_ref, coef_ref, work_ref):
    C, zl, yl, kxl, sources, part_rows = sizes
    table = table_x(out_ref.shape[1], sources * kxl, 0)
    kr = 2 * kxl
    chunk = yl * kr + part_rows
    edge = 2 * C * yl
    for y in range(yl):
        column = jnp.concatenate(
            [recv_ref[pl.ds(s * chunk + y * kr, kr), :] for s in range(sources)], axis=0
        )
        value = dot(column.T, table)
        if y == 0:
            value = value + fix_ref[pl.ds(edge, zl * C), :]
        if y == yl - 1:
            value = value + fix_ref[pl.ds(edge + zl * C, zl * C), :]
        for z in range(zl):
            for half in range(value.shape[1] // LANES):
                work_ref[half, pl.ds(z * yl + y, C, stride=zl * yl), :] = value[
                    z * C : (z + 1) * C, half * LANES : (half + 1) * LANES
                ]
    for half in range(out_ref.shape[1] // LANES):
        cut = pl.ds(half * LANES, LANES)
        for c in range(C):
            for z in range(zl):
                row = pl.ds((c * zl + z) * yl, yl)
                value = work_ref[half, row, :] + local_ref[row, cut]
                if z == 0:
                    value = value + fix_ref[pl.ds(c * yl, yl), cut]
                if z == zl - 1:
                    value = value + fix_ref[pl.ds((C + c) * yl, yl), cut]
                out_ref[row, cut] = value
    total = recv_ref[pl.ds(yl * kr, part_rows), :]
    for s in range(1, sources):
        total = total + recv_ref[pl.ds(s * chunk + yl * kr, part_rows), :]
    total = total * (1.0 / 1024.0)
    high = C // kxl
    for b in range(kxl):
        mix_ref[pl.ds(b * high, high), :] = total[:high, b * C : (b + 1) * C]
    coef_ref[...] = total[high : high + 5, :C]


EXACT = lax.Precision.HIGHEST


def one_hot(rows, columns, times, major):
    if rows > columns:
        channel = iota((rows, columns), 0)
        channel = channel // times if major else jnp.remainder(channel, columns)
        return (channel == iota((rows, columns), 1)).astype(jnp.float32)
    channel = iota((rows, columns), 1)
    channel = channel // times if major else jnp.remainder(channel, rows)
    return (channel == iota((rows, columns), 0)).astype(jnp.float32)


def mixer(mix, C, times, major):
    n = C * times
    tall, flat = one_hot(n, C, times, major), one_hot(C, n, times, major)
    full = dot(dot(tall, mix, ((1,), (1,)), EXACT), flat, precision=EXACT)
    if major:
        place = [jnp.remainder(iota((n, n), axis), times) for axis in range(2)]
    else:
        place = [iota((n, n), axis) // C for axis in range(2)]
    return jnp.where(place[0] == place[1], full, 0.0)


def layer(ref, z, C, zl, yl):
    return jnp.concatenate([ref[pl.ds((c * zl + z) * yl, yl), :] for c in range(C)], axis=0)


def inner_kernel(sizes, in_hbm, slope_ref, mix_hbm, coefs_hbm, weights_hbm, out_ref, gram_ref,
                 sums_ref, kron_ref, packed_ref, in_ref, mix_ref, coefs_ref, raw_ref, sems):
    C, zl, yl, kxl, kyl, kz = sizes
    length = in_ref.shape[1]
    copies = fetch((mix_hbm, coefs_hbm, in_hbm), (mix_ref, coefs_ref, in_ref), sems)

    def raw_copy(z):
        return pltpu.make_async_copy(weights_hbm.at[:, z], raw_ref.at[z], sems.at[3 + z])

    for z in range(kz):
        raw_copy(z).start()

    def up(values):
        cube = values.reshape(C, yl, length)
        return jnp.concatenate(
            [jnp.zeros((C, 1, length), jnp.float32), cube[:, : yl - 1]], axis=1
        ).reshape(C * yl, length)

    def down(values):
        cube = values.reshape(C, yl, length)
        return jnp.concatenate(
            [cube[:, 1:], jnp.zeros((C, 1, length), jnp.float32)], axis=1
        ).reshape(C * yl, length)

    tall = one_hot(C * yl, C, yl, True)
    copies[0].wait()
    copies[1].wait()
    coef_rows = dot(tall, coefs_ref[...], ((1,), (1,)), EXACT)
    coef = [coef_rows[:, j : j + 1] for j in range(5)]
    kron = mixer(mix_ref[...], C, yl, True)
    kron_ref[...] = kron
    slopes = [layer(slope_ref, z, C, zl, yl) for z in range(zl)]
    hidden = [dot(kron, slopes[z]) for z in range(zl)]
    copies[2].wait()
    inputs = [layer(in_ref, z, C, zl, yl) for z in range(zl)]
    gram = None
    sums = [None] * 5
    for z in range(zl):
        shifted = {0: hidden[z], 1: up(hidden[z]), 2: down(hidden[z])}
        if z > 0:
            shifted[3] = hidden[z - 1]
        if z + 1 < zl:
            shifted[4] = hidden[z + 1]
        total = None
        for j, value in shifted.items():
            term = coef[j] * value
            total = term if total is None else total + term
            term = inputs[z] * value
            sums[j] = term if sums[j] is None else sums[j] + term
        for c in range(C):
            out_ref[pl.ds((c * zl + z) * yl, yl), :] = total[c * yl : (c + 1) * yl]
        stencil = coef[0] * inputs[z] + coef[1] * down(inputs[z]) + coef[2] * up(inputs[z])
        if z + 1 < zl:
            stencil = stencil + coef[3] * inputs[z + 1]
        if z > 0:
            stencil = stencil + coef[4] * inputs[z - 1]
        term = dot(slopes[z], stencil, ((1,), (1,)))
        gram = term if gram is None else gram + term
    gram_ref[...] = gram
    columns = []
    for term in sums:
        if term is None:
            columns.append(jnp.zeros((C * yl, 1), jnp.float32))
        else:
            columns.append(jnp.sum(term, axis=1, keepdims=True))
    columns.append(jnp.zeros((C * yl, SUB - 5), jnp.float32))
    sums_ref[...] = jnp.concatenate(columns, axis=1)
    for z in range(kz):
        raw_copy(z).wait()
        for part in range(2):
            for k in range(kyl):
                packed_ref[part, k, z] = jnp.concatenate(
                    [raw_ref[z, part, k, kx] for kx in range(kxl)], axis=1
                )


def edge_kernel(sizes, ybefore_ref, yafter_ref, zbefore_ref, zafter_ref, *refs):
    C, zl, yl, kxl = sizes
    hbms, (fix_ref, part_ref), refs, sems = refs[:6], refs[6:8], refs[8:-1], refs[-1]
    for copy in fetch(hbms, refs, sems):
        copy.wait()
    in_ref, mix_ref, coefs_ref, kron_ref, gram_ref, sums_ref = refs
    length = in_ref.shape[1]
    first, last = layer(in_ref, 0, C, zl, yl), layer(in_ref, zl - 1, C, zl, yl)
    layers = [layer(in_ref, z, C, zl, yl) for z in range(zl)]

    def row_of(y):
        return jnp.concatenate([each.reshape(C, yl, length)[:, y] for each in layers], axis=0)

    low, high_row = row_of(0), row_of(yl - 1)
    flat_y, tall_y = one_hot(C, C * yl, yl, True), one_hot(C * yl, C, yl, True)
    flat_z, tall_z = one_hot(C, C * zl, zl, False), one_hot(C * zl, C, zl, False)
    coef_y = dot(tall_y, coefs_ref[...], ((1,), (1,)), EXACT)
    coef_z = dot(tall_z, coefs_ref[...], ((1,), (1,)), EXACT)
    kron_z = mixer(mix_ref[...], C, zl, False)
    zbefore, zafter = zbefore_ref[...], zafter_ref[...]
    ybefore, yafter = ybefore_ref[...], yafter_ref[...]
    hidden_zb, hidden_za = dot(kron_ref[...], zbefore), dot(kron_ref[...], zafter)
    hidden_yb, hidden_ya = dot(kron_z, ybefore), dot(kron_z, yafter)
    n, m = C * yl, C * zl
    fix_ref[pl.ds(0, n), :] = coef_y[:, 3:4] * hidden_zb
    fix_ref[pl.ds(n, n), :] = coef_y[:, 4:5] * hidden_za
    fix_ref[pl.ds(2 * n, m), :] = coef_z[:, 1:2] * hidden_yb
    fix_ref[pl.ds(2 * n + m, m), :] = coef_z[:, 2:3] * hidden_ya
    gram = gram_ref[...]
    gram = gram + dot(zbefore, coef_y[:, 3:4] * first, ((1,), (1,)))
    gram = gram + dot(zafter, coef_y[:, 4:5] * last, ((1,), (1,)))
    edge = dot(ybefore, coef_z[:, 1:2] * low, ((1,), (1,)))
    edge = edge + dot(yafter, coef_z[:, 2:3] * high_row, ((1,), (1,)))
    same_y = jnp.remainder(iota((n, n), 0), yl) == jnp.remainder(iota((n, n), 1), yl)
    same_z = iota((m, m), 0) // C == iota((m, m), 1) // C
    mix = dot(dot(flat_y, jnp.where(same_y, gram, 0.0)), flat_y, ((1,), (1,)))
    mix = mix + dot(dot(flat_z, jnp.where(same_z, edge, 0.0)), flat_z, ((1,), (1,)))

    def column(values, place):
        total = jnp.sum(values, axis=1, keepdims=True)
        return jnp.where(iota((values.shape[0], SUB), 1) == place, total, 0.0)

    by_y = sums_ref[...] + column(first * hidden_zb, 3) + column(last * hidden_za, 4)
    by_z = column(low * hidden_yb, 1) + column(high_row * hidden_ya, 2)
    by_channel = dot(flat_y, by_y) + dot(flat_z, by_z)
    eye = (iota((SUB, SUB), 0) == iota((SUB, SUB), 1)).astype(jnp.float32)
    coefs = dot(eye, by_channel, ((1,), (1,)))
    high = C // kxl
    packed = jnp.concatenate([mix[b * high : (b + 1) * high] for b in range(kxl)], axis=1)
    part_ref[pl.ds(0, high), :] = widen(packed, part_ref.shape[1])
    part_ref[pl.ds(high, SUB), :] = widen(coefs, part_ref.shape[1])


def per_device(input_field, pre_activation, cotangent, spectral_weights, mix_weights, coefficients):
    C, zl, yl, length = input_field.shape
    groups_y = lax.axis_size("gy")
    groups_z = lax.axis_size("gz")
    cells_y, cells_z = yl * groups_y, zl * groups_z
    kz, kyl, kxl = spectral_weights.shape[1:4]
    modes_y, modes_x = kyl * groups_z, kxl * groups_y
    scale = 1.0 / (length * cells_y * cells_z)
    rows = C * zl * yl
    kr = 2 * kxl
    kc = kxl * C
    lanes = zl * C
    wide = max(kc, LANES)
    part_rows = C // kxl + SUB

    flat = lambda values: values.reshape(rows, length)
    exchange = functools.partial(lax.all_to_all, split_axis=0, concat_axis=0, tiled=True)
    far = pl.BlockSpec(memory_space=pl.ANY)
    near = pl.BlockSpec(memory_space=pltpu.VMEM)

    slope, send, ylast, yfirst, zlast, zfirst = call(
        functools.partial(x_kernel, (C, zl, yl, groups_y, kr)),
        (
            vmem(rows, length),
            f32(groups_y * 2 * yl * kr, lanes),
            far_out(C * zl, length),
            far_out(C * zl, length),
            far_out(C * yl, length),
            far_out(C * yl, length),
        ),
        (
            hbm(flat(input_field)),
            hbm(flat(pre_activation)),
            hbm(flat(cotangent)),
        ),
        24,
        flops=4 * rows * length * 2 * modes_x,
        bytes_accessed=6 * rows * length * 4,
        in_specs=[far] * 3,
        scratch=[
            pltpu.VMEM((rows, length), jnp.float32),
            pltpu.VMEM((rows, length), jnp.float32),
            pltpu.VMEM((rows, length), jnp.float32),
            pltpu.VMEM((2, rows, -(-2 * modes_x // LANES) * LANES), jnp.float32),
            pltpu.VMEM((rows, LANES), jnp.float32),
            pltpu.SemaphoreType.DMA((3,)),
        ],
    )
    lines = exchange(send, "gy")

    def from_below(values, axis):
        return lax.ppermute(values, axis, [(i, i + 1) for i in range(lax.axis_size(axis) - 1)])

    def from_above(values, axis):
        return lax.ppermute(values, axis, [(i + 1, i) for i in range(lax.axis_size(axis) - 1)])

    ybefore, yafter = from_below(ylast, "gy"), from_above(yfirst, "gy")
    zbefore, zafter = from_below(zlast, "gz"), from_above(zfirst, "gz")

    local, gram, sums, kron, weights = call(
        functools.partial(inner_kernel, (C, zl, yl, kxl, kyl, kz)),
        (
            vmem(rows, length),
            far_out(C * yl, C * yl),
            far_out(C * yl, SUB),
            far_out(C * yl, C * yl),
            far_out(2, kyl, kz, C, kc),
        ),
        (
            hbm(flat(input_field)),
            held(slope),
            hbm(mix_weights),
            hbm(coefficients),
            hbm(spectral_weights),
        ),
        44,
        flops=2 * 12 * (C * yl) ** 2 * length,
        bytes_accessed=2 * kz * kyl * kxl * C * 128 * 4 * 2,
        in_specs=[far, near, far, far, far],
        scratch=[
            pltpu.VMEM((rows, length), jnp.float32),
            pltpu.VMEM((C, C), jnp.float32),
            pltpu.VMEM(coefficients.shape, jnp.float32),
            pltpu.VMEM((kz, 2, kyl, kxl, C, C), jnp.float32),
            pltpu.SemaphoreType.DMA((3 + kz,)),
        ],
    )

    send = call(
        functools.partial(y_kernel, (C, zl, kxl, modes_y, kyl, yl, groups_y)),
        f32(groups_z * 2 * kyl * 2 * zl, wide),
        (lines, held(ybefore), held(yafter), held(zbefore), held(zafter), hbm(gram)),
        16,
        flops=16 * modes_y * cells_y * kxl * lanes,
        bytes_accessed=4 * MIB,
        in_specs=[near] + [far] * 5,
    )
    owned = exchange(send, "gz")

    fix, part = call(
        functools.partial(edge_kernel, (C, zl, yl, kxl)),
        (vmem(2 * C * yl + 2 * C * zl, length), far_out(part_rows, wide)),
        (
            held(ybefore),
            held(yafter),
            held(zbefore),
            held(zafter),
            hbm(flat(input_field)),
            hbm(mix_weights),
            hbm(coefficients),
            hbm(kron),
            hbm(gram),
            hbm(sums),
        ),
        24,
        flops=2 * 6 * (C * yl) ** 2 * length,
        bytes_accessed=3 * MIB,
        in_specs=[near] * 4 + [far] * 6,
        scratch=[
            pltpu.VMEM((rows, length), jnp.float32),
            pltpu.VMEM((C, C), jnp.float32),
            pltpu.VMEM(coefficients.shape, jnp.float32),
            pltpu.VMEM(kron.shape, jnp.float32),
            pltpu.VMEM(gram.shape, jnp.float32),
            pltpu.VMEM(sums.shape, jnp.float32),
            pltpu.SemaphoreType.DMA((6,)),
        ],
    )

    chunk = kyl * 2 * zl + part_rows
    send, hats = call(
        functools.partial(z_kernel, (C, zl, kxl, kyl, kz, groups_z, part_rows, scale)),
        (f32(groups_z * chunk, wide), vmem(kz * 4 * kyl, wide)),
        (owned, hbm(weights), hbm(part)),
        24,
        flops=16 * kz * kyl * C * kc,
        bytes_accessed=6 * MIB,
        in_specs=[near, far, far],
        scratch=[
            pltpu.VMEM((2, kyl, kz, C, kc), jnp.float32),
            pltpu.VMEM((part_rows, wide), jnp.float32),
            pltpu.SemaphoreType.DMA((kyl + 1,)),
        ],
    )
    returned = exchange(send, "gz")

    def gradient(first, steps, *before):
        return call(
            functools.partial(grad_kernel, (C, kxl, kyl, kz, steps), first),
            pltpu.HBM((2, kz, kyl, kxl, C, C), jnp.float32),
            (held(hats), *[hbm(each) for each in before]),
            16,
            flops=16 * steps * kyl * C * kc,
            bytes_accessed=2 * steps * kyl * kxl * C * 128 * 4,
            in_specs=[near] + [far] * len(before),
            out_specs=far,
            scratch=[
                pltpu.VMEM((steps, 2, kyl, kxl, C, C), jnp.float32),
                pltpu.SemaphoreType.DMA((steps,)),
            ],
            input_output_aliases={1: 0} if before else {},
        )

    grad_half = gradient(0, kz // 2)

    send = call(
        functools.partial(
            y_back_kernel,
            (C, zl, kxl, modes_y, kyl, cells_y, yl, groups_z, groups_y, part_rows),
        ),
        f32(groups_y * (yl * kr + part_rows), lanes),
        (returned, hbm(grad_half)),
        16,
        flops=8 * modes_y * cells_y * kxl * lanes,
        bytes_accessed=2 * MIB,
        in_specs=[near, far],
    )
    arrived = exchange(send, "gy")
    grad_spectral = gradient(kz // 2, kz - kz // 2, grad_half)

    grad_input, grad_mix, grad_coef = call(
        functools.partial(x_back_kernel, (C, zl, yl, kxl, groups_y, part_rows)),
        (f32(rows, length), f32(C, C), f32(5, C)),
        (arrived, held(local), held(fix)),
        16,
        flops=2 * rows * length * 2 * modes_x,
        bytes_accessed=3 * MIB,
        scratch=[pltpu.VMEM((length // LANES, rows, LANES), jnp.float32)],
    )
    return (grad_input.reshape(input_field.shape), grad_spectral, grad_mix, grad_coef)


def solution(mesh):
    in_specs = (
        P(None, "gz", "gy", None),
        P(None, "gz", "gy", None),
        P(None, "gz", "gy", None),
        P(None, None, "gz", "gy", None, None),
        P(),
        P(),
    )
    out_specs = (P(None, "gz", "gy", None), P(None, None, "gz", "gy", None, None), P(), P())
    return jax.shard_map(
        per_device, mesh=mesh, in_specs=in_specs, out_specs=out_specs, check_vma=False
    )
```

```python
import functools
import math

import jax
import jax.numpy as jnp
import numpy as np
from jax import lax
from jax.experimental import pallas as pl
from jax.experimental.pallas import tpu as pltpu
from jax.sharding import PartitionSpec as P

PRECISION = lax.Precision.HIGH
MIB = 1 << 20
SUB = 8
LANES = 128


def dot(left, right, dims=((1,), (0,)), precision=PRECISION):
    return lax.dot_general(
        left, right, (dims, ((), ())), precision=precision, preferred_element_type=jnp.float32
    )


def call(body, outs, operands, limit_mib, flops, bytes_accessed, scratch=(), **grid):
    return pl.pallas_call(
        body,
        out_shape=outs,
        scratch_shapes=list(scratch),
        compiler_params=pltpu.CompilerParams(vmem_limit_bytes=limit_mib * MIB),
        cost_estimate=pl.CostEstimate(
            flops=flops, bytes_accessed=bytes_accessed, transcendentals=0
        ),
        **grid,
    )(*operands)


def f32(*shape):
    return jax.ShapeDtypeStruct(shape, jnp.float32)


def vmem(*shape):
    return pltpu.VMEM(shape, jnp.float32)


def far_out(*shape):
    return pltpu.HBM(shape, jnp.float32)


def hbm(values):
    return pltpu.with_memory_space_constraint(values, pltpu.HBM)


def held(values):
    return pltpu.with_memory_space_constraint(values, pltpu.VMEM)


def iota(shape, axis):
    return lax.broadcasted_iota(jnp.int32, shape, axis)


SERIES = [(-1.0) ** n * (2.0 * math.pi) ** (2 * n) / math.factorial(2 * n) for n in range(10)]


def cos_turns(turns):
    part = turns - jnp.floor(turns + 0.5)
    size = jnp.abs(part)
    flip = size > 0.25
    part = jnp.where(flip, 0.5 - size, size)
    square = part * part
    total = jnp.full_like(square, SERIES[-1])
    for factor in SERIES[-2::-1]:
        total = total * square + factor
    return jnp.where(flip, -total, total)


def mode_of(position, modes):
    return jnp.where(position < modes // 2, position, position - modes)


def turns_of(cell, mode, cells, quarter):
    return (cell * mode).astype(jnp.float32) * (1.0 / cells) - 0.25 * quarter.astype(jnp.float32)


def split(index, size):
    high = index // size
    return high, index - high * size


def table_x(cells, modes, mode_axis, columns=None):
    shape = [cells, cells]
    shape[mode_axis] = columns or 2 * modes
    mode, part = split(iota(tuple(shape), mode_axis), 2)
    value = cos_turns(turns_of(iota(tuple(shape), 1 - mode_axis), mode_of(mode, modes), cells, part))
    value = jnp.where(part == 1, -value, value)
    return jnp.where(mode < modes, value, 0.0)


def pair_table(mode, mode_part, cell, cell_part, modes, cells):
    value = cos_turns(turns_of(cell, mode_of(mode, modes), cells, mode_part ^ cell_part))
    return jnp.where((mode_part == 1) & (cell_part == 0), -value, value)


def table_y(cells, modes, mode_axis):
    shape = [2 * cells, 2 * cells]
    shape[mode_axis] = 2 * modes
    mode_part, mode = split(iota(tuple(shape), mode_axis), modes)
    cell_part, cell = split(iota(tuple(shape), 1 - mode_axis), cells)
    return pair_table(mode, mode_part, cell, cell_part, modes, cells)


def table_z(cells, modes, mode_axis, groups, times=1):
    shape = [2 * cells, 2 * cells]
    shape[mode_axis] = 2 * modes * times
    mode_part, mode = split(iota(tuple(shape), mode_axis) // times, modes)
    depth = cells // groups
    group, rest = split(iota(tuple(shape), 1 - mode_axis), 2 * depth)
    cell_part, cell = split(rest, depth)
    return pair_table(mode, mode_part, cell + group * depth, cell_part, modes, cells)


def gelu_slope(values):
    normal_cdf = 0.5 * (1.0 + lax.erf(values * 0.7071067811865476))
    return normal_cdf + values * jnp.exp(-0.5 * values * values) * 0.3989422804014327


def fetch(sources, targets, sems):
    copies = [
        pltpu.make_async_copy(source, target, sems.at[i])
        for i, (source, target) in enumerate(zip(sources, targets))
    ]
    for copy in copies:
        copy.start()
    return copies


def halves(values):
    high = values.astype(jnp.bfloat16)
    return high, (values - high.astype(jnp.float32)).astype(jnp.bfloat16)


def x_kernel(sizes, in_hbm, pre_hbm, cot_hbm, slope_ref, send_ref, ylast_ref, yfirst_ref,
             zlast_ref, zfirst_ref, in_ref, pre_ref, cot_ref, work_ref, half_ref, sems):
    C, zl, yl, dests, kr = sizes
    copies = fetch((in_hbm, pre_hbm, cot_hbm), (in_ref, pre_ref, cot_ref), sems)
    table = table_x(in_ref.shape[1], dests * kr // 2, 1, dests * kr)
    high, low = halves(table)
    both = jnp.concatenate([high, low], axis=1)
    alone = jnp.concatenate([high, jnp.zeros_like(low)], axis=1)

    def transform(f, field):
        upper, lower = halves(field)
        work_ref[f] = dot(upper, both, precision=None) + dot(lower, alone, precision=None)
        for y in range(yl):
            rows = [work_ref[f, pl.ds(z * yl + y, C, stride=zl * yl), :] for z in range(zl)]
            turned = jnp.concatenate(rows, axis=0).T
            turned = turned[: dests * kr] + turned[dests * kr :]
            for d in range(dests):
                send_ref[pl.ds(((d * 2 + f) * yl + y) * kr, kr), :] = turned[d * kr : (d + 1) * kr]

    copies[0].wait()
    transform(0, in_ref[...])
    copies[1].wait()
    copies[2].wait()
    slope = cot_ref[...] * gelu_slope(pre_ref[...])
    slope_ref[...] = slope
    transform(1, slope)
    for half in range(slope_ref.shape[1] // LANES):
        cut = pl.ds(half * LANES, LANES)
        half_ref[...] = slope[:, half * LANES : (half + 1) * LANES]
        for z in range(zl):
            to = pl.ds(z * C, C)
            ylast_ref[to, cut] = half_ref[pl.ds(z * yl + yl - 1, C, stride=zl * yl), :]
            yfirst_ref[to, cut] = half_ref[pl.ds(z * yl, C, stride=zl * yl), :]
    for c in range(C):
        zlast_ref[pl.ds(c * yl, yl), :] = slope_ref[pl.ds((c * zl + zl - 1) * yl, yl), :]
        zfirst_ref[pl.ds(c * yl, yl), :] = slope_ref[pl.ds(c * zl * yl, yl), :]


def widen(values, lanes):
    spare = lanes - values.shape[1]
    if spare == 0:
        return values
    return jnp.concatenate([values, jnp.zeros((values.shape[0], spare), jnp.float32)], axis=1)


def y_kernel(sizes, recv_ref, *refs):
    send_ref = refs[-1]
    C, zl, kxl, ky, kyl, yl, sources = sizes
    kr = 2 * kxl
    lanes = zl * C
    pieces = []
    for kx in range(kxl):
        for f in range(2):
            pieces.append(
                jnp.concatenate(
                    [
                        recv_ref[pl.ds((s * 2 + f) * yl * kr + kx * 2 + r, yl, stride=kr), :]
                        for r in range(2)
                        for s in range(sources)
                    ],
                    axis=0,
                )
            )
    out = dot(table_y(yl * sources, ky, 0), jnp.concatenate(pieces, axis=1))
    for f in range(2):
        for r in range(2):
            for z in range(zl):
                parts = []
                for kx in range(kxl):
                    base = (kx * 2 + f) * lanes + z * C
                    parts.append(out[r * ky : (r + 1) * ky, base : base + C])
                block = widen(jnp.concatenate(parts, axis=1), send_ref.shape[1])
                for g in range(ky // kyl):
                    start = (g * 2 + f) * kyl * 2 * zl + r * zl + z
                    send_ref[pl.ds(start, kyl, stride=2 * zl), :] = block[g * kyl : (g + 1) * kyl]


def spread(rows, C):
    n, kc = rows.shape
    high = rows.astype(jnp.bfloat16).astype(jnp.float32)
    both = jnp.concatenate([high, rows - high], axis=1)
    own = jnp.remainder(iota((C, 2 * kc), 1), C) == iota((C, 2 * kc), 0)
    wide = jnp.where(own[None], jnp.broadcast_to(both[:, None, :], (n, C, 2 * kc)), 0.0)
    wide = wide.reshape(n * C, 2 * kc).astype(jnp.bfloat16)
    same = jnp.remainder(iota((2 * kc, kc), 0), kc) // C == iota((2 * kc, kc), 1) // C
    return dot(wide, same.astype(jnp.bfloat16), precision=None)


def z_kernel(sizes, recv_ref, weights_hbm, part_hbm, send_ref, hat_ref, weights_ref, part_ref,
             sems):
    C, zl, kxl, kyl, kz, groups, part_rows, scale = sizes
    copies = fetch(
        [weights_hbm.at[:, k] for k in range(kyl)] + [part_hbm],
        [weights_ref.at[:, k] for k in range(kyl)] + [part_ref],
        sems,
    )
    forward = table_z(zl * groups, kz, 1, groups).T
    back_table = table_z(zl * groups, kz, 1, groups, SUB)
    kc = kxl * C
    rows = 2 * zl
    chunk = kyl * rows
    wide = send_ref.shape[1]
    cols = []
    for k in range(kyl):
        for f in range(2):
            cols.append(
                jnp.concatenate(
                    [
                        recv_ref[pl.ds((s * 2 + f) * chunk + k * rows, rows), :]
                        for s in range(groups)
                    ],
                    axis=0,
                )
            )
    hat = dot(forward, jnp.concatenate(cols, axis=1))
    for k in range(kyl):
        slope_hat = None
        for f in range(2):
            base = (k * 2 + f) * wide
            value = hat[:, base : base + wide]
            if f == 1:
                value = value * scale
                slope_hat = value[:, :kc]
            for r in range(2):
                hat_ref[pl.ds((f * 2 + r) * kyl + k, kz, stride=4 * kyl), :] = value[
                    r * kz : (r + 1) * kz
                ]
        each = spread(slope_hat, C).reshape(2, kz, C, kc)
        copies[k].wait()
        w_re, w_im = weights_ref[0, k], weights_ref[1, k]
        re = w_re * each[0] + w_im * each[1]
        im = w_re * each[1] - w_im * each[0]
        dual = jnp.stack([re, im]).reshape(2, kz, C // SUB, SUB, kc)
        dual = jnp.sum(dual, axis=2).reshape(2 * kz * SUB, kc)
        back = widen(dot(back_table, dual), wide)
        for g in range(groups):
            send_ref[pl.ds(g * (chunk + part_rows) + k * rows, rows), :] = back[
                g * rows : (g + 1) * rows
            ]
    copies[kyl].wait()
    for g in range(groups):
        send_ref[pl.ds(g * (chunk + part_rows) + chunk, part_rows), :] = part_ref[...]


def grad_kernel(sizes, first, hat_ref, *refs):
    C, kxl, kyl, kz, steps = sizes
    out_hbm, out_ref, sems = refs[-3:]
    kc = kxl * C

    def copy(step):
        return pltpu.make_async_copy(
            out_ref.at[step], out_hbm.at[:, first + step], sems.at[step]
        )

    for step in range(steps):
        base = (first + step) * 4 * kyl
        in_re = hat_ref[pl.ds(base, kyl), :][:, :kc]
        in_im = hat_ref[pl.ds(base + kyl, kyl), :][:, :kc]
        wide = spread(hat_ref[pl.ds(base + 2 * kyl, 2 * kyl), :][:, :kc], C)
        wide = wide.reshape(2, kyl, C, kc)
        re, im = wide[0], wide[1]
        grad_re = re * in_re[:, None, :] + im * in_im[:, None, :]
        grad_im = im * in_re[:, None, :] - re * in_im[:, None, :]
        for kx in range(kxl):
            out_ref[step, 0, :, kx] = grad_re[:, :, kx * C : (kx + 1) * C]
            out_ref[step, 1, :, kx] = grad_im[:, :, kx * C : (kx + 1) * C]
        copy(step).start()
    for step in range(steps):
        copy(step).wait()


def y_back_kernel(sizes, recv_ref, *refs):
    send_ref = refs[-1]
    C, zl, kxl, ky, kyl, cells, yl, groups, dests, part_rows = sizes
    wide = recv_ref.shape[1]
    rows = 2 * zl
    kr = 2 * kxl
    chunk = kyl * rows + part_rows
    out_chunk = yl * kr + part_rows
    cols = []
    for z in range(zl):
        cols.append(
            jnp.concatenate(
                [
                    recv_ref[pl.ds(s * chunk + r * zl + z, kyl, stride=rows), :]
                    for r in range(2)
                    for s in range(groups)
                ],
                axis=0,
            )
        )
    out = dot(table_y(cells, ky, 1), jnp.concatenate(cols, axis=1))
    total = recv_ref[pl.ds(kyl * rows, part_rows), :]
    for s in range(1, groups):
        total = total + recv_ref[pl.ds(s * chunk + kyl * rows, part_rows), :]
    for kx in range(kxl):
        for r in range(2):
            block = out[r * cells : (r + 1) * cells]
            piece = jnp.concatenate(
                [block[:, z * wide + kx * C : z * wide + (kx + 1) * C] for z in range(zl)], axis=1
            )
            for d in range(dests):
                send_ref[pl.ds(d * out_chunk + kx * 2 + r, yl, stride=kr), :] = piece[
                    d * yl : (d + 1) * yl
                ]
    for d in range(dests):
        send_ref[pl.ds(d * out_chunk + yl * kr, part_rows), :] = total


def x_back_kernel(sizes, recv_ref, local_ref, fix_ref, out_ref, mix_ref, coef_ref, work_ref):
    C, zl, yl, kxl, sources, part_rows = sizes
    table = table_x(out_ref.shape[1], sources * kxl, 0)
    kr = 2 * kxl
    chunk = yl * kr + part_rows
    edge = 2 * C * yl
    for y in range(yl):
        column = jnp.concatenate(
            [recv_ref[pl.ds(s * chunk + y * kr, kr), :] for s in range(sources)], axis=0
        )
        value = dot(column.T, table)
        if y == 0:
            value = value + fix_ref[pl.ds(edge, zl * C), :]
        if y == yl - 1:
            value = value + fix_ref[pl.ds(edge + zl * C, zl * C), :]
        for z in range(zl):
            for half in range(value.shape[1] // LANES):
                work_ref[half, pl.ds(z * yl + y, C, stride=zl * yl), :] = value[
                    z * C : (z + 1) * C, half * LANES : (half + 1) * LANES
                ]
    for half in range(out_ref.shape[1] // LANES):
        cut = pl.ds(half * LANES, LANES)
        for c in range(C):
            for z in range(zl):
                row = pl.ds((c * zl + z) * yl, yl)
                value = work_ref[half, row, :] + local_ref[row, cut]
                if z == 0:
                    value = value + fix_ref[pl.ds(c * yl, yl), cut]
                if z == zl - 1:
                    value = value + fix_ref[pl.ds((C + c) * yl, yl), cut]
                out_ref[row, cut] = value
    total = recv_ref[pl.ds(yl * kr, part_rows), :]
    for s in range(1, sources):
        total = total + recv_ref[pl.ds(s * chunk + yl * kr, part_rows), :]
    total = total * (1.0 / 1024.0)
    high = C // kxl
    for b in range(kxl):
        mix_ref[pl.ds(b * high, high), :] = total[:high, b * C : (b + 1) * C]
    coef_ref[...] = total[high : high + 5, :C]


EXACT = PRECISION


def one_hot(rows, columns, times, major):
    if rows > columns:
        channel = iota((rows, columns), 0)
        channel = channel // times if major else jnp.remainder(channel, columns)
        return (channel == iota((rows, columns), 1)).astype(jnp.float32)
    channel = iota((rows, columns), 1)
    channel = channel // times if major else jnp.remainder(channel, rows)
    return (channel == iota((rows, columns), 0)).astype(jnp.float32)


def mixer(mix, C, times, major):
    n = C * times
    tall, flat = one_hot(n, C, times, major), one_hot(C, n, times, major)
    full = dot(dot(tall, mix, ((1,), (1,)), EXACT), flat, precision=EXACT)
    if major:
        place = [jnp.remainder(iota((n, n), axis), times) for axis in range(2)]
    else:
        place = [iota((n, n), axis) // C for axis in range(2)]
    return jnp.where(place[0] == place[1], full, 0.0)


def layer(ref, z, C, zl, yl):
    return jnp.concatenate([ref[pl.ds((c * zl + z) * yl, yl), :] for c in range(C)], axis=0)


def inner_kernel(sizes, in_hbm, slope_ref, mix_hbm, coefs_hbm, weights_hbm, out_ref, gram_ref,
                 sums_ref, packed_ref, in_ref, mix_ref, coefs_ref, raw_ref, sems):
    C, zl, yl, kxl, kyl, kz = sizes
    length = in_ref.shape[1]
    copies = fetch((mix_hbm, coefs_hbm, in_hbm), (mix_ref, coefs_ref, in_ref), sems)

    groups = math.gcd(4, kz)
    size = kz // groups

    def raw_copy(g):
        cut = pl.ds(g * size, size)
        return pltpu.make_async_copy(weights_hbm.at[:, cut], raw_ref.at[:, cut], sems.at[3 + g])

    for g in range(groups):
        raw_copy(g).start()

    def up(values):
        cube = values.reshape(C, yl, length)
        return jnp.concatenate(
            [jnp.zeros((C, 1, length), jnp.float32), cube[:, : yl - 1]], axis=1
        ).reshape(C * yl, length)

    def down(values):
        cube = values.reshape(C, yl, length)
        return jnp.concatenate(
            [cube[:, 1:], jnp.zeros((C, 1, length), jnp.float32)], axis=1
        ).reshape(C * yl, length)

    tall = one_hot(C * yl, C, yl, True)
    copies[0].wait()
    copies[1].wait()
    coef_rows = dot(tall, coefs_ref[...], ((1,), (1,)), EXACT)
    coef = [coef_rows[:, j : j + 1] for j in range(5)]
    kron = mixer(mix_ref[...], C, yl, True)
    slopes = [layer(slope_ref, z, C, zl, yl) for z in range(zl)]
    hidden = [dot(kron, slopes[z]) for z in range(zl)]
    copies[2].wait()
    inputs = [layer(in_ref, z, C, zl, yl) for z in range(zl)]
    gram = None
    sums = [None] * 5
    for z in range(zl):
        shifted = {0: hidden[z], 1: up(hidden[z]), 2: down(hidden[z])}
        if z > 0:
            shifted[3] = hidden[z - 1]
        if z + 1 < zl:
            shifted[4] = hidden[z + 1]
        total = None
        for j, value in shifted.items():
            term = coef[j] * value
            total = term if total is None else total + term
            term = inputs[z] * value
            sums[j] = term if sums[j] is None else sums[j] + term
        for c in range(C):
            out_ref[pl.ds((c * zl + z) * yl, yl), :] = total[c * yl : (c + 1) * yl]
        stencil = coef[0] * inputs[z] + coef[1] * down(inputs[z]) + coef[2] * up(inputs[z])
        if z + 1 < zl:
            stencil = stencil + coef[3] * inputs[z + 1]
        if z > 0:
            stencil = stencil + coef[4] * inputs[z - 1]
        term = dot(slopes[z], stencil, ((1,), (1,)))
        gram = term if gram is None else gram + term
    gram_ref[...] = gram
    columns = []
    for term in sums:
        if term is None:
            columns.append(jnp.zeros((C * yl, 1), jnp.float32))
        else:
            columns.append(jnp.sum(term, axis=1, keepdims=True))
    columns.append(jnp.zeros((C * yl, SUB - 5), jnp.float32))
    sums_ref[...] = jnp.concatenate(columns, axis=1)
    for z in range(kz):
        if z % size == 0:
            raw_copy(z // size).wait()
        for part in range(2):
            for k in range(kyl):
                packed_ref[part, k, z] = jnp.concatenate(
                    [raw_ref[part, z, k, kx] for kx in range(kxl)], axis=1
                )


def edge_kernel(sizes, ybefore_ref, yafter_ref, zbefore_ref, zafter_ref, *refs):
    C, zl, yl, kxl = sizes
    *hbms, fix_ref, part_ref, mix_ref, coefs_ref, in_ref, gram_ref, sums_ref, sems = refs
    copies = fetch(hbms, (mix_ref, coefs_ref, in_ref, gram_ref, sums_ref), sems)

    def inside(ref, axis, place):
        return ref[...] * (lax.axis_index(axis) != place).astype(jnp.float32)

    last_y, last_z = lax.axis_size("gy") - 1, lax.axis_size("gz") - 1
    zbefore, zafter = inside(zbefore_ref, "gz", 0), inside(zafter_ref, "gz", last_z)
    ybefore, yafter = inside(ybefore_ref, "gy", 0), inside(yafter_ref, "gy", last_y)
    copies[0].wait()
    copies[1].wait()
    kron_y = mixer(mix_ref[...], C, yl, True)
    kron_z = mixer(mix_ref[...], C, zl, False)
    hidden_zb, hidden_za = dot(kron_y, zbefore), dot(kron_y, zafter)
    hidden_yb, hidden_ya = dot(kron_z, ybefore), dot(kron_z, yafter)
    for copy in copies[2:]:
        copy.wait()
    length = in_ref.shape[1]
    first, last = layer(in_ref, 0, C, zl, yl), layer(in_ref, zl - 1, C, zl, yl)
    layers = [layer(in_ref, z, C, zl, yl) for z in range(zl)]

    def row_of(y):
        return jnp.concatenate([each.reshape(C, yl, length)[:, y] for each in layers], axis=0)

    low, high_row = row_of(0), row_of(yl - 1)
    flat_y, tall_y = one_hot(C, C * yl, yl, True), one_hot(C * yl, C, yl, True)
    flat_z, tall_z = one_hot(C, C * zl, zl, False), one_hot(C * zl, C, zl, False)
    coef_y = dot(tall_y, coefs_ref[...], ((1,), (1,)), EXACT)
    coef_z = dot(tall_z, coefs_ref[...], ((1,), (1,)), EXACT)
    n, m = C * yl, C * zl
    fix_ref[pl.ds(0, n), :] = coef_y[:, 3:4] * hidden_zb
    fix_ref[pl.ds(n, n), :] = coef_y[:, 4:5] * hidden_za
    fix_ref[pl.ds(2 * n, m), :] = coef_z[:, 1:2] * hidden_yb
    fix_ref[pl.ds(2 * n + m, m), :] = coef_z[:, 2:3] * hidden_ya
    gram = gram_ref[...]
    gram = gram + dot(zbefore, coef_y[:, 3:4] * first, ((1,), (1,)))
    gram = gram + dot(zafter, coef_y[:, 4:5] * last, ((1,), (1,)))
    edge = dot(ybefore, coef_z[:, 1:2] * low, ((1,), (1,)))
    edge = edge + dot(yafter, coef_z[:, 2:3] * high_row, ((1,), (1,)))
    same_y = jnp.remainder(iota((n, n), 0), yl) == jnp.remainder(iota((n, n), 1), yl)
    same_z = iota((m, m), 0) // C == iota((m, m), 1) // C
    mix = dot(dot(flat_y, jnp.where(same_y, gram, 0.0)), flat_y, ((1,), (1,)))
    mix = mix + dot(dot(flat_z, jnp.where(same_z, edge, 0.0)), flat_z, ((1,), (1,)))

    def column(values, place):
        total = jnp.sum(values, axis=1, keepdims=True)
        return jnp.where(iota((values.shape[0], SUB), 1) == place, total, 0.0)

    by_y = sums_ref[...] + column(first * hidden_zb, 3) + column(last * hidden_za, 4)
    by_z = column(low * hidden_yb, 1) + column(high_row * hidden_ya, 2)
    by_channel = dot(flat_y, by_y) + dot(flat_z, by_z)
    eye = (iota((SUB, SUB), 0) == iota((SUB, SUB), 1)).astype(jnp.float32)
    coefs = dot(eye, by_channel, ((1,), (1,)))
    high = C // kxl
    packed = jnp.concatenate([mix[b * high : (b + 1) * high] for b in range(kxl)], axis=1)
    part_ref[pl.ds(0, high), :] = widen(packed, part_ref.shape[1])
    part_ref[pl.ds(high, SUB), :] = widen(coefs, part_ref.shape[1])


def per_device(input_field, pre_activation, cotangent, spectral_weights, mix_weights, coefficients):
    C, zl, yl, length = input_field.shape
    groups_y = lax.axis_size("gy")
    groups_z = lax.axis_size("gz")
    cells_y, cells_z = yl * groups_y, zl * groups_z
    kz, kyl, kxl = spectral_weights.shape[1:4]
    modes_y, modes_x = kyl * groups_z, kxl * groups_y
    scale = 1.0 / (length * cells_y * cells_z)
    rows = C * zl * yl
    kr = 2 * kxl
    kc = kxl * C
    lanes = zl * C
    wide = max(kc, LANES)
    part_rows = C // kxl + SUB

    flat = lambda values: values.reshape(rows, length)
    exchange = functools.partial(lax.all_to_all, split_axis=0, concat_axis=0, tiled=True)
    far = pl.BlockSpec(memory_space=pl.ANY)
    near = pl.BlockSpec(memory_space=pltpu.VMEM)

    slope, send, ylast, yfirst, zlast, zfirst = call(
        functools.partial(x_kernel, (C, zl, yl, groups_y, kr)),
        (
            vmem(rows, length),
            f32(groups_y * 2 * yl * kr, lanes),
            far_out(C * zl, length),
            far_out(C * zl, length),
            far_out(C * yl, length),
            far_out(C * yl, length),
        ),
        (
            hbm(flat(input_field)),
            hbm(flat(pre_activation)),
            hbm(flat(cotangent)),
        ),
        24,
        flops=4 * rows * length * 2 * modes_x,
        bytes_accessed=6 * rows * length * 4,
        in_specs=[far] * 3,
        scratch=[
            pltpu.VMEM((rows, length), jnp.float32),
            pltpu.VMEM((rows, length), jnp.float32),
            pltpu.VMEM((rows, length), jnp.float32),
            pltpu.VMEM((2, rows, 4 * modes_x), jnp.float32),
            pltpu.VMEM((rows, LANES), jnp.float32),
            pltpu.SemaphoreType.DMA((3,)),
        ],
    )
    lines = exchange(send, "gy")

    def from_below(values, axis):
        size = lax.axis_size(axis)
        return lax.ppermute(values, axis, [(i, (i + 1) % size) for i in range(size)])

    def from_above(values, axis):
        size = lax.axis_size(axis)
        return lax.ppermute(values, axis, [((i + 1) % size, i) for i in range(size)])

    ybefore, yafter = from_below(ylast, "gy"), from_above(yfirst, "gy")
    zbefore, zafter = from_below(zlast, "gz"), from_above(zfirst, "gz")

    local, gram, sums, weights = call(
        functools.partial(inner_kernel, (C, zl, yl, kxl, kyl, kz)),
        (
            vmem(rows, length),
            far_out(C * yl, C * yl),
            far_out(C * yl, SUB),
            far_out(2, kyl, kz, C, kc),
        ),
        (
            hbm(flat(input_field)),
            held(slope),
            hbm(mix_weights),
            hbm(coefficients),
            hbm(spectral_weights),
        ),
        44,
        flops=2 * 12 * (C * yl) ** 2 * length,
        bytes_accessed=2 * kz * kyl * kxl * C * 128 * 4 * 2,
        in_specs=[far, near, far, far, far],
        scratch=[
            pltpu.VMEM((rows, length), jnp.float32),
            pltpu.VMEM((C, C), jnp.float32),
            pltpu.VMEM(coefficients.shape, jnp.float32),
            pltpu.VMEM((2, kz, kyl, kxl, C, C), jnp.float32),
            pltpu.SemaphoreType.DMA((3 + math.gcd(4, kz),)),
        ],
    )

    send = call(
        functools.partial(y_kernel, (C, zl, kxl, modes_y, kyl, yl, groups_y)),
        f32(groups_z * 2 * kyl * 2 * zl, wide),
        (lines, held(ybefore), held(yafter), held(zbefore), held(zafter), hbm(weights)),
        16,
        flops=16 * modes_y * cells_y * kxl * lanes,
        bytes_accessed=4 * MIB,
        in_specs=[near] + [far] * 5,
    )
    owned = exchange(send, "gz")

    fix, part = call(
        functools.partial(edge_kernel, (C, zl, yl, kxl)),
        (vmem(2 * C * yl + 2 * C * zl, length), far_out(part_rows, wide)),
        (
            held(ybefore),
            held(yafter),
            held(zbefore),
            held(zafter),
            hbm(mix_weights),
            hbm(coefficients),
            hbm(flat(input_field)),
            hbm(gram),
            hbm(sums),
        ),
        24,
        flops=2 * 6 * (C * yl) ** 2 * length,
        bytes_accessed=3 * MIB,
        in_specs=[near] * 4 + [far] * 5,
        scratch=[
            pltpu.VMEM((C, C), jnp.float32),
            pltpu.VMEM(coefficients.shape, jnp.float32),
            pltpu.VMEM((rows, length), jnp.float32),
            pltpu.VMEM(gram.shape, jnp.float32),
            pltpu.VMEM(sums.shape, jnp.float32),
            pltpu.SemaphoreType.DMA((5,)),
        ],
    )

    chunk = kyl * 2 * zl + part_rows
    send, hats = call(
        functools.partial(z_kernel, (C, zl, kxl, kyl, kz, groups_z, part_rows, scale)),
        (f32(groups_z * chunk, wide), vmem(kz * 4 * kyl, wide)),
        (owned, hbm(weights), hbm(part)),
        24,
        flops=16 * kz * kyl * C * kc,
        bytes_accessed=6 * MIB,
        in_specs=[near, far, far],
        scratch=[
            pltpu.VMEM((2, kyl, kz, C, kc), jnp.float32),
            pltpu.VMEM((part_rows, wide), jnp.float32),
            pltpu.SemaphoreType.DMA((kyl + 1,)),
        ],
    )
    returned = exchange(send, "gz")

    def gradient(first, steps, *before):
        return call(
            functools.partial(grad_kernel, (C, kxl, kyl, kz, steps), first),
            pltpu.HBM((2, kz, kyl, kxl, C, C), jnp.float32),
            (held(hats), *[hbm(each) for each in before]),
            16,
            flops=16 * steps * kyl * C * kc,
            bytes_accessed=2 * steps * kyl * kxl * C * 128 * 4,
            in_specs=[near] + [far] * len(before),
            out_specs=far,
            scratch=[
                pltpu.VMEM((steps, 2, kyl, kxl, C, C), jnp.float32),
                pltpu.SemaphoreType.DMA((steps,)),
            ],
            input_output_aliases={1: 0} if before else {},
        )

    grad_half = gradient(0, kz // 2)

    send = call(
        functools.partial(
            y_back_kernel,
            (C, zl, kxl, modes_y, kyl, cells_y, yl, groups_z, groups_y, part_rows),
        ),
        f32(groups_y * (yl * kr + part_rows), lanes),
        (returned, hbm(grad_half)),
        16,
        flops=8 * modes_y * cells_y * kxl * lanes,
        bytes_accessed=2 * MIB,
        in_specs=[near, far],
    )
    arrived = exchange(send, "gy")
    grad_spectral = gradient(kz // 2, kz - kz // 2, grad_half)

    grad_input, grad_mix, grad_coef = call(
        functools.partial(x_back_kernel, (C, zl, yl, kxl, groups_y, part_rows)),
        (f32(rows, length), f32(C, C), f32(5, C)),
        (arrived, held(local), held(fix)),
        16,
        flops=2 * rows * length * 2 * modes_x,
        bytes_accessed=3 * MIB,
        scratch=[pltpu.VMEM((length // LANES, rows, LANES), jnp.float32)],
    )
    return (grad_input.reshape(input_field.shape), grad_spectral, grad_mix, grad_coef)


def solution(mesh):
    in_specs = (
        P(None, "gz", "gy", None),
        P(None, "gz", "gy", None),
        P(None, "gz", "gy", None),
        P(None, None, "gz", "gy", None, None),
        P(),
        P(),
    )
    out_specs = (P(None, "gz", "gy", None), P(None, None, "gz", "gy", None, None), P(), P())
    return jax.shard_map(
        per_device, mesh=mesh, in_specs=in_specs, out_specs=out_specs, check_vma=False
    )
```

```python
import functools
import math

import jax
import jax.numpy as jnp
import numpy as np
from jax import lax
from jax.experimental import pallas as pl
from jax.experimental.pallas import tpu as pltpu
from jax.sharding import PartitionSpec as P

PRECISION = lax.Precision.HIGH
MIB = 1 << 20
SUB = 8
LANES = 128


def dot(left, right, dims=((1,), (0,)), precision=PRECISION):
    return lax.dot_general(
        left, right, (dims, ((), ())), precision=precision, preferred_element_type=jnp.float32
    )


def call(body, outs, operands, limit_mib, flops, bytes_accessed, scratch=(), **grid):
    return pl.pallas_call(
        body,
        out_shape=outs,
        scratch_shapes=list(scratch),
        compiler_params=pltpu.CompilerParams(vmem_limit_bytes=limit_mib * MIB),
        cost_estimate=pl.CostEstimate(
            flops=flops, bytes_accessed=bytes_accessed, transcendentals=0
        ),
        **grid,
    )(*operands)


def f32(*shape):
    return jax.ShapeDtypeStruct(shape, jnp.float32)


def vmem(*shape):
    return pltpu.VMEM(shape, jnp.float32)


def far_out(*shape):
    return pltpu.HBM(shape, jnp.float32)


def hbm(values):
    return pltpu.with_memory_space_constraint(values, pltpu.HBM)


def held(values):
    return pltpu.with_memory_space_constraint(values, pltpu.VMEM)


def iota(shape, axis):
    return lax.broadcasted_iota(jnp.int32, shape, axis)


SERIES = [(-1.0) ** n * (2.0 * math.pi) ** (2 * n) / math.factorial(2 * n) for n in range(10)]


def cos_turns(turns):
    part = turns - jnp.floor(turns + 0.5)
    size = jnp.abs(part)
    flip = size > 0.25
    part = jnp.where(flip, 0.5 - size, size)
    square = part * part
    total = jnp.full_like(square, SERIES[-1])
    for factor in SERIES[-2::-1]:
        total = total * square + factor
    return jnp.where(flip, -total, total)


def mode_of(position, modes):
    return jnp.where(position < modes // 2, position, position - modes)


def turns_of(cell, mode, cells, quarter):
    return (cell * mode).astype(jnp.float32) * (1.0 / cells) - 0.25 * quarter.astype(jnp.float32)


def split(index, size):
    high = index // size
    return high, index - high * size


def table_x(cells, modes, mode_axis, columns=None):
    shape = [cells, cells]
    shape[mode_axis] = columns or 2 * modes
    mode, part = split(iota(tuple(shape), mode_axis), 2)
    value = cos_turns(turns_of(iota(tuple(shape), 1 - mode_axis), mode_of(mode, modes), cells, part))
    value = jnp.where(part == 1, -value, value)
    return jnp.where(mode < modes, value, 0.0)


def pair_table(mode, mode_part, cell, cell_part, modes, cells):
    value = cos_turns(turns_of(cell, mode_of(mode, modes), cells, mode_part ^ cell_part))
    return jnp.where((mode_part == 1) & (cell_part == 0), -value, value)


def table_y(cells, modes, mode_axis):
    shape = [2 * cells, 2 * cells]
    shape[mode_axis] = 2 * modes
    mode_part, mode = split(iota(tuple(shape), mode_axis), modes)
    cell_part, cell = split(iota(tuple(shape), 1 - mode_axis), cells)
    return pair_table(mode, mode_part, cell, cell_part, modes, cells)


def table_z(cells, modes, mode_axis, groups, times=1):
    shape = [2 * cells, 2 * cells]
    shape[mode_axis] = 2 * modes * times
    mode_part, mode = split(iota(tuple(shape), mode_axis) // times, modes)
    depth = cells // groups
    group, rest = split(iota(tuple(shape), 1 - mode_axis), 2 * depth)
    cell_part, cell = split(rest, depth)
    return pair_table(mode, mode_part, cell + group * depth, cell_part, modes, cells)


def gelu_slope(values):
    normal_cdf = 0.5 * (1.0 + lax.erf(values * 0.7071067811865476))
    return normal_cdf + values * jnp.exp(-0.5 * values * values) * 0.3989422804014327


def fetch(sources, targets, sems):
    copies = [
        pltpu.make_async_copy(source, target, sems.at[i])
        for i, (source, target) in enumerate(zip(sources, targets))
    ]
    for copy in copies:
        copy.start()
    return copies


def halves(values):
    high = values.astype(jnp.bfloat16)
    return high, (values - high.astype(jnp.float32)).astype(jnp.bfloat16)


def x_kernel(sizes, in_hbm, pre_hbm, cot_hbm, slope_ref, send_ref, ylast_ref, yfirst_ref,
             zlast_ref, zfirst_ref, in_ref, pre_ref, cot_ref, work_ref, half_ref, sems):
    C, zl, yl, dests, kr = sizes
    copies = fetch((in_hbm, pre_hbm, cot_hbm), (in_ref, pre_ref, cot_ref), sems)
    table = table_x(in_ref.shape[1], dests * kr // 2, 1, dests * kr)
    high, low = halves(table)
    both = jnp.concatenate([high, low], axis=1)
    alone = jnp.concatenate([high, jnp.zeros_like(low)], axis=1)

    def transform(f, field):
        upper, lower = halves(field)
        work_ref[f] = dot(upper, both, precision=None) + dot(lower, alone, precision=None)
        for y in range(yl):
            rows = [work_ref[f, pl.ds(z * yl + y, C, stride=zl * yl), :] for z in range(zl)]
            turned = jnp.concatenate(rows, axis=0).T
            turned = turned[: dests * kr] + turned[dests * kr :]
            for d in range(dests):
                send_ref[pl.ds(((d * 2 + f) * yl + y) * kr, kr), :] = turned[d * kr : (d + 1) * kr]

    copies[0].wait()
    transform(0, in_ref[...])
    copies[1].wait()
    copies[2].wait()
    slope = cot_ref[...] * gelu_slope(pre_ref[...])
    slope_ref[...] = slope
    transform(1, slope)
    for half in range(slope_ref.shape[1] // LANES):
        cut = pl.ds(half * LANES, LANES)
        half_ref[...] = slope[:, half * LANES : (half + 1) * LANES]
        for z in range(zl):
            to = pl.ds(z * C, C)
            ylast_ref[to, cut] = half_ref[pl.ds(z * yl + yl - 1, C, stride=zl * yl), :]
            yfirst_ref[to, cut] = half_ref[pl.ds(z * yl, C, stride=zl * yl), :]
    for c in range(C):
        zlast_ref[pl.ds(c * yl, yl), :] = slope_ref[pl.ds((c * zl + zl - 1) * yl, yl), :]
        zfirst_ref[pl.ds(c * yl, yl), :] = slope_ref[pl.ds(c * zl * yl, yl), :]


def widen(values, lanes):
    spare = lanes - values.shape[1]
    if spare == 0:
        return values
    return jnp.concatenate([values, jnp.zeros((values.shape[0], spare), jnp.float32)], axis=1)


def y_kernel(sizes, recv_ref, *refs):
    send_ref = refs[-1]
    C, zl, kxl, ky, kyl, yl, sources = sizes
    kr = 2 * kxl
    lanes = zl * C
    pieces = []
    for kx in range(kxl):
        for f in range(2):
            pieces.append(
                jnp.concatenate(
                    [
                        recv_ref[pl.ds((s * 2 + f) * yl * kr + kx * 2 + r, yl, stride=kr), :]
                        for r in range(2)
                        for s in range(sources)
                    ],
                    axis=0,
                )
            )
    out = dot(table_y(yl * sources, ky, 0), jnp.concatenate(pieces, axis=1))
    for f in range(2):
        for r in range(2):
            for z in range(zl):
                parts = []
                for kx in range(kxl):
                    base = (kx * 2 + f) * lanes + z * C
                    parts.append(out[r * ky : (r + 1) * ky, base : base + C])
                block = widen(jnp.concatenate(parts, axis=1), send_ref.shape[1])
                for g in range(ky // kyl):
                    start = (g * 2 + f) * kyl * 2 * zl + r * zl + z
                    send_ref[pl.ds(start, kyl, stride=2 * zl), :] = block[g * kyl : (g + 1) * kyl]


def spread(rows, C):
    n, kc = rows.shape
    high = rows.astype(jnp.bfloat16).astype(jnp.float32)
    both = jnp.concatenate([high, rows - high], axis=1)
    own = jnp.remainder(iota((C, 2 * kc), 1), C) == iota((C, 2 * kc), 0)
    wide = jnp.where(own[None], jnp.broadcast_to(both[:, None, :], (n, C, 2 * kc)), 0.0)
    wide = wide.reshape(n * C, 2 * kc).astype(jnp.bfloat16)
    same = jnp.remainder(iota((2 * kc, kc), 0), kc) // C == iota((2 * kc, kc), 1) // C
    return dot(wide, same.astype(jnp.bfloat16), precision=None)


def z_kernel(sizes, recv_ref, weights_hbm, part_hbm, send_ref, hat_ref, weights_ref, part_ref,
             each_ref, sems):
    C, zl, kxl, kyl, kz, groups, part_rows, scale = sizes
    copies = fetch(
        (part_hbm, weights_hbm.at[0], weights_hbm.at[1]),
        (part_ref, weights_ref.at[0], weights_ref.at[1]),
        sems,
    )
    forward = table_z(zl * groups, kz, 1, groups).T
    back_table = table_z(zl * groups, kz, 1, groups, SUB)
    kc = kxl * C
    rows = 2 * zl
    chunk = kyl * rows
    wide = send_ref.shape[1]
    cols = []
    for k in range(kyl):
        for f in range(2):
            cols.append(
                jnp.concatenate(
                    [
                        recv_ref[pl.ds((s * 2 + f) * chunk + k * rows, rows), :]
                        for s in range(groups)
                    ],
                    axis=0,
                )
            )
    hat = dot(forward, jnp.concatenate(cols, axis=1))
    for k in range(kyl):
        slope_hat = None
        for f in range(2):
            base = (k * 2 + f) * wide
            value = hat[:, base : base + wide]
            if f == 1:
                value = value * scale
                slope_hat = value[:, :kc]
            for r in range(2):
                hat_ref[pl.ds((f * 2 + r) * kyl + k, kz, stride=4 * kyl), :] = value[
                    r * kz : (r + 1) * kz
                ]
        each_ref[k] = spread(slope_hat, C).reshape(2, kz, C, kc)
    for copy in copies:
        copy.wait()
    duals = []
    for k in range(kyl):
        w_re, w_im = weights_ref[0, k], weights_ref[1, k]
        re = w_re * each_ref[k, 0] + w_im * each_ref[k, 1]
        im = w_re * each_ref[k, 1] - w_im * each_ref[k, 0]
        dual = jnp.stack([re, im]).reshape(2, kz, C // SUB, SUB, kc)
        duals.append(jnp.sum(dual, axis=2).reshape(2 * kz * SUB, kc))
    back = dot(back_table, jnp.concatenate(duals, axis=1))
    for g in range(groups):
        start = g * (chunk + part_rows)
        for k in range(kyl):
            piece = back[g * rows : (g + 1) * rows, k * kc : (k + 1) * kc]
            send_ref[pl.ds(start + k * rows, rows), :] = widen(piece, wide)
        send_ref[pl.ds(start + chunk, part_rows), :] = part_ref[...]


def grad_kernel(sizes, first, hat_ref, *refs):
    C, kxl, kyl, kz, steps = sizes
    out_hbm, out_ref, sems = refs[-3:]
    kc = kxl * C

    def copy(step):
        return pltpu.make_async_copy(
            out_ref.at[step], out_hbm.at[:, first + step], sems.at[step]
        )

    for step in range(steps):
        base = (first + step) * 4 * kyl
        in_re = hat_ref[pl.ds(base, kyl), :][:, :kc]
        in_im = hat_ref[pl.ds(base + kyl, kyl), :][:, :kc]
        wide = spread(hat_ref[pl.ds(base + 2 * kyl, 2 * kyl), :][:, :kc], C)
        wide = wide.reshape(2, kyl, C, kc)
        re, im = wide[0], wide[1]
        grad_re = re * in_re[:, None, :] + im * in_im[:, None, :]
        grad_im = im * in_re[:, None, :] - re * in_im[:, None, :]
        for kx in range(kxl):
            out_ref[step, 0, :, kx] = grad_re[:, :, kx * C : (kx + 1) * C]
            out_ref[step, 1, :, kx] = grad_im[:, :, kx * C : (kx + 1) * C]
        copy(step).start()
    for step in range(steps):
        copy(step).wait()


def y_back_kernel(sizes, recv_ref, *refs):
    send_ref = refs[-1]
    C, zl, kxl, ky, kyl, cells, yl, groups, dests, part_rows = sizes
    wide = recv_ref.shape[1]
    rows = 2 * zl
    kr = 2 * kxl
    chunk = kyl * rows + part_rows
    out_chunk = yl * kr + part_rows
    cols = []
    for z in range(zl):
        cols.append(
            jnp.concatenate(
                [
                    recv_ref[pl.ds(s * chunk + r * zl + z, kyl, stride=rows), :]
                    for r in range(2)
                    for s in range(groups)
                ],
                axis=0,
            )
        )
    out = dot(table_y(cells, ky, 1), jnp.concatenate(cols, axis=1))
    total = recv_ref[pl.ds(kyl * rows, part_rows), :]
    for s in range(1, groups):
        total = total + recv_ref[pl.ds(s * chunk + kyl * rows, part_rows), :]
    for kx in range(kxl):
        for r in range(2):
            block = out[r * cells : (r + 1) * cells]
            piece = jnp.concatenate(
                [block[:, z * wide + kx * C : z * wide + (kx + 1) * C] for z in range(zl)], axis=1
            )
            for d in range(dests):
                send_ref[pl.ds(d * out_chunk + kx * 2 + r, yl, stride=kr), :] = piece[
                    d * yl : (d + 1) * yl
                ]
    for d in range(dests):
        send_ref[pl.ds(d * out_chunk + yl * kr, part_rows), :] = total


def x_back_kernel(sizes, recv_ref, local_ref, fix_ref, out_ref, mix_ref, coef_ref, work_ref):
    C, zl, yl, kxl, sources, part_rows = sizes
    table = table_x(out_ref.shape[1], sources * kxl, 0)
    kr = 2 * kxl
    chunk = yl * kr + part_rows
    edge = 2 * C * yl
    for y in range(yl):
        column = jnp.concatenate(
            [recv_ref[pl.ds(s * chunk + y * kr, kr), :] for s in range(sources)], axis=0
        )
        value = dot(column.T, table)
        if y == 0:
            value = value + fix_ref[pl.ds(edge, zl * C), :]
        if y == yl - 1:
            value = value + fix_ref[pl.ds(edge + zl * C, zl * C), :]
        for z in range(zl):
            for half in range(value.shape[1] // LANES):
                work_ref[half, pl.ds(z * yl + y, C, stride=zl * yl), :] = value[
                    z * C : (z + 1) * C, half * LANES : (half + 1) * LANES
                ]
    for half in range(out_ref.shape[1] // LANES):
        cut = pl.ds(half * LANES, LANES)
        for c in range(C):
            for z in range(zl):
                row = pl.ds((c * zl + z) * yl, yl)
                value = work_ref[half, row, :] + local_ref[row, cut]
                if z == 0:
                    value = value + fix_ref[pl.ds(c * yl, yl), cut]
                if z == zl - 1:
                    value = value + fix_ref[pl.ds((C + c) * yl, yl), cut]
                out_ref[row, cut] = value
    total = recv_ref[pl.ds(yl * kr, part_rows), :]
    for s in range(1, sources):
        total = total + recv_ref[pl.ds(s * chunk + yl * kr, part_rows), :]
    total = total * (1.0 / 1024.0)
    high = C // kxl
    for b in range(kxl):
        mix_ref[pl.ds(b * high, high), :] = total[:high, b * C : (b + 1) * C]
    coef_ref[...] = total[high : high + 5, :C]


EXACT = PRECISION


def one_hot(rows, columns, times, major):
    if rows > columns:
        channel = iota((rows, columns), 0)
        channel = channel // times if major else jnp.remainder(channel, columns)
        return (channel == iota((rows, columns), 1)).astype(jnp.float32)
    channel = iota((rows, columns), 1)
    channel = channel // times if major else jnp.remainder(channel, rows)
    return (channel == iota((rows, columns), 0)).astype(jnp.float32)


def mixer(mix, C, times, major):
    n = C * times
    tall, flat = one_hot(n, C, times, major), one_hot(C, n, times, major)
    full = dot(dot(tall, mix, ((1,), (1,)), EXACT), flat, precision=EXACT)
    if major:
        place = [jnp.remainder(iota((n, n), axis), times) for axis in range(2)]
    else:
        place = [iota((n, n), axis) // C for axis in range(2)]
    return jnp.where(place[0] == place[1], full, 0.0)


def layer(ref, z, C, zl, yl):
    return jnp.concatenate([ref[pl.ds((c * zl + z) * yl, yl), :] for c in range(C)], axis=0)


def inner_kernel(sizes, in_hbm, slope_ref, mix_hbm, coefs_hbm, weights_hbm, out_ref, gram_ref,
                 sums_ref, packed_ref, in_ref, mix_ref, coefs_ref, raw_ref, sems):
    C, zl, yl, kxl, kyl, kz = sizes
    length = in_ref.shape[1]
    copies = fetch((mix_hbm, coefs_hbm, in_hbm), (mix_ref, coefs_ref, in_ref), sems)

    groups = math.gcd(4, kz)
    size = kz // groups

    def raw_copy(g):
        cut = pl.ds(g * size, size)
        return pltpu.make_async_copy(weights_hbm.at[:, cut], raw_ref.at[:, cut], sems.at[3 + g])

    for g in range(groups):
        raw_copy(g).start()

    def up(values):
        cube = values.reshape(C, yl, length)
        return jnp.concatenate(
            [jnp.zeros((C, 1, length), jnp.float32), cube[:, : yl - 1]], axis=1
        ).reshape(C * yl, length)

    def down(values):
        cube = values.reshape(C, yl, length)
        return jnp.concatenate(
            [cube[:, 1:], jnp.zeros((C, 1, length), jnp.float32)], axis=1
        ).reshape(C * yl, length)

    tall = one_hot(C * yl, C, yl, True)
    copies[0].wait()
    copies[1].wait()
    coef_rows = dot(tall, coefs_ref[...], ((1,), (1,)), EXACT)
    coef = [coef_rows[:, j : j + 1] for j in range(5)]
    kron = mixer(mix_ref[...], C, yl, True)
    slopes = [layer(slope_ref, z, C, zl, yl) for z in range(zl)]
    hidden = [dot(kron, slopes[z]) for z in range(zl)]
    copies[2].wait()
    inputs = [layer(in_ref, z, C, zl, yl) for z in range(zl)]
    gram = None
    sums = [None] * 5
    for z in range(zl):
        shifted = {0: hidden[z], 1: up(hidden[z]), 2: down(hidden[z])}
        if z > 0:
            shifted[3] = hidden[z - 1]
        if z + 1 < zl:
            shifted[4] = hidden[z + 1]
        total = None
        for j, value in shifted.items():
            term = coef[j] * value
            total = term if total is None else total + term
            term = inputs[z] * value
            sums[j] = term if sums[j] is None else sums[j] + term
        for c in range(C):
            out_ref[pl.ds((c * zl + z) * yl, yl), :] = total[c * yl : (c + 1) * yl]
        stencil = coef[0] * inputs[z] + coef[1] * down(inputs[z]) + coef[2] * up(inputs[z])
        if z + 1 < zl:
            stencil = stencil + coef[3] * inputs[z + 1]
        if z > 0:
            stencil = stencil + coef[4] * inputs[z - 1]
        term = dot(slopes[z], stencil, ((1,), (1,)))
        gram = term if gram is None else gram + term
    gram_ref[...] = gram
    columns = []
    for term in sums:
        if term is None:
            columns.append(jnp.zeros((C * yl, 1), jnp.float32))
        else:
            columns.append(jnp.sum(term, axis=1, keepdims=True))
    columns.append(jnp.zeros((C * yl, SUB - 5), jnp.float32))
    sums_ref[...] = jnp.concatenate(columns, axis=1)
    for z in range(kz):
        if z % size == 0:
            raw_copy(z // size).wait()
        for part in range(2):
            for k in range(kyl):
                packed_ref[part, k, z] = jnp.concatenate(
                    [raw_ref[part, z, k, kx] for kx in range(kxl)], axis=1
                )


def edge_kernel(sizes, ybefore_ref, yafter_ref, zbefore_ref, zafter_ref, *refs):
    C, zl, yl, kxl = sizes
    *hbms, fix_ref, part_ref, mix_ref, coefs_ref, in_ref, gram_ref, sums_ref, sems = refs
    copies = fetch(hbms, (mix_ref, coefs_ref, in_ref, gram_ref, sums_ref), sems)

    def inside(ref, axis, place):
        return ref[...] * (lax.axis_index(axis) != place).astype(jnp.float32)

    last_y, last_z = lax.axis_size("gy") - 1, lax.axis_size("gz") - 1
    zbefore, zafter = inside(zbefore_ref, "gz", 0), inside(zafter_ref, "gz", last_z)
    ybefore, yafter = inside(ybefore_ref, "gy", 0), inside(yafter_ref, "gy", last_y)
    copies[0].wait()
    copies[1].wait()
    kron_y = mixer(mix_ref[...], C, yl, True)
    kron_z = mixer(mix_ref[...], C, zl, False)
    hidden_zb, hidden_za = dot(kron_y, zbefore), dot(kron_y, zafter)
    hidden_yb, hidden_ya = dot(kron_z, ybefore), dot(kron_z, yafter)
    for copy in copies[2:]:
        copy.wait()
    length = in_ref.shape[1]
    first, last = layer(in_ref, 0, C, zl, yl), layer(in_ref, zl - 1, C, zl, yl)
    layers = [layer(in_ref, z, C, zl, yl) for z in range(zl)]

    def row_of(y):
        return jnp.concatenate([each.reshape(C, yl, length)[:, y] for each in layers], axis=0)

    low, high_row = row_of(0), row_of(yl - 1)
    flat_y, tall_y = one_hot(C, C * yl, yl, True), one_hot(C * yl, C, yl, True)
    flat_z, tall_z = one_hot(C, C * zl, zl, False), one_hot(C * zl, C, zl, False)
    coef_y = dot(tall_y, coefs_ref[...], ((1,), (1,)), EXACT)
    coef_z = dot(tall_z, coefs_ref[...], ((1,), (1,)), EXACT)
    n, m = C * yl, C * zl
    fix_ref[pl.ds(0, n), :] = coef_y[:, 3:4] * hidden_zb
    fix_ref[pl.ds(n, n), :] = coef_y[:, 4:5] * hidden_za
    fix_ref[pl.ds(2 * n, m), :] = coef_z[:, 1:2] * hidden_yb
    fix_ref[pl.ds(2 * n + m, m), :] = coef_z[:, 2:3] * hidden_ya
    gram = gram_ref[...]
    gram = gram + dot(zbefore, coef_y[:, 3:4] * first, ((1,), (1,)))
    gram = gram + dot(zafter, coef_y[:, 4:5] * last, ((1,), (1,)))
    edge = dot(ybefore, coef_z[:, 1:2] * low, ((1,), (1,)))
    edge = edge + dot(yafter, coef_z[:, 2:3] * high_row, ((1,), (1,)))
    same_y = jnp.remainder(iota((n, n), 0), yl) == jnp.remainder(iota((n, n), 1), yl)
    same_z = iota((m, m), 0) // C == iota((m, m), 1) // C
    mix = dot(dot(flat_y, jnp.where(same_y, gram, 0.0)), flat_y, ((1,), (1,)))
    mix = mix + dot(dot(flat_z, jnp.where(same_z, edge, 0.0)), flat_z, ((1,), (1,)))

    def column(values, place):
        total = jnp.sum(values, axis=1, keepdims=True)
        return jnp.where(iota((values.shape[0], SUB), 1) == place, total, 0.0)

    by_y = sums_ref[...] + column(first * hidden_zb, 3) + column(last * hidden_za, 4)
    by_z = column(low * hidden_yb, 1) + column(high_row * hidden_ya, 2)
    by_channel = dot(flat_y, by_y) + dot(flat_z, by_z)
    eye = (iota((SUB, SUB), 0) == iota((SUB, SUB), 1)).astype(jnp.float32)
    coefs = dot(eye, by_channel, ((1,), (1,)))
    high = C // kxl
    packed = jnp.concatenate([mix[b * high : (b + 1) * high] for b in range(kxl)], axis=1)
    part_ref[pl.ds(0, high), :] = widen(packed, part_ref.shape[1])
    part_ref[pl.ds(high, SUB), :] = widen(coefs, part_ref.shape[1])


def per_device(input_field, pre_activation, cotangent, spectral_weights, mix_weights, coefficients):
    C, zl, yl, length = input_field.shape
    groups_y = lax.axis_size("gy")
    groups_z = lax.axis_size("gz")
    cells_y, cells_z = yl * groups_y, zl * groups_z
    kz, kyl, kxl = spectral_weights.shape[1:4]
    modes_y, modes_x = kyl * groups_z, kxl * groups_y
    scale = 1.0 / (length * cells_y * cells_z)
    rows = C * zl * yl
    kr = 2 * kxl
    kc = kxl * C
    lanes = zl * C
    wide = max(kc, LANES)
    part_rows = C // kxl + SUB

    flat = lambda values: values.reshape(rows, length)
    exchange = functools.partial(lax.all_to_all, split_axis=0, concat_axis=0, tiled=True)
    far = pl.BlockSpec(memory_space=pl.ANY)
    near = pl.BlockSpec(memory_space=pltpu.VMEM)

    slope, send, ylast, yfirst, zlast, zfirst = call(
        functools.partial(x_kernel, (C, zl, yl, groups_y, kr)),
        (
            vmem(rows, length),
            f32(groups_y * 2 * yl * kr, lanes),
            far_out(C * zl, length),
            far_out(C * zl, length),
            far_out(C * yl, length),
            far_out(C * yl, length),
        ),
        (
            hbm(flat(input_field)),
            hbm(flat(pre_activation)),
            hbm(flat(cotangent)),
        ),
        24,
        flops=4 * rows * length * 2 * modes_x,
        bytes_accessed=6 * rows * length * 4,
        in_specs=[far] * 3,
        scratch=[
            pltpu.VMEM((rows, length), jnp.float32),
            pltpu.VMEM((rows, length), jnp.float32),
            pltpu.VMEM((rows, length), jnp.float32),
            pltpu.VMEM((2, rows, 4 * modes_x), jnp.float32),
            pltpu.VMEM((rows, LANES), jnp.float32),
            pltpu.SemaphoreType.DMA((3,)),
        ],
    )
    lines = exchange(send, "gy")

    def from_below(values, axis):
        size = lax.axis_size(axis)
        return lax.ppermute(values, axis, [(i, (i + 1) % size) for i in range(size)])

    def from_above(values, axis):
        size = lax.axis_size(axis)
        return lax.ppermute(values, axis, [((i + 1) % size, i) for i in range(size)])

    ybefore, yafter = from_below(ylast, "gy"), from_above(yfirst, "gy")
    zbefore, zafter = from_below(zlast, "gz"), from_above(zfirst, "gz")

    local, gram, sums, weights = call(
        functools.partial(inner_kernel, (C, zl, yl, kxl, kyl, kz)),
        (
            vmem(rows, length),
            far_out(C * yl, C * yl),
            far_out(C * yl, SUB),
            far_out(2, kyl, kz, C, kc),
        ),
        (
            hbm(flat(input_field)),
            held(slope),
            hbm(mix_weights),
            hbm(coefficients),
            hbm(spectral_weights),
        ),
        44,
        flops=2 * 12 * (C * yl) ** 2 * length,
        bytes_accessed=2 * kz * kyl * kxl * C * 128 * 4 * 2,
        in_specs=[far, near, far, far, far],
        scratch=[
            pltpu.VMEM((rows, length), jnp.float32),
            pltpu.VMEM((C, C), jnp.float32),
            pltpu.VMEM(coefficients.shape, jnp.float32),
            pltpu.VMEM((2, kz, kyl, kxl, C, C), jnp.float32),
            pltpu.SemaphoreType.DMA((3 + math.gcd(4, kz),)),
        ],
    )

    send = call(
        functools.partial(y_kernel, (C, zl, kxl, modes_y, kyl, yl, groups_y)),
        f32(groups_z * 2 * kyl * 2 * zl, wide),
        (lines, held(ybefore), held(yafter), held(zbefore), held(zafter), hbm(weights)),
        16,
        flops=16 * modes_y * cells_y * kxl * lanes,
        bytes_accessed=4 * MIB,
        in_specs=[near] + [far] * 5,
    )
    owned = exchange(send, "gz")

    fix, part = call(
        functools.partial(edge_kernel, (C, zl, yl, kxl)),
        (vmem(2 * C * yl + 2 * C * zl, length), far_out(part_rows, wide)),
        (
            held(ybefore),
            held(yafter),
            held(zbefore),
            held(zafter),
            hbm(mix_weights),
            hbm(coefficients),
            hbm(flat(input_field)),
            hbm(gram),
            hbm(sums),
        ),
        24,
        flops=2 * 6 * (C * yl) ** 2 * length,
        bytes_accessed=3 * MIB,
        in_specs=[near] * 4 + [far] * 5,
        scratch=[
            pltpu.VMEM((C, C), jnp.float32),
            pltpu.VMEM(coefficients.shape, jnp.float32),
            pltpu.VMEM((rows, length), jnp.float32),
            pltpu.VMEM(gram.shape, jnp.float32),
            pltpu.VMEM(sums.shape, jnp.float32),
            pltpu.SemaphoreType.DMA((5,)),
        ],
    )

    chunk = kyl * 2 * zl + part_rows
    send, hats = call(
        functools.partial(z_kernel, (C, zl, kxl, kyl, kz, groups_z, part_rows, scale)),
        (f32(groups_z * chunk, wide), vmem(kz * 4 * kyl, wide)),
        (owned, hbm(weights), hbm(part)),
        24,
        flops=16 * kz * kyl * C * kc,
        bytes_accessed=6 * MIB,
        in_specs=[near, far, far],
        scratch=[
            pltpu.VMEM((2, kyl, kz, C, kc), jnp.float32),
            pltpu.VMEM((part_rows, wide), jnp.float32),
            pltpu.VMEM((kyl, 2, kz, C, kc), jnp.float32),
            pltpu.SemaphoreType.DMA((3,)),
        ],
    )
    returned = exchange(send, "gz")

    def gradient(first, steps, *before):
        return call(
            functools.partial(grad_kernel, (C, kxl, kyl, kz, steps), first),
            pltpu.HBM((2, kz, kyl, kxl, C, C), jnp.float32),
            (held(hats), *[hbm(each) for each in before]),
            16,
            flops=16 * steps * kyl * C * kc,
            bytes_accessed=2 * steps * kyl * kxl * C * 128 * 4,
            in_specs=[near] + [far] * len(before),
            out_specs=far,
            scratch=[
                pltpu.VMEM((steps, 2, kyl, kxl, C, C), jnp.float32),
                pltpu.SemaphoreType.DMA((steps,)),
            ],
            input_output_aliases={1: 0} if before else {},
        )

    few = max(1, kz * 5 // 16)
    grad_half = gradient(0, few)

    send = call(
        functools.partial(
            y_back_kernel,
            (C, zl, kxl, modes_y, kyl, cells_y, yl, groups_z, groups_y, part_rows),
        ),
        f32(groups_y * (yl * kr + part_rows), lanes),
        (returned, hbm(grad_half)),
        16,
        flops=8 * modes_y * cells_y * kxl * lanes,
        bytes_accessed=2 * MIB,
        in_specs=[near, far],
    )
    arrived = exchange(send, "gy")
    grad_spectral = gradient(few, kz - few, grad_half)

    grad_input, grad_mix, grad_coef = call(
        functools.partial(x_back_kernel, (C, zl, yl, kxl, groups_y, part_rows)),
        (f32(rows, length), f32(C, C), f32(5, C)),
        (arrived, held(local), held(fix)),
        16,
        flops=2 * rows * length * 2 * modes_x,
        bytes_accessed=3 * MIB,
        scratch=[pltpu.VMEM((length // LANES, rows, LANES), jnp.float32)],
    )
    return (grad_input.reshape(input_field.shape), grad_spectral, grad_mix, grad_coef)


def solution(mesh):
    in_specs = (
        P(None, "gz", "gy", None),
        P(None, "gz", "gy", None),
        P(None, "gz", "gy", None),
        P(None, None, "gz", "gy", None, None),
        P(),
        P(),
    )
    out_specs = (P(None, "gz", "gy", None), P(None, None, "gz", "gy", None, None), P(), P())
    return jax.shard_map(
        per_device, mesh=mesh, in_specs=in_specs, out_specs=out_specs, check_vma=False
    )
```

```python
import functools
import math

import jax
import jax.numpy as jnp
import numpy as np
from jax import lax
from jax.experimental import pallas as pl
from jax.experimental.pallas import tpu as pltpu
from jax.sharding import PartitionSpec as P

PRECISION = lax.Precision.HIGH
MIB = 1 << 20
SUB = 8
LANES = 128


def dot(left, right, dims=((1,), (0,)), precision=PRECISION):
    return lax.dot_general(
        left, right, (dims, ((), ())), precision=precision, preferred_element_type=jnp.float32
    )


def call(body, outs, operands, limit_mib, flops, bytes_accessed, scratch=(), **grid):
    return pl.pallas_call(
        body,
        out_shape=outs,
        scratch_shapes=list(scratch),
        compiler_params=pltpu.CompilerParams(vmem_limit_bytes=limit_mib * MIB),
        cost_estimate=pl.CostEstimate(
            flops=flops, bytes_accessed=bytes_accessed, transcendentals=0
        ),
        **grid,
    )(*operands)


def f32(*shape):
    return jax.ShapeDtypeStruct(shape, jnp.float32)


def vmem(*shape):
    return pltpu.VMEM(shape, jnp.float32)


def far_out(*shape):
    return pltpu.HBM(shape, jnp.float32)


def hbm(values):
    return pltpu.with_memory_space_constraint(values, pltpu.HBM)


def held(values):
    return pltpu.with_memory_space_constraint(values, pltpu.VMEM)


def iota(shape, axis):
    return lax.broadcasted_iota(jnp.int32, shape, axis)


SERIES = [(-1.0) ** n * (2.0 * math.pi) ** (2 * n) / math.factorial(2 * n) for n in range(10)]


def cos_turns(turns):
    part = turns - jnp.floor(turns + 0.5)
    size = jnp.abs(part)
    flip = size > 0.25
    part = jnp.where(flip, 0.5 - size, size)
    square = part * part
    total = jnp.full_like(square, SERIES[-1])
    for factor in SERIES[-2::-1]:
        total = total * square + factor
    return jnp.where(flip, -total, total)


def mode_of(position, modes):
    return jnp.where(position < modes // 2, position, position - modes)


def turns_of(cell, mode, cells, quarter):
    return (cell * mode).astype(jnp.float32) * (1.0 / cells) - 0.25 * quarter.astype(jnp.float32)


def split(index, size):
    high = index // size
    return high, index - high * size


def table_x(cells, modes, mode_axis, columns=None):
    shape = [cells, cells]
    shape[mode_axis] = columns or 2 * modes
    mode, part = split(iota(tuple(shape), mode_axis), 2)
    value = cos_turns(turns_of(iota(tuple(shape), 1 - mode_axis), mode_of(mode, modes), cells, part))
    value = jnp.where(part == 1, -value, value)
    return jnp.where(mode < modes, value, 0.0)


def pair_table(mode, mode_part, cell, cell_part, modes, cells):
    value = cos_turns(turns_of(cell, mode_of(mode, modes), cells, mode_part ^ cell_part))
    return jnp.where((mode_part == 1) & (cell_part == 0), -value, value)


def table_y(cells, modes, mode_axis):
    shape = [2 * cells, 2 * cells]
    shape[mode_axis] = 2 * modes
    mode_part, mode = split(iota(tuple(shape), mode_axis), modes)
    cell_part, cell = split(iota(tuple(shape), 1 - mode_axis), cells)
    return pair_table(mode, mode_part, cell, cell_part, modes, cells)


def table_z(cells, modes, mode_axis, groups, times=1):
    shape = [2 * cells, 2 * cells]
    shape[mode_axis] = 2 * modes * times
    mode_part, mode = split(iota(tuple(shape), mode_axis) // times, modes)
    depth = cells // groups
    group, rest = split(iota(tuple(shape), 1 - mode_axis), 2 * depth)
    cell_part, cell = split(rest, depth)
    return pair_table(mode, mode_part, cell + group * depth, cell_part, modes, cells)


def gelu_slope(values):
    normal_cdf = 0.5 * (1.0 + lax.erf(values * 0.7071067811865476))
    return normal_cdf + values * jnp.exp(-0.5 * values * values) * 0.3989422804014327


def fetch(sources, targets, sems):
    copies = [
        pltpu.make_async_copy(source, target, sems.at[i])
        for i, (source, target) in enumerate(zip(sources, targets))
    ]
    for copy in copies:
        copy.start()
    return copies


def halves(values):
    high = values.astype(jnp.bfloat16)
    return high, (values - high.astype(jnp.float32)).astype(jnp.bfloat16)


def x_kernel(sizes, in_hbm, pre_hbm, cot_hbm, slope_ref, send_ref, ylast_ref, yfirst_ref,
             zlast_ref, zfirst_ref, in_ref, pre_ref, cot_ref, work_ref, half_ref, sems):
    C, zl, yl, dests, kr = sizes
    copies = fetch((in_hbm, pre_hbm, cot_hbm), (in_ref, pre_ref, cot_ref), sems)
    table = table_x(in_ref.shape[1], dests * kr // 2, 1, dests * kr)
    high, low = halves(table)
    both = jnp.concatenate([high, low], axis=1)
    alone = jnp.concatenate([high, jnp.zeros_like(low)], axis=1)

    def transform(f, field):
        upper, lower = halves(field)
        work_ref[f] = dot(upper, both, precision=None) + dot(lower, alone, precision=None)
        for y in range(yl):
            rows = [work_ref[f, pl.ds(z * yl + y, C, stride=zl * yl), :] for z in range(zl)]
            turned = jnp.concatenate(rows, axis=0).T
            turned = turned[: dests * kr] + turned[dests * kr :]
            for d in range(dests):
                send_ref[pl.ds(((d * 2 + f) * yl + y) * kr, kr), :] = turned[d * kr : (d + 1) * kr]

    copies[0].wait()
    transform(0, in_ref[...])
    copies[1].wait()
    copies[2].wait()
    slope = cot_ref[...] * gelu_slope(pre_ref[...])
    slope_ref[...] = slope
    transform(1, slope)
    for half in range(slope_ref.shape[1] // LANES):
        cut = pl.ds(half * LANES, LANES)
        half_ref[...] = slope[:, half * LANES : (half + 1) * LANES]
        for z in range(zl):
            to = pl.ds(z * C, C)
            ylast_ref[to, cut] = half_ref[pl.ds(z * yl + yl - 1, C, stride=zl * yl), :]
            yfirst_ref[to, cut] = half_ref[pl.ds(z * yl, C, stride=zl * yl), :]
    for c in range(C):
        zlast_ref[pl.ds(c * yl, yl), :] = slope_ref[pl.ds((c * zl + zl - 1) * yl, yl), :]
        zfirst_ref[pl.ds(c * yl, yl), :] = slope_ref[pl.ds(c * zl * yl, yl), :]


def widen(values, lanes):
    spare = lanes - values.shape[1]
    if spare == 0:
        return values
    return jnp.concatenate([values, jnp.zeros((values.shape[0], spare), jnp.float32)], axis=1)


def y_kernel(sizes, recv_ref, *refs):
    send_ref = refs[-1]
    C, zl, kxl, ky, kyl, yl, sources = sizes
    kr = 2 * kxl
    lanes = zl * C
    pieces = []
    for kx in range(kxl):
        for f in range(2):
            pieces.append(
                jnp.concatenate(
                    [
                        recv_ref[pl.ds((s * 2 + f) * yl * kr + kx * 2 + r, yl, stride=kr), :]
                        for r in range(2)
                        for s in range(sources)
                    ],
                    axis=0,
                )
            )
    out = dot(table_y(yl * sources, ky, 0), jnp.concatenate(pieces, axis=1))
    for f in range(2):
        for r in range(2):
            for z in range(zl):
                parts = []
                for kx in range(kxl):
                    base = (kx * 2 + f) * lanes + z * C
                    parts.append(out[r * ky : (r + 1) * ky, base : base + C])
                block = widen(jnp.concatenate(parts, axis=1), send_ref.shape[1])
                for g in range(ky // kyl):
                    start = (g * 2 + f) * kyl * 2 * zl + r * zl + z
                    send_ref[pl.ds(start, kyl, stride=2 * zl), :] = block[g * kyl : (g + 1) * kyl]


def spread(rows, C):
    n, kc = rows.shape
    high = rows.astype(jnp.bfloat16).astype(jnp.float32)
    both = jnp.concatenate([high, rows - high], axis=1)
    own = jnp.remainder(iota((C, 2 * kc), 1), C) == iota((C, 2 * kc), 0)
    wide = jnp.where(own[None], jnp.broadcast_to(both[:, None, :], (n, C, 2 * kc)), 0.0)
    wide = wide.reshape(n * C, 2 * kc).astype(jnp.bfloat16)
    same = jnp.remainder(iota((2 * kc, kc), 0), kc) // C == iota((2 * kc, kc), 1) // C
    return dot(wide, same.astype(jnp.bfloat16), precision=None)


def z_kernel(sizes, recv_ref, weights_hbm, part_hbm, send_ref, hat_ref, weights_ref, part_ref,
             each_ref, sems):
    C, zl, kxl, kyl, kz, groups, part_rows, scale = sizes
    copies = fetch(
        (part_hbm, weights_hbm.at[0], weights_hbm.at[1]),
        (part_ref, weights_ref.at[0], weights_ref.at[1]),
        sems,
    )
    forward = table_z(zl * groups, kz, 1, groups).T
    back_table = table_z(zl * groups, kz, 1, groups, SUB)
    kc = kxl * C
    rows = 2 * zl
    chunk = kyl * rows
    wide = send_ref.shape[1]
    cols = []
    for k in range(kyl):
        for f in range(2):
            cols.append(
                jnp.concatenate(
                    [
                        recv_ref[pl.ds((s * 2 + f) * chunk + k * rows, rows), :]
                        for s in range(groups)
                    ],
                    axis=0,
                )
            )
    hat = dot(forward, jnp.concatenate(cols, axis=1))
    for k in range(kyl):
        slope_hat = None
        for f in range(2):
            base = (k * 2 + f) * wide
            value = hat[:, base : base + wide]
            if f == 1:
                value = value * scale
                slope_hat = value[:, :kc]
            for r in range(2):
                hat_ref[pl.ds((f * 2 + r) * kyl + k, kz, stride=4 * kyl), :] = value[
                    r * kz : (r + 1) * kz
                ]
        each_ref[k] = spread(slope_hat, C).reshape(2, kz, C, kc)
    for copy in copies:
        copy.wait()
    duals = []
    for k in range(kyl):
        w_re, w_im = weights_ref[0, k], weights_ref[1, k]
        re = w_re * each_ref[k, 0] + w_im * each_ref[k, 1]
        im = w_re * each_ref[k, 1] - w_im * each_ref[k, 0]
        dual = jnp.stack([re, im]).reshape(2, kz, C // SUB, SUB, kc)
        duals.append(jnp.sum(dual, axis=2).reshape(2 * kz * SUB, kc))
    back = dot(back_table, jnp.concatenate(duals, axis=1))
    for g in range(groups):
        start = g * (chunk + part_rows)
        for k in range(kyl):
            piece = back[g * rows : (g + 1) * rows, k * kc : (k + 1) * kc]
            send_ref[pl.ds(start + k * rows, rows), :] = widen(piece, wide)
        send_ref[pl.ds(start + chunk, part_rows), :] = part_ref[...]


def grad_kernel(sizes, first, hat_ref, *refs):
    C, kxl, kyl, kz, steps = sizes
    out_hbm, out_ref, sems = refs[-3:]
    kc = kxl * C

    def copy(step):
        return pltpu.make_async_copy(
            out_ref.at[step], out_hbm.at[:, first + step], sems.at[step]
        )

    for step in range(steps):
        base = (first + step) * 4 * kyl
        in_re = hat_ref[pl.ds(base, kyl), :][:, :kc]
        in_im = hat_ref[pl.ds(base + kyl, kyl), :][:, :kc]
        wide = spread(hat_ref[pl.ds(base + 2 * kyl, 2 * kyl), :][:, :kc], C)
        wide = wide.reshape(2, kyl, C, kc)
        re, im = wide[0], wide[1]
        grad_re = re * in_re[:, None, :] + im * in_im[:, None, :]
        grad_im = im * in_re[:, None, :] - re * in_im[:, None, :]
        for kx in range(kxl):
            out_ref[step, 0, :, kx] = grad_re[:, :, kx * C : (kx + 1) * C]
            out_ref[step, 1, :, kx] = grad_im[:, :, kx * C : (kx + 1) * C]
        copy(step).start()
    for step in range(steps):
        copy(step).wait()


def y_back_kernel(sizes, recv_ref, *refs):
    send_ref = refs[-1]
    C, zl, kxl, ky, kyl, cells, yl, groups, dests, part_rows = sizes
    wide = recv_ref.shape[1]
    rows = 2 * zl
    kr = 2 * kxl
    chunk = kyl * rows + part_rows
    out_chunk = yl * kr + part_rows
    cols = []
    for z in range(zl):
        cols.append(
            jnp.concatenate(
                [
                    recv_ref[pl.ds(s * chunk + r * zl + z, kyl, stride=rows), :]
                    for r in range(2)
                    for s in range(groups)
                ],
                axis=0,
            )
        )
    out = dot(table_y(cells, ky, 1), jnp.concatenate(cols, axis=1))
    total = recv_ref[pl.ds(kyl * rows, part_rows), :]
    for s in range(1, groups):
        total = total + recv_ref[pl.ds(s * chunk + kyl * rows, part_rows), :]
    for kx in range(kxl):
        for r in range(2):
            block = out[r * cells : (r + 1) * cells]
            piece = jnp.concatenate(
                [block[:, z * wide + kx * C : z * wide + (kx + 1) * C] for z in range(zl)], axis=1
            )
            for d in range(dests):
                send_ref[pl.ds(d * out_chunk + kx * 2 + r, yl, stride=kr), :] = piece[
                    d * yl : (d + 1) * yl
                ]
    for d in range(dests):
        send_ref[pl.ds(d * out_chunk + yl * kr, part_rows), :] = total


def x_back_kernel(sizes, recv_ref, local_ref, fix_ref, out_ref, mix_ref, coef_ref, work_ref):
    C, zl, yl, kxl, sources, part_rows = sizes
    table = table_x(out_ref.shape[1], sources * kxl, 0)
    kr = 2 * kxl
    chunk = yl * kr + part_rows
    edge = 2 * C * yl
    for y in range(yl):
        column = jnp.concatenate(
            [recv_ref[pl.ds(s * chunk + y * kr, kr), :] for s in range(sources)], axis=0
        )
        value = dot(column.T, table)
        if y == 0:
            value = value + fix_ref[pl.ds(edge, zl * C), :]
        if y == yl - 1:
            value = value + fix_ref[pl.ds(edge + zl * C, zl * C), :]
        for z in range(zl):
            for half in range(value.shape[1] // LANES):
                work_ref[half, pl.ds(z * yl + y, C, stride=zl * yl), :] = value[
                    z * C : (z + 1) * C, half * LANES : (half + 1) * LANES
                ]
    for half in range(out_ref.shape[1] // LANES):
        cut = pl.ds(half * LANES, LANES)
        for c in range(C):
            for z in range(zl):
                row = pl.ds((c * zl + z) * yl, yl)
                value = work_ref[half, row, :] + local_ref[row, cut]
                if z == 0:
                    value = value + fix_ref[pl.ds(c * yl, yl), cut]
                if z == zl - 1:
                    value = value + fix_ref[pl.ds((C + c) * yl, yl), cut]
                out_ref[row, cut] = value
    total = recv_ref[pl.ds(yl * kr, part_rows), :]
    for s in range(1, sources):
        total = total + recv_ref[pl.ds(s * chunk + yl * kr, part_rows), :]
    total = total * (1.0 / 1024.0)
    high = C // kxl
    for b in range(kxl):
        mix_ref[pl.ds(b * high, high), :] = total[:high, b * C : (b + 1) * C]
    coef_ref[...] = total[high : high + 5, :C]


EXACT = PRECISION


def one_hot(rows, columns, times, major):
    if rows > columns:
        channel = iota((rows, columns), 0)
        channel = channel // times if major else jnp.remainder(channel, columns)
        return (channel == iota((rows, columns), 1)).astype(jnp.float32)
    channel = iota((rows, columns), 1)
    channel = channel // times if major else jnp.remainder(channel, rows)
    return (channel == iota((rows, columns), 0)).astype(jnp.float32)


def mixer(mix, C, times, major):
    n = C * times
    tall, flat = one_hot(n, C, times, major), one_hot(C, n, times, major)
    full = dot(dot(tall, mix, ((1,), (1,)), EXACT), flat, precision=EXACT)
    if major:
        place = [jnp.remainder(iota((n, n), axis), times) for axis in range(2)]
    else:
        place = [iota((n, n), axis) // C for axis in range(2)]
    return jnp.where(place[0] == place[1], full, 0.0)


def layer(ref, z, C, zl, yl):
    return jnp.concatenate([ref[pl.ds((c * zl + z) * yl, yl), :] for c in range(C)], axis=0)


def inner_kernel(sizes, in_hbm, slope_ref, mix_hbm, coefs_hbm, weights_hbm, out_ref, gram_ref,
                 sums_ref, kron_ref, packed_ref, in_ref, mix_ref, coefs_ref, raw_ref, sems):
    C, zl, yl, kxl, kyl, kz = sizes
    length = in_ref.shape[1]
    copies = fetch((mix_hbm, coefs_hbm, in_hbm), (mix_ref, coefs_ref, in_ref), sems)

    groups = math.gcd(4, kz)
    size = kz // groups

    def raw_copy(g):
        cut = pl.ds(g * size, size)
        return pltpu.make_async_copy(weights_hbm.at[:, cut], raw_ref.at[:, cut], sems.at[3 + g])

    for g in range(groups):
        raw_copy(g).start()

    def up(values):
        cube = values.reshape(C, yl, length)
        return jnp.concatenate(
            [jnp.zeros((C, 1, length), jnp.float32), cube[:, : yl - 1]], axis=1
        ).reshape(C * yl, length)

    def down(values):
        cube = values.reshape(C, yl, length)
        return jnp.concatenate(
            [cube[:, 1:], jnp.zeros((C, 1, length), jnp.float32)], axis=1
        ).reshape(C * yl, length)

    tall = one_hot(C * yl, C, yl, True)
    copies[0].wait()
    copies[1].wait()
    coef_rows = dot(tall, coefs_ref[...], ((1,), (1,)), EXACT)
    coef = [coef_rows[:, j : j + 1] for j in range(5)]
    kron = mixer(mix_ref[...], C, yl, True)
    kron_ref[...] = kron
    slopes = [layer(slope_ref, z, C, zl, yl) for z in range(zl)]
    hidden = [dot(kron, slopes[z]) for z in range(zl)]
    copies[2].wait()
    inputs = [layer(in_ref, z, C, zl, yl) for z in range(zl)]
    gram = None
    sums = [None] * 5
    for z in range(zl):
        shifted = {0: hidden[z], 1: up(hidden[z]), 2: down(hidden[z])}
        if z > 0:
            shifted[3] = hidden[z - 1]
        if z + 1 < zl:
            shifted[4] = hidden[z + 1]
        total = None
        for j, value in shifted.items():
            term = coef[j] * value
            total = term if total is None else total + term
            term = inputs[z] * value
            sums[j] = term if sums[j] is None else sums[j] + term
        for c in range(C):
            out_ref[pl.ds((c * zl + z) * yl, yl), :] = total[c * yl : (c + 1) * yl]
        stencil = coef[0] * inputs[z] + coef[1] * down(inputs[z]) + coef[2] * up(inputs[z])
        if z + 1 < zl:
            stencil = stencil + coef[3] * inputs[z + 1]
        if z > 0:
            stencil = stencil + coef[4] * inputs[z - 1]
        term = dot(slopes[z], stencil, ((1,), (1,)))
        gram = term if gram is None else gram + term
    gram_ref[...] = gram
    columns = []
    for term in sums:
        if term is None:
            columns.append(jnp.zeros((C * yl, 1), jnp.float32))
        else:
            columns.append(jnp.sum(term, axis=1, keepdims=True))
    columns.append(jnp.zeros((C * yl, SUB - 5), jnp.float32))
    sums_ref[...] = jnp.concatenate(columns, axis=1)
    for z in range(kz):
        if z % size == 0:
            raw_copy(z // size).wait()
        for part in range(2):
            for k in range(kyl):
                packed_ref[part, k, z] = jnp.concatenate(
                    [raw_ref[part, z, k, kx] for kx in range(kxl)], axis=1
                )


def edge_kernel(sizes, ybefore_ref, yafter_ref, zbefore_ref, zafter_ref, *refs):
    C, zl, yl, kxl = sizes
    hbms, (fix_ref, part_ref), refs, sems = refs[:6], refs[6:8], refs[8:-1], refs[-1]
    copies = fetch(hbms, refs, sems)
    mix_ref, coefs_ref, kron_ref, in_ref, gram_ref, sums_ref = refs

    def inside(ref, axis, place):
        return ref[...] * (lax.axis_index(axis) != place).astype(jnp.float32)

    last_y, last_z = lax.axis_size("gy") - 1, lax.axis_size("gz") - 1
    zbefore, zafter = inside(zbefore_ref, "gz", 0), inside(zafter_ref, "gz", last_z)
    ybefore, yafter = inside(ybefore_ref, "gy", 0), inside(yafter_ref, "gy", last_y)
    for copy in copies:
        copy.wait()
    kron_y = kron_ref[...]
    kron_z = mixer(mix_ref[...], C, zl, False)
    hidden_zb, hidden_za = dot(kron_y, zbefore), dot(kron_y, zafter)
    hidden_yb, hidden_ya = dot(kron_z, ybefore), dot(kron_z, yafter)
    length = in_ref.shape[1]
    first, last = layer(in_ref, 0, C, zl, yl), layer(in_ref, zl - 1, C, zl, yl)
    layers = [layer(in_ref, z, C, zl, yl) for z in range(zl)]

    def row_of(y):
        return jnp.concatenate([each.reshape(C, yl, length)[:, y] for each in layers], axis=0)

    low, high_row = row_of(0), row_of(yl - 1)
    flat_y, tall_y = one_hot(C, C * yl, yl, True), one_hot(C * yl, C, yl, True)
    flat_z, tall_z = one_hot(C, C * zl, zl, False), one_hot(C * zl, C, zl, False)
    coef_y = dot(tall_y, coefs_ref[...], ((1,), (1,)), EXACT)
    coef_z = dot(tall_z, coefs_ref[...], ((1,), (1,)), EXACT)
    n, m = C * yl, C * zl
    fix_ref[pl.ds(0, n), :] = coef_y[:, 3:4] * hidden_zb
    fix_ref[pl.ds(n, n), :] = coef_y[:, 4:5] * hidden_za
    fix_ref[pl.ds(2 * n, m), :] = coef_z[:, 1:2] * hidden_yb
    fix_ref[pl.ds(2 * n + m, m), :] = coef_z[:, 2:3] * hidden_ya
    gram = gram_ref[...]
    gram = gram + dot(zbefore, coef_y[:, 3:4] * first, ((1,), (1,)))
    gram = gram + dot(zafter, coef_y[:, 4:5] * last, ((1,), (1,)))
    edge = dot(ybefore, coef_z[:, 1:2] * low, ((1,), (1,)))
    edge = edge + dot(yafter, coef_z[:, 2:3] * high_row, ((1,), (1,)))
    same_y = jnp.remainder(iota((n, n), 0), yl) == jnp.remainder(iota((n, n), 1), yl)
    same_z = iota((m, m), 0) // C == iota((m, m), 1) // C
    mix = dot(dot(flat_y, jnp.where(same_y, gram, 0.0)), flat_y, ((1,), (1,)))
    mix = mix + dot(dot(flat_z, jnp.where(same_z, edge, 0.0)), flat_z, ((1,), (1,)))

    def column(values, place):
        total = jnp.sum(values, axis=1, keepdims=True)
        return jnp.where(iota((values.shape[0], SUB), 1) == place, total, 0.0)

    by_y = sums_ref[...] + column(first * hidden_zb, 3) + column(last * hidden_za, 4)
    by_z = column(low * hidden_yb, 1) + column(high_row * hidden_ya, 2)
    by_channel = dot(flat_y, by_y) + dot(flat_z, by_z)
    eye = (iota((SUB, SUB), 0) == iota((SUB, SUB), 1)).astype(jnp.float32)
    coefs = dot(eye, by_channel, ((1,), (1,)))
    high = C // kxl
    packed = jnp.concatenate([mix[b * high : (b + 1) * high] for b in range(kxl)], axis=1)
    part_ref[pl.ds(0, high), :] = widen(packed, part_ref.shape[1])
    part_ref[pl.ds(high, SUB), :] = widen(coefs, part_ref.shape[1])


def per_device(input_field, pre_activation, cotangent, spectral_weights, mix_weights, coefficients):
    C, zl, yl, length = input_field.shape
    groups_y = lax.axis_size("gy")
    groups_z = lax.axis_size("gz")
    cells_y, cells_z = yl * groups_y, zl * groups_z
    kz, kyl, kxl = spectral_weights.shape[1:4]
    modes_y, modes_x = kyl * groups_z, kxl * groups_y
    scale = 1.0 / (length * cells_y * cells_z)
    rows = C * zl * yl
    kr = 2 * kxl
    kc = kxl * C
    lanes = zl * C
    wide = max(kc, LANES)
    part_rows = C // kxl + SUB

    flat = lambda values: values.reshape(rows, length)
    exchange = functools.partial(lax.all_to_all, split_axis=0, concat_axis=0, tiled=True)
    far = pl.BlockSpec(memory_space=pl.ANY)
    near = pl.BlockSpec(memory_space=pltpu.VMEM)

    slope, send, ylast, yfirst, zlast, zfirst = call(
        functools.partial(x_kernel, (C, zl, yl, groups_y, kr)),
        (
            vmem(rows, length),
            f32(groups_y * 2 * yl * kr, lanes),
            far_out(C * zl, length),
            far_out(C * zl, length),
            far_out(C * yl, length),
            far_out(C * yl, length),
        ),
        (
            hbm(flat(input_field)),
            hbm(flat(pre_activation)),
            hbm(flat(cotangent)),
        ),
        24,
        flops=4 * rows * length * 2 * modes_x,
        bytes_accessed=6 * rows * length * 4,
        in_specs=[far] * 3,
        scratch=[
            pltpu.VMEM((rows, length), jnp.float32),
            pltpu.VMEM((rows, length), jnp.float32),
            pltpu.VMEM((rows, length), jnp.float32),
            pltpu.VMEM((2, rows, 4 * modes_x), jnp.float32),
            pltpu.VMEM((rows, LANES), jnp.float32),
            pltpu.SemaphoreType.DMA((3,)),
        ],
    )
    lines = exchange(send, "gy")

    def from_below(values, axis):
        size = lax.axis_size(axis)
        return lax.ppermute(values, axis, [(i, (i + 1) % size) for i in range(size)])

    def from_above(values, axis):
        size = lax.axis_size(axis)
        return lax.ppermute(values, axis, [((i + 1) % size, i) for i in range(size)])

    ybefore, yafter = from_below(ylast, "gy"), from_above(yfirst, "gy")
    zbefore, zafter = from_below(zlast, "gz"), from_above(zfirst, "gz")

    local, gram, sums, kron, weights = call(
        functools.partial(inner_kernel, (C, zl, yl, kxl, kyl, kz)),
        (
            vmem(rows, length),
            far_out(C * yl, C * yl),
            far_out(C * yl, SUB),
            far_out(C * yl, C * yl),
            far_out(2, kyl, kz, C, kc),
        ),
        (
            hbm(flat(input_field)),
            held(slope),
            hbm(mix_weights),
            hbm(coefficients),
            hbm(spectral_weights),
        ),
        44,
        flops=2 * 12 * (C * yl) ** 2 * length,
        bytes_accessed=2 * kz * kyl * kxl * C * 128 * 4 * 2,
        in_specs=[far, near, far, far, far],
        scratch=[
            pltpu.VMEM((rows, length), jnp.float32),
            pltpu.VMEM((C, C), jnp.float32),
            pltpu.VMEM(coefficients.shape, jnp.float32),
            pltpu.VMEM((2, kz, kyl, kxl, C, C), jnp.float32),
            pltpu.SemaphoreType.DMA((3 + math.gcd(4, kz),)),
        ],
    )

    send = call(
        functools.partial(y_kernel, (C, zl, kxl, modes_y, kyl, yl, groups_y)),
        f32(groups_z * 2 * kyl * 2 * zl, wide),
        (lines, held(ybefore), held(yafter), held(zbefore), held(zafter), hbm(weights)),
        16,
        flops=16 * modes_y * cells_y * kxl * lanes,
        bytes_accessed=4 * MIB,
        in_specs=[near] + [far] * 5,
    )
    owned = exchange(send, "gz")

    fix, part = call(
        functools.partial(edge_kernel, (C, zl, yl, kxl)),
        (vmem(2 * C * yl + 2 * C * zl, length), far_out(part_rows, wide)),
        (
            held(ybefore),
            held(yafter),
            held(zbefore),
            held(zafter),
            hbm(mix_weights),
            hbm(coefficients),
            hbm(kron),
            hbm(flat(input_field)),
            hbm(gram),
            hbm(sums),
        ),
        24,
        flops=2 * 6 * (C * yl) ** 2 * length,
        bytes_accessed=3 * MIB,
        in_specs=[near] * 4 + [far] * 6,
        scratch=[
            pltpu.VMEM((C, C), jnp.float32),
            pltpu.VMEM(coefficients.shape, jnp.float32),
            pltpu.VMEM(kron.shape, jnp.float32),
            pltpu.VMEM((rows, length), jnp.float32),
            pltpu.VMEM(gram.shape, jnp.float32),
            pltpu.VMEM(sums.shape, jnp.float32),
            pltpu.SemaphoreType.DMA((6,)),
        ],
    )

    chunk = kyl * 2 * zl + part_rows
    send, hats = call(
        functools.partial(z_kernel, (C, zl, kxl, kyl, kz, groups_z, part_rows, scale)),
        (f32(groups_z * chunk, wide), vmem(kz * 4 * kyl, wide)),
        (owned, hbm(weights), hbm(part)),
        24,
        flops=16 * kz * kyl * C * kc,
        bytes_accessed=6 * MIB,
        in_specs=[near, far, far],
        scratch=[
            pltpu.VMEM((2, kyl, kz, C, kc), jnp.float32),
            pltpu.VMEM((part_rows, wide), jnp.float32),
            pltpu.VMEM((kyl, 2, kz, C, kc), jnp.float32),
            pltpu.SemaphoreType.DMA((3,)),
        ],
    )
    returned = exchange(send, "gz")

    def gradient(first, steps, *before):
        return call(
            functools.partial(grad_kernel, (C, kxl, kyl, kz, steps), first),
            pltpu.HBM((2, kz, kyl, kxl, C, C), jnp.float32),
            (held(hats), *[hbm(each) for each in before]),
            16,
            flops=16 * steps * kyl * C * kc,
            bytes_accessed=2 * steps * kyl * kxl * C * 128 * 4,
            in_specs=[near] + [far] * len(before),
            out_specs=far,
            scratch=[
                pltpu.VMEM((steps, 2, kyl, kxl, C, C), jnp.float32),
                pltpu.SemaphoreType.DMA((steps,)),
            ],
            input_output_aliases={1: 0} if before else {},
        )

    few = max(1, kz * 5 // 16)
    grad_half = gradient(0, few)

    send = call(
        functools.partial(
            y_back_kernel,
            (C, zl, kxl, modes_y, kyl, cells_y, yl, groups_z, groups_y, part_rows),
        ),
        f32(groups_y * (yl * kr + part_rows), lanes),
        (returned, hbm(grad_half)),
        16,
        flops=8 * modes_y * cells_y * kxl * lanes,
        bytes_accessed=2 * MIB,
        in_specs=[near, far],
    )
    arrived = exchange(send, "gy")
    grad_spectral = gradient(few, kz - few, grad_half)

    grad_input, grad_mix, grad_coef = call(
        functools.partial(x_back_kernel, (C, zl, yl, kxl, groups_y, part_rows)),
        (f32(rows, length), f32(C, C), f32(5, C)),
        (arrived, held(local), held(fix)),
        16,
        flops=2 * rows * length * 2 * modes_x,
        bytes_accessed=3 * MIB,
        scratch=[pltpu.VMEM((length // LANES, rows, LANES), jnp.float32)],
    )
    return (grad_input.reshape(input_field.shape), grad_spectral, grad_mix, grad_coef)


def solution(mesh):
    in_specs = (
        P(None, "gz", "gy", None),
        P(None, "gz", "gy", None),
        P(None, "gz", "gy", None),
        P(None, None, "gz", "gy", None, None),
        P(),
        P(),
    )
    out_specs = (P(None, "gz", "gy", None), P(None, None, "gz", "gy", None, None), P(), P())
    return jax.shard_map(
        per_device, mesh=mesh, in_specs=in_specs, out_specs=out_specs, check_vma=False
    )
```

```python
import functools
import math

import jax
import jax.numpy as jnp
import numpy as np
from jax import lax
from jax.experimental import pallas as pl
from jax.experimental.pallas import tpu as pltpu
from jax.sharding import PartitionSpec as P

PRECISION = lax.Precision.HIGH
MIB = 1 << 20
SUB = 8
LANES = 128


def dot(left, right, dims=((1,), (0,)), precision=PRECISION):
    return lax.dot_general(
        left, right, (dims, ((), ())), precision=precision, preferred_element_type=jnp.float32
    )


def call(body, outs, operands, limit_mib, flops, bytes_accessed, scratch=(), **grid):
    return pl.pallas_call(
        body,
        out_shape=outs,
        scratch_shapes=list(scratch),
        compiler_params=pltpu.CompilerParams(vmem_limit_bytes=limit_mib * MIB),
        cost_estimate=pl.CostEstimate(
            flops=flops, bytes_accessed=bytes_accessed, transcendentals=0
        ),
        **grid,
    )(*operands)


def f32(*shape):
    return jax.ShapeDtypeStruct(shape, jnp.float32)


def vmem(*shape):
    return pltpu.VMEM(shape, jnp.float32)


def far_out(*shape):
    return pltpu.HBM(shape, jnp.float32)


def hbm(values):
    return pltpu.with_memory_space_constraint(values, pltpu.HBM)


def held(values):
    return pltpu.with_memory_space_constraint(values, pltpu.VMEM)


def iota(shape, axis):
    return lax.broadcasted_iota(jnp.int32, shape, axis)


SERIES = [(-1.0) ** n * (2.0 * math.pi) ** (2 * n) / math.factorial(2 * n) for n in range(10)]


def cos_turns(turns):
    part = turns - jnp.floor(turns + 0.5)
    size = jnp.abs(part)
    flip = size > 0.25
    part = jnp.where(flip, 0.5 - size, size)
    square = part * part
    total = jnp.full_like(square, SERIES[-1])
    for factor in SERIES[-2::-1]:
        total = total * square + factor
    return jnp.where(flip, -total, total)


def mode_of(position, modes):
    return jnp.where(position < modes // 2, position, position - modes)


def turns_of(cell, mode, cells, quarter):
    return (cell * mode).astype(jnp.float32) * (1.0 / cells) - 0.25 * quarter.astype(jnp.float32)


def split(index, size):
    high = index // size
    return high, index - high * size


def table_x(cells, modes, mode_axis, columns=None):
    shape = [cells, cells]
    shape[mode_axis] = columns or 2 * modes
    mode, part = split(iota(tuple(shape), mode_axis), 2)
    value = cos_turns(turns_of(iota(tuple(shape), 1 - mode_axis), mode_of(mode, modes), cells, part))
    value = jnp.where(part == 1, -value, value)
    return jnp.where(mode < modes, value, 0.0)


def pair_table(mode, mode_part, cell, cell_part, modes, cells):
    value = cos_turns(turns_of(cell, mode_of(mode, modes), cells, mode_part ^ cell_part))
    return jnp.where((mode_part == 1) & (cell_part == 0), -value, value)


def table_y(cells, modes, mode_axis):
    shape = [2 * cells, 2 * cells]
    shape[mode_axis] = 2 * modes
    mode_part, mode = split(iota(tuple(shape), mode_axis), modes)
    cell_part, cell = split(iota(tuple(shape), 1 - mode_axis), cells)
    return pair_table(mode, mode_part, cell, cell_part, modes, cells)


def table_z(cells, modes, mode_axis, groups, times=1):
    shape = [2 * cells, 2 * cells]
    shape[mode_axis] = 2 * modes * times
    mode_part, mode = split(iota(tuple(shape), mode_axis) // times, modes)
    depth = cells // groups
    group, rest = split(iota(tuple(shape), 1 - mode_axis), 2 * depth)
    cell_part, cell = split(rest, depth)
    return pair_table(mode, mode_part, cell + group * depth, cell_part, modes, cells)


def gelu_slope(values):
    normal_cdf = 0.5 * (1.0 + lax.erf(values * 0.7071067811865476))
    return normal_cdf + values * jnp.exp(-0.5 * values * values) * 0.3989422804014327


def fetch(sources, targets, sems):
    copies = [
        pltpu.make_async_copy(source, target, sems.at[i])
        for i, (source, target) in enumerate(zip(sources, targets))
    ]
    for copy in copies:
        copy.start()
    return copies


def halves(values):
    high = values.astype(jnp.bfloat16)
    return high, (values - high.astype(jnp.float32)).astype(jnp.bfloat16)


def x_kernel(sizes, in_hbm, pre_hbm, cot_hbm, slope_ref, send_ref, ylast_ref, yfirst_ref,
             zlast_ref, zfirst_ref, in_ref, pre_ref, cot_ref, work_ref, half_ref, sems):
    C, zl, yl, dests, kr = sizes
    copies = fetch((in_hbm, pre_hbm, cot_hbm), (in_ref, pre_ref, cot_ref), sems)
    table = table_x(in_ref.shape[1], dests * kr // 2, 1, dests * kr)
    high, low = halves(table)
    both = jnp.concatenate([high, low], axis=1)
    alone = jnp.concatenate([high, jnp.zeros_like(low)], axis=1)

    def transform(f, field):
        upper, lower = halves(field)
        work_ref[f] = dot(upper, both, precision=None) + dot(lower, alone, precision=None)
        for y in range(yl):
            rows = [work_ref[f, pl.ds(z * yl + y, C, stride=zl * yl), :] for z in range(zl)]
            turned = jnp.concatenate(rows, axis=0).T
            turned = turned[: dests * kr] + turned[dests * kr :]
            for d in range(dests):
                send_ref[pl.ds(((d * 2 + f) * yl + y) * kr, kr), :] = turned[d * kr : (d + 1) * kr]

    copies[0].wait()
    transform(0, in_ref[...])
    copies[1].wait()
    copies[2].wait()
    slope = cot_ref[...] * gelu_slope(pre_ref[...])
    slope_ref[...] = slope
    transform(1, slope)
    for half in range(slope_ref.shape[1] // LANES):
        cut = pl.ds(half * LANES, LANES)
        half_ref[...] = slope[:, half * LANES : (half + 1) * LANES]
        for z in range(zl):
            to = pl.ds(z * C, C)
            ylast_ref[to, cut] = half_ref[pl.ds(z * yl + yl - 1, C, stride=zl * yl), :]
            yfirst_ref[to, cut] = half_ref[pl.ds(z * yl, C, stride=zl * yl), :]
    for c in range(C):
        zlast_ref[pl.ds(c * yl, yl), :] = slope_ref[pl.ds((c * zl + zl - 1) * yl, yl), :]
        zfirst_ref[pl.ds(c * yl, yl), :] = slope_ref[pl.ds(c * zl * yl, yl), :]


def widen(values, lanes):
    spare = lanes - values.shape[1]
    if spare == 0:
        return values
    return jnp.concatenate([values, jnp.zeros((values.shape[0], spare), jnp.float32)], axis=1)


def y_kernel(sizes, recv_ref, *refs):
    send_ref = refs[-1]
    C, zl, kxl, ky, kyl, yl, sources = sizes
    kr = 2 * kxl
    lanes = zl * C
    pieces = []
    for kx in range(kxl):
        for f in range(2):
            pieces.append(
                jnp.concatenate(
                    [
                        recv_ref[pl.ds((s * 2 + f) * yl * kr + kx * 2 + r, yl, stride=kr), :]
                        for r in range(2)
                        for s in range(sources)
                    ],
                    axis=0,
                )
            )
    out = dot(table_y(yl * sources, ky, 0), jnp.concatenate(pieces, axis=1))
    for f in range(2):
        for r in range(2):
            for z in range(zl):
                parts = []
                for kx in range(kxl):
                    base = (kx * 2 + f) * lanes + z * C
                    parts.append(out[r * ky : (r + 1) * ky, base : base + C])
                block = widen(jnp.concatenate(parts, axis=1), send_ref.shape[1])
                for g in range(ky // kyl):
                    start = (g * 2 + f) * kyl * 2 * zl + r * zl + z
                    send_ref[pl.ds(start, kyl, stride=2 * zl), :] = block[g * kyl : (g + 1) * kyl]


def spread(rows, C):
    n, kc = rows.shape
    high = rows.astype(jnp.bfloat16).astype(jnp.float32)
    both = jnp.concatenate([high, rows - high], axis=1)
    own = jnp.remainder(iota((C, 2 * kc), 1), C) == iota((C, 2 * kc), 0)
    wide = jnp.where(own[None], jnp.broadcast_to(both[:, None, :], (n, C, 2 * kc)), 0.0)
    wide = wide.reshape(n * C, 2 * kc).astype(jnp.bfloat16)
    same = jnp.remainder(iota((2 * kc, kc), 0), kc) // C == iota((2 * kc, kc), 1) // C
    return dot(wide, same.astype(jnp.bfloat16), precision=None)


def z_kernel(sizes, recv_ref, weights_hbm, part_hbm, send_ref, hat_ref, weights_ref, part_ref,
             each_ref, sems):
    C, zl, kxl, kyl, kz, groups, part_rows, scale = sizes
    copies = fetch(
        (part_hbm, weights_hbm.at[0], weights_hbm.at[1]),
        (part_ref, weights_ref.at[0], weights_ref.at[1]),
        sems,
    )
    forward = table_z(zl * groups, kz, 1, groups).T
    back_table = table_z(zl * groups, kz, 1, groups, SUB)
    kc = kxl * C
    rows = 2 * zl
    chunk = kyl * rows
    wide = send_ref.shape[1]
    cols = []
    for k in range(kyl):
        for f in range(2):
            cols.append(
                jnp.concatenate(
                    [
                        recv_ref[pl.ds((s * 2 + f) * chunk + k * rows, rows), :]
                        for s in range(groups)
                    ],
                    axis=0,
                )
            )
    hat = dot(forward, jnp.concatenate(cols, axis=1))
    for k in range(kyl):
        slope_hat = None
        for f in range(2):
            base = (k * 2 + f) * wide
            value = hat[:, base : base + wide]
            if f == 1:
                value = value * scale
                slope_hat = value[:, :kc]
            for r in range(2):
                hat_ref[pl.ds((f * 2 + r) * kyl + k, kz, stride=4 * kyl), :] = value[
                    r * kz : (r + 1) * kz
                ]
        each_ref[k] = spread(slope_hat, C).reshape(2, kz, C, kc)
    for copy in copies:
        copy.wait()
    duals = []
    for k in range(kyl):
        w_re, w_im = weights_ref[0, k], weights_ref[1, k]
        re = w_re * each_ref[k, 0] + w_im * each_ref[k, 1]
        im = w_re * each_ref[k, 1] - w_im * each_ref[k, 0]
        dual = jnp.stack([re, im]).reshape(2, kz, C // SUB, SUB, kc)
        duals.append(jnp.sum(dual, axis=2).reshape(2 * kz * SUB, kc))
    back = dot(back_table, jnp.concatenate(duals, axis=1))
    for g in range(groups):
        start = g * (chunk + part_rows)
        for k in range(kyl):
            piece = back[g * rows : (g + 1) * rows, k * kc : (k + 1) * kc]
            send_ref[pl.ds(start + k * rows, rows), :] = widen(piece, wide)
        send_ref[pl.ds(start + chunk, part_rows), :] = part_ref[...]


def grad_kernel(sizes, first, hat_ref, *refs):
    C, kxl, kyl, kz, steps = sizes
    out_hbm, out_ref, sems = refs[-3:]
    kc = kxl * C

    def copy(step):
        return pltpu.make_async_copy(
            out_ref.at[step], out_hbm.at[:, first + step], sems.at[step]
        )

    for step in range(steps):
        base = (first + step) * 4 * kyl
        in_re = hat_ref[pl.ds(base, kyl), :][:, :kc]
        in_im = hat_ref[pl.ds(base + kyl, kyl), :][:, :kc]
        wide = spread(hat_ref[pl.ds(base + 2 * kyl, 2 * kyl), :][:, :kc], C)
        wide = wide.reshape(2, kyl, C, kc)
        re, im = wide[0], wide[1]
        grad_re = re * in_re[:, None, :] + im * in_im[:, None, :]
        grad_im = im * in_re[:, None, :] - re * in_im[:, None, :]
        for kx in range(kxl):
            out_ref[step, 0, :, kx] = grad_re[:, :, kx * C : (kx + 1) * C]
            out_ref[step, 1, :, kx] = grad_im[:, :, kx * C : (kx + 1) * C]
        copy(step).start()
    for step in range(steps):
        copy(step).wait()


def y_back_kernel(sizes, recv_ref, *refs):
    send_ref = refs[-1]
    C, zl, kxl, ky, kyl, cells, yl, groups, dests, part_rows = sizes
    wide = recv_ref.shape[1]
    rows = 2 * zl
    kr = 2 * kxl
    chunk = kyl * rows + part_rows
    out_chunk = yl * kr + part_rows
    cols = []
    for z in range(zl):
        cols.append(
            jnp.concatenate(
                [
                    recv_ref[pl.ds(s * chunk + r * zl + z, kyl, stride=rows), :]
                    for r in range(2)
                    for s in range(groups)
                ],
                axis=0,
            )
        )
    out = dot(table_y(cells, ky, 1), jnp.concatenate(cols, axis=1))
    total = recv_ref[pl.ds(kyl * rows, part_rows), :]
    for s in range(1, groups):
        total = total + recv_ref[pl.ds(s * chunk + kyl * rows, part_rows), :]
    for kx in range(kxl):
        for r in range(2):
            block = out[r * cells : (r + 1) * cells]
            piece = jnp.concatenate(
                [block[:, z * wide + kx * C : z * wide + (kx + 1) * C] for z in range(zl)], axis=1
            )
            for d in range(dests):
                send_ref[pl.ds(d * out_chunk + kx * 2 + r, yl, stride=kr), :] = piece[
                    d * yl : (d + 1) * yl
                ]
    for d in range(dests):
        send_ref[pl.ds(d * out_chunk + yl * kr, part_rows), :] = total


def x_back_kernel(sizes, recv_ref, local_ref, fix_ref, out_ref, mix_ref, coef_ref, work_ref):
    C, zl, yl, kxl, sources, part_rows = sizes
    table = table_x(out_ref.shape[1], sources * kxl, 0)
    kr = 2 * kxl
    chunk = yl * kr + part_rows
    edge = 2 * C * yl
    for y in range(yl):
        column = jnp.concatenate(
            [recv_ref[pl.ds(s * chunk + y * kr, kr), :] for s in range(sources)], axis=0
        )
        value = dot(column.T, table)
        if y == 0:
            value = value + fix_ref[pl.ds(edge, zl * C), :]
        if y == yl - 1:
            value = value + fix_ref[pl.ds(edge + zl * C, zl * C), :]
        for z in range(zl):
            for half in range(value.shape[1] // LANES):
                work_ref[half, pl.ds(z * yl + y, C, stride=zl * yl), :] = value[
                    z * C : (z + 1) * C, half * LANES : (half + 1) * LANES
                ]
    for half in range(out_ref.shape[1] // LANES):
        cut = pl.ds(half * LANES, LANES)
        for c in range(C):
            for z in range(zl):
                row = pl.ds((c * zl + z) * yl, yl)
                value = work_ref[half, row, :] + local_ref[row, cut]
                if z == 0:
                    value = value + fix_ref[pl.ds(c * yl, yl), cut]
                if z == zl - 1:
                    value = value + fix_ref[pl.ds((C + c) * yl, yl), cut]
                out_ref[row, cut] = value
    total = recv_ref[pl.ds(yl * kr, part_rows), :]
    for s in range(1, sources):
        total = total + recv_ref[pl.ds(s * chunk + yl * kr, part_rows), :]
    total = total * (1.0 / 1024.0)
    high = C // kxl
    for b in range(kxl):
        mix_ref[pl.ds(b * high, high), :] = total[:high, b * C : (b + 1) * C]
    coef_ref[...] = total[high : high + 5, :C]


EXACT = PRECISION


def one_hot(rows, columns, times, major):
    if rows > columns:
        channel = iota((rows, columns), 0)
        channel = channel // times if major else jnp.remainder(channel, columns)
        return (channel == iota((rows, columns), 1)).astype(jnp.float32)
    channel = iota((rows, columns), 1)
    channel = channel // times if major else jnp.remainder(channel, rows)
    return (channel == iota((rows, columns), 0)).astype(jnp.float32)


def mixer(mix, C, times, major):
    n = C * times
    tall, flat = one_hot(n, C, times, major), one_hot(C, n, times, major)
    full = dot(dot(tall, mix, ((1,), (1,)), EXACT), flat, precision=EXACT)
    if major:
        place = [jnp.remainder(iota((n, n), axis), times) for axis in range(2)]
    else:
        place = [iota((n, n), axis) // C for axis in range(2)]
    return jnp.where(place[0] == place[1], full, 0.0)


def layer(ref, z, C, zl, yl):
    return jnp.concatenate([ref[pl.ds((c * zl + z) * yl, yl), :] for c in range(C)], axis=0)


def inner_kernel(sizes, in_hbm, slope_ref, mix_hbm, coefs_hbm, weights_hbm, out_ref, gram_ref,
                 sums_ref, kron_ref, packed_ref, in_ref, mix_ref, coefs_ref, raw_ref, sems):
    C, zl, yl, kxl, kyl, kz = sizes
    length = in_ref.shape[1]
    copies = fetch((mix_hbm, coefs_hbm, in_hbm), (mix_ref, coefs_ref, in_ref), sems)

    groups = math.gcd(4, kz)
    size = kz // groups

    def raw_copy(g):
        cut = pl.ds(g * size, size)
        return pltpu.make_async_copy(weights_hbm.at[:, cut], raw_ref.at[:, cut], sems.at[3 + g])

    for g in range(groups):
        raw_copy(g).start()

    def up(values):
        cube = values.reshape(C, yl, length)
        return jnp.concatenate(
            [jnp.zeros((C, 1, length), jnp.float32), cube[:, : yl - 1]], axis=1
        ).reshape(C * yl, length)

    def down(values):
        cube = values.reshape(C, yl, length)
        return jnp.concatenate(
            [cube[:, 1:], jnp.zeros((C, 1, length), jnp.float32)], axis=1
        ).reshape(C * yl, length)

    tall = one_hot(C * yl, C, yl, True)
    copies[0].wait()
    copies[1].wait()
    coef_rows = dot(tall, coefs_ref[...], ((1,), (1,)), EXACT)
    coef = [coef_rows[:, j : j + 1] for j in range(5)]
    kron = mixer(mix_ref[...], C, yl, True)
    kron_ref[...] = kron
    slopes = [layer(slope_ref, z, C, zl, yl) for z in range(zl)]
    hidden = [dot(kron, slopes[z]) for z in range(zl)]
    copies[2].wait()
    inputs = [layer(in_ref, z, C, zl, yl) for z in range(zl)]
    gram = None
    sums = [None] * 5
    for z in range(zl):
        shifted = {0: hidden[z], 1: up(hidden[z]), 2: down(hidden[z])}
        if z > 0:
            shifted[3] = hidden[z - 1]
        if z + 1 < zl:
            shifted[4] = hidden[z + 1]
        total = None
        for j, value in shifted.items():
            term = coef[j] * value
            total = term if total is None else total + term
            term = inputs[z] * value
            sums[j] = term if sums[j] is None else sums[j] + term
        for c in range(C):
            out_ref[pl.ds((c * zl + z) * yl, yl), :] = total[c * yl : (c + 1) * yl]
        stencil = coef[0] * inputs[z] + coef[1] * down(inputs[z]) + coef[2] * up(inputs[z])
        if z + 1 < zl:
            stencil = stencil + coef[3] * inputs[z + 1]
        if z > 0:
            stencil = stencil + coef[4] * inputs[z - 1]
        term = dot(slopes[z], stencil, ((1,), (1,)))
        gram = term if gram is None else gram + term
    gram_ref[...] = gram
    columns = []
    for term in sums:
        if term is None:
            columns.append(jnp.zeros((C * yl, 1), jnp.float32))
        else:
            columns.append(jnp.sum(term, axis=1, keepdims=True))
    columns.append(jnp.zeros((C * yl, SUB - 5), jnp.float32))
    sums_ref[...] = jnp.concatenate(columns, axis=1)
    for z in range(kz):
        if z % size == 0:
            raw_copy(z // size).wait()
        for part in range(2):
            for k in range(kyl):
                packed_ref[part, k, z] = jnp.concatenate(
                    [raw_ref[part, z, k, kx] for kx in range(kxl)], axis=1
                )


def edge_kernel(sizes, ybefore_ref, yafter_ref, zbefore_ref, zafter_ref, *refs):
    C, zl, yl, kxl = sizes
    hbms, (fix_ref, part_ref), refs, sems = refs[:6], refs[6:8], refs[8:-1], refs[-1]
    copies = fetch(hbms, refs, sems)
    mix_ref, coefs_ref, kron_ref, in_ref, gram_ref, sums_ref = refs

    def inside(ref, axis, place):
        return ref[...] * (lax.axis_index(axis) != place).astype(jnp.float32)

    last_y, last_z = lax.axis_size("gy") - 1, lax.axis_size("gz") - 1
    zbefore, zafter = inside(zbefore_ref, "gz", 0), inside(zafter_ref, "gz", last_z)
    ybefore, yafter = inside(ybefore_ref, "gy", 0), inside(yafter_ref, "gy", last_y)
    for copy in copies:
        copy.wait()
    kron_y = kron_ref[...]
    kron_z = mixer(mix_ref[...], C, zl, False)
    hidden_zb, hidden_za = dot(kron_y, zbefore), dot(kron_y, zafter)
    hidden_yb, hidden_ya = dot(kron_z, ybefore), dot(kron_z, yafter)
    length = in_ref.shape[1]
    first, last = layer(in_ref, 0, C, zl, yl), layer(in_ref, zl - 1, C, zl, yl)
    layers = [layer(in_ref, z, C, zl, yl) for z in range(zl)]

    def row_of(y):
        return jnp.concatenate([each.reshape(C, yl, length)[:, y] for each in layers], axis=0)

    low, high_row = row_of(0), row_of(yl - 1)
    flat_y, tall_y = one_hot(C, C * yl, yl, True), one_hot(C * yl, C, yl, True)
    flat_z, tall_z = one_hot(C, C * zl, zl, False), one_hot(C * zl, C, zl, False)
    coef_y = dot(tall_y, coefs_ref[...], ((1,), (1,)), EXACT)
    coef_z = dot(tall_z, coefs_ref[...], ((1,), (1,)), EXACT)
    n, m = C * yl, C * zl
    fix_ref[pl.ds(0, n), :] = coef_y[:, 3:4] * hidden_zb
    fix_ref[pl.ds(n, n), :] = coef_y[:, 4:5] * hidden_za
    fix_ref[pl.ds(2 * n, m), :] = coef_z[:, 1:2] * hidden_yb
    fix_ref[pl.ds(2 * n + m, m), :] = coef_z[:, 2:3] * hidden_ya
    gram = gram_ref[...]
    gram = gram + dot(zbefore, coef_y[:, 3:4] * first, ((1,), (1,)))
    gram = gram + dot(zafter, coef_y[:, 4:5] * last, ((1,), (1,)))
    edge = dot(ybefore, coef_z[:, 1:2] * low, ((1,), (1,)))
    edge = edge + dot(yafter, coef_z[:, 2:3] * high_row, ((1,), (1,)))
    same_y = jnp.remainder(iota((n, n), 0), yl) == jnp.remainder(iota((n, n), 1), yl)
    same_z = iota((m, m), 0) // C == iota((m, m), 1) // C
    mix = dot(dot(flat_y, jnp.where(same_y, gram, 0.0)), flat_y, ((1,), (1,)))
    mix = mix + dot(dot(flat_z, jnp.where(same_z, edge, 0.0)), flat_z, ((1,), (1,)))

    def column(values, place):
        total = jnp.sum(values, axis=1, keepdims=True)
        return jnp.where(iota((values.shape[0], SUB), 1) == place, total, 0.0)

    by_y = sums_ref[...] + column(first * hidden_zb, 3) + column(last * hidden_za, 4)
    by_z = column(low * hidden_yb, 1) + column(high_row * hidden_ya, 2)
    by_channel = dot(flat_y, by_y) + dot(flat_z, by_z)
    eye = (iota((SUB, SUB), 0) == iota((SUB, SUB), 1)).astype(jnp.float32)
    coefs = dot(eye, by_channel, ((1,), (1,)))
    high = C // kxl
    packed = jnp.concatenate([mix[b * high : (b + 1) * high] for b in range(kxl)], axis=1)
    part_ref[pl.ds(0, high), :] = widen(packed, part_ref.shape[1])
    part_ref[pl.ds(high, SUB), :] = widen(coefs, part_ref.shape[1])


def per_device(input_field, pre_activation, cotangent, spectral_weights, mix_weights, coefficients):
    C, zl, yl, length = input_field.shape
    groups_y = lax.axis_size("gy")
    groups_z = lax.axis_size("gz")
    cells_y, cells_z = yl * groups_y, zl * groups_z
    kz, kyl, kxl = spectral_weights.shape[1:4]
    modes_y, modes_x = kyl * groups_z, kxl * groups_y
    scale = 1.0 / (length * cells_y * cells_z)
    rows = C * zl * yl
    kr = 2 * kxl
    kc = kxl * C
    lanes = zl * C
    wide = max(kc, LANES)
    part_rows = C // kxl + SUB

    flat = lambda values: values.reshape(rows, length)
    exchange = functools.partial(lax.all_to_all, split_axis=0, concat_axis=0, tiled=True)
    far = pl.BlockSpec(memory_space=pl.ANY)
    near = pl.BlockSpec(memory_space=pltpu.VMEM)

    slope, send, ylast, yfirst, zlast, zfirst = call(
        functools.partial(x_kernel, (C, zl, yl, groups_y, kr)),
        (
            vmem(rows, length),
            f32(groups_y * 2 * yl * kr, lanes),
            far_out(C * zl, length),
            far_out(C * zl, length),
            far_out(C * yl, length),
            far_out(C * yl, length),
        ),
        (
            hbm(flat(input_field)),
            hbm(flat(pre_activation)),
            hbm(flat(cotangent)),
        ),
        24,
        flops=4 * rows * length * 2 * modes_x,
        bytes_accessed=6 * rows * length * 4,
        in_specs=[far] * 3,
        scratch=[
            pltpu.VMEM((rows, length), jnp.float32),
            pltpu.VMEM((rows, length), jnp.float32),
            pltpu.VMEM((rows, length), jnp.float32),
            pltpu.VMEM((2, rows, 4 * modes_x), jnp.float32),
            pltpu.VMEM((rows, LANES), jnp.float32),
            pltpu.SemaphoreType.DMA((3,)),
        ],
    )
    lines = exchange(send, "gy")

    def from_below(values, axis):
        size = lax.axis_size(axis)
        return lax.ppermute(values, axis, [(i, (i + 1) % size) for i in range(size)])

    def from_above(values, axis):
        size = lax.axis_size(axis)
        return lax.ppermute(values, axis, [((i + 1) % size, i) for i in range(size)])

    ybefore, yafter = from_below(ylast, "gy"), from_above(yfirst, "gy")
    zbefore, zafter = from_below(zlast, "gz"), from_above(zfirst, "gz")

    local, gram, sums, kron, weights = call(
        functools.partial(inner_kernel, (C, zl, yl, kxl, kyl, kz)),
        (
            vmem(rows, length),
            far_out(C * yl, C * yl),
            far_out(C * yl, SUB),
            far_out(C * yl, C * yl),
            far_out(2, kyl, kz, C, kc),
        ),
        (
            hbm(flat(input_field)),
            held(slope),
            hbm(mix_weights),
            hbm(coefficients),
            hbm(spectral_weights),
        ),
        44,
        flops=2 * 12 * (C * yl) ** 2 * length,
        bytes_accessed=2 * kz * kyl * kxl * C * 128 * 4 * 2,
        in_specs=[far, near, far, far, far],
        scratch=[
            pltpu.VMEM((rows, length), jnp.float32),
            pltpu.VMEM((C, C), jnp.float32),
            pltpu.VMEM(coefficients.shape, jnp.float32),
            pltpu.VMEM((2, kz, kyl, kxl, C, C), jnp.float32),
            pltpu.SemaphoreType.DMA((3 + math.gcd(4, kz),)),
        ],
    )

    send = call(
        functools.partial(y_kernel, (C, zl, kxl, modes_y, kyl, yl, groups_y)),
        f32(groups_z * 2 * kyl * 2 * zl, wide),
        (lines, held(ybefore), held(yafter), held(zbefore), held(zafter), hbm(weights)),
        16,
        flops=16 * modes_y * cells_y * kxl * lanes,
        bytes_accessed=4 * MIB,
        in_specs=[near] + [far] * 5,
    )
    owned = exchange(send, "gz")

    fix, part = call(
        functools.partial(edge_kernel, (C, zl, yl, kxl)),
        (vmem(2 * C * yl + 2 * C * zl, length), far_out(part_rows, wide)),
        (
            held(ybefore),
            held(yafter),
            held(zbefore),
            held(zafter),
            hbm(mix_weights),
            hbm(coefficients),
            hbm(kron),
            hbm(flat(input_field)),
            hbm(gram),
            hbm(sums),
        ),
        24,
        flops=2 * 6 * (C * yl) ** 2 * length,
        bytes_accessed=3 * MIB,
        in_specs=[near] * 4 + [far] * 6,
        scratch=[
            pltpu.VMEM((C, C), jnp.float32),
            pltpu.VMEM(coefficients.shape, jnp.float32),
            pltpu.VMEM(kron.shape, jnp.float32),
            pltpu.VMEM((rows, length), jnp.float32),
            pltpu.VMEM(gram.shape, jnp.float32),
            pltpu.VMEM(sums.shape, jnp.float32),
            pltpu.SemaphoreType.DMA((6,)),
        ],
    )

    chunk = kyl * 2 * zl + part_rows
    send, hats = call(
        functools.partial(z_kernel, (C, zl, kxl, kyl, kz, groups_z, part_rows, scale)),
        (f32(groups_z * chunk, wide), vmem(kz * 4 * kyl, wide)),
        (owned, hbm(weights), hbm(part)),
        24,
        flops=16 * kz * kyl * C * kc,
        bytes_accessed=6 * MIB,
        in_specs=[near, far, far],
        scratch=[
            pltpu.VMEM((2, kyl, kz, C, kc), jnp.float32),
            pltpu.VMEM((part_rows, wide), jnp.float32),
            pltpu.VMEM((kyl, 2, kz, C, kc), jnp.float32),
            pltpu.SemaphoreType.DMA((3,)),
        ],
    )
    returned = exchange(send, "gz")

    def gradient(first, steps, *before):
        return call(
            functools.partial(grad_kernel, (C, kxl, kyl, kz, steps), first),
            pltpu.HBM((2, kz, kyl, kxl, C, C), jnp.float32),
            (held(hats), *[hbm(each) for each in before]),
            16,
            flops=16 * steps * kyl * C * kc,
            bytes_accessed=2 * steps * kyl * kxl * C * 128 * 4,
            in_specs=[near] + [far] * len(before),
            out_specs=far,
            scratch=[
                pltpu.VMEM((steps, 2, kyl, kxl, C, C), jnp.float32),
                pltpu.SemaphoreType.DMA((steps,)),
            ],
            input_output_aliases={1: 0} if before else {},
        )

    few = max(1, kz * 3 // 16)
    grad_half = gradient(0, few)

    send = call(
        functools.partial(
            y_back_kernel,
            (C, zl, kxl, modes_y, kyl, cells_y, yl, groups_z, groups_y, part_rows),
        ),
        f32(groups_y * (yl * kr + part_rows), lanes),
        (returned, hbm(grad_half)),
        16,
        flops=8 * modes_y * cells_y * kxl * lanes,
        bytes_accessed=2 * MIB,
        in_specs=[near, far],
    )
    arrived = exchange(send, "gy")
    grad_spectral = gradient(few, kz - few, grad_half)

    grad_input, grad_mix, grad_coef = call(
        functools.partial(x_back_kernel, (C, zl, yl, kxl, groups_y, part_rows)),
        (f32(rows, length), f32(C, C), f32(5, C)),
        (arrived, held(local), held(fix)),
        16,
        flops=2 * rows * length * 2 * modes_x,
        bytes_accessed=3 * MIB,
        scratch=[pltpu.VMEM((length // LANES, rows, LANES), jnp.float32)],
    )
    return (grad_input.reshape(input_field.shape), grad_spectral, grad_mix, grad_coef)


def solution(mesh):
    in_specs = (
        P(None, "gz", "gy", None),
        P(None, "gz", "gy", None),
        P(None, "gz", "gy", None),
        P(None, None, "gz", "gy", None, None),
        P(),
        P(),
    )
    out_specs = (P(None, "gz", "gy", None), P(None, None, "gz", "gy", None, None), P(), P())
    return jax.shard_map(
        per_device, mesh=mesh, in_specs=in_specs, out_specs=out_specs, check_vma=False
    )
```

```python
import functools
import math

import jax
import jax.numpy as jnp
import numpy as np
from jax import lax
from jax.experimental import pallas as pl
from jax.experimental.pallas import tpu as pltpu
from jax.sharding import PartitionSpec as P

PRECISION = lax.Precision.HIGH
MIB = 1 << 20
SUB = 8
LANES = 128


def dot(left, right, dims=((1,), (0,)), precision=PRECISION):
    return lax.dot_general(
        left, right, (dims, ((), ())), precision=precision, preferred_element_type=jnp.float32
    )


def call(body, outs, operands, limit_mib, flops, bytes_accessed, scratch=(), **grid):
    return pl.pallas_call(
        body,
        out_shape=outs,
        scratch_shapes=list(scratch),
        compiler_params=pltpu.CompilerParams(vmem_limit_bytes=limit_mib * MIB),
        cost_estimate=pl.CostEstimate(
            flops=flops, bytes_accessed=bytes_accessed, transcendentals=0
        ),
        **grid,
    )(*operands)


def f32(*shape):
    return jax.ShapeDtypeStruct(shape, jnp.float32)


def vmem(*shape):
    return pltpu.VMEM(shape, jnp.float32)


def far_out(*shape):
    return pltpu.HBM(shape, jnp.float32)


def hbm(values):
    return pltpu.with_memory_space_constraint(values, pltpu.HBM)


def held(values):
    return pltpu.with_memory_space_constraint(values, pltpu.VMEM)


def iota(shape, axis):
    return lax.broadcasted_iota(jnp.int32, shape, axis)


SERIES = [(-1.0) ** n * (2.0 * math.pi) ** (2 * n) / math.factorial(2 * n) for n in range(10)]


def cos_turns(turns):
    part = turns - jnp.floor(turns + 0.5)
    size = jnp.abs(part)
    flip = size > 0.25
    part = jnp.where(flip, 0.5 - size, size)
    square = part * part
    total = jnp.full_like(square, SERIES[-1])
    for factor in SERIES[-2::-1]:
        total = total * square + factor
    return jnp.where(flip, -total, total)


def mode_of(position, modes):
    return jnp.where(position < modes // 2, position, position - modes)


def turns_of(cell, mode, cells, quarter):
    return (cell * mode).astype(jnp.float32) * (1.0 / cells) - 0.25 * quarter.astype(jnp.float32)


def split(index, size):
    high = index // size
    return high, index - high * size


def table_x(cells, modes, mode_axis, columns=None):
    shape = [cells, cells]
    shape[mode_axis] = columns or 2 * modes
    mode, part = split(iota(tuple(shape), mode_axis), 2)
    value = cos_turns(turns_of(iota(tuple(shape), 1 - mode_axis), mode_of(mode, modes), cells, part))
    value = jnp.where(part == 1, -value, value)
    return jnp.where(mode < modes, value, 0.0)


def pair_table(mode, mode_part, cell, cell_part, modes, cells):
    value = cos_turns(turns_of(cell, mode_of(mode, modes), cells, mode_part ^ cell_part))
    return jnp.where((mode_part == 1) & (cell_part == 0), -value, value)


def table_y(cells, modes, mode_axis):
    shape = [2 * cells, 2 * cells]
    shape[mode_axis] = 2 * modes
    mode_part, mode = split(iota(tuple(shape), mode_axis), modes)
    cell_part, cell = split(iota(tuple(shape), 1 - mode_axis), cells)
    return pair_table(mode, mode_part, cell, cell_part, modes, cells)


def table_z(cells, modes, mode_axis, groups, times=1):
    shape = [2 * cells, 2 * cells]
    shape[mode_axis] = 2 * modes * times
    mode_part, mode = split(iota(tuple(shape), mode_axis) // times, modes)
    depth = cells // groups
    group, rest = split(iota(tuple(shape), 1 - mode_axis), 2 * depth)
    cell_part, cell = split(rest, depth)
    return pair_table(mode, mode_part, cell + group * depth, cell_part, modes, cells)


def gelu_slope(values):
    normal_cdf = 0.5 * (1.0 + lax.erf(values * 0.7071067811865476))
    return normal_cdf + values * jnp.exp(-0.5 * values * values) * 0.3989422804014327


def fetch(sources, targets, sems):
    copies = [
        pltpu.make_async_copy(source, target, sems.at[i])
        for i, (source, target) in enumerate(zip(sources, targets))
    ]
    for copy in copies:
        copy.start()
    return copies


def halves(values):
    high = values.astype(jnp.bfloat16)
    return high, (values - high.astype(jnp.float32)).astype(jnp.bfloat16)


def x_kernel(sizes, in_hbm, pre_hbm, cot_hbm, slope_ref, send_ref, ylast_ref, yfirst_ref,
             zlast_ref, zfirst_ref, in_ref, pre_ref, cot_ref, work_ref, half_ref, sems):
    C, zl, yl, dests, kr = sizes
    copies = fetch((in_hbm, pre_hbm, cot_hbm), (in_ref, pre_ref, cot_ref), sems)
    table = table_x(in_ref.shape[1], dests * kr // 2, 1, dests * kr)
    high, low = halves(table)
    both = jnp.concatenate([high, low], axis=1)
    alone = jnp.concatenate([high, jnp.zeros_like(low)], axis=1)

    def transform(f, field):
        upper, lower = halves(field)
        work_ref[f] = dot(upper, both, precision=None) + dot(lower, alone, precision=None)
        for y in range(yl):
            rows = [work_ref[f, pl.ds(z * yl + y, C, stride=zl * yl), :] for z in range(zl)]
            turned = jnp.concatenate(rows, axis=0).T
            turned = turned[: dests * kr] + turned[dests * kr :]
            for d in range(dests):
                send_ref[pl.ds(((d * 2 + f) * yl + y) * kr, kr), :] = turned[d * kr : (d + 1) * kr]

    copies[0].wait()
    transform(0, in_ref[...])
    copies[1].wait()
    copies[2].wait()
    slope = cot_ref[...] * gelu_slope(pre_ref[...])
    slope_ref[...] = slope
    transform(1, slope)
    for half in range(slope_ref.shape[1] // LANES):
        cut = pl.ds(half * LANES, LANES)
        half_ref[...] = slope[:, half * LANES : (half + 1) * LANES]
        for z in range(zl):
            to = pl.ds(z * C, C)
            ylast_ref[to, cut] = half_ref[pl.ds(z * yl + yl - 1, C, stride=zl * yl), :]
            yfirst_ref[to, cut] = half_ref[pl.ds(z * yl, C, stride=zl * yl), :]
    for c in range(C):
        zlast_ref[pl.ds(c * yl, yl), :] = slope_ref[pl.ds((c * zl + zl - 1) * yl, yl), :]
        zfirst_ref[pl.ds(c * yl, yl), :] = slope_ref[pl.ds(c * zl * yl, yl), :]


def widen(values, lanes):
    spare = lanes - values.shape[1]
    if spare == 0:
        return values
    return jnp.concatenate([values, jnp.zeros((values.shape[0], spare), jnp.float32)], axis=1)


def y_kernel(sizes, recv_ref, *refs):
    send_ref = refs[-1]
    C, zl, kxl, ky, kyl, yl, sources = sizes
    kr = 2 * kxl
    lanes = zl * C
    pieces = []
    for kx in range(kxl):
        for f in range(2):
            pieces.append(
                jnp.concatenate(
                    [
                        recv_ref[pl.ds((s * 2 + f) * yl * kr + kx * 2 + r, yl, stride=kr), :]
                        for r in range(2)
                        for s in range(sources)
                    ],
                    axis=0,
                )
            )
    out = dot(table_y(yl * sources, ky, 0), jnp.concatenate(pieces, axis=1))
    for f in range(2):
        for r in range(2):
            for z in range(zl):
                parts = []
                for kx in range(kxl):
                    base = (kx * 2 + f) * lanes + z * C
                    parts.append(out[r * ky : (r + 1) * ky, base : base + C])
                block = widen(jnp.concatenate(parts, axis=1), send_ref.shape[1])
                for g in range(ky // kyl):
                    start = (g * 2 + f) * kyl * 2 * zl + r * zl + z
                    send_ref[pl.ds(start, kyl, stride=2 * zl), :] = block[g * kyl : (g + 1) * kyl]


def spread(rows, C):
    n, kc = rows.shape
    high = rows.astype(jnp.bfloat16).astype(jnp.float32)
    both = jnp.concatenate([high, rows - high], axis=1)
    own = jnp.remainder(iota((C, 2 * kc), 1), C) == iota((C, 2 * kc), 0)
    wide = jnp.where(own[None], jnp.broadcast_to(both[:, None, :], (n, C, 2 * kc)), 0.0)
    wide = wide.reshape(n * C, 2 * kc).astype(jnp.bfloat16)
    same = jnp.remainder(iota((2 * kc, kc), 0), kc) // C == iota((2 * kc, kc), 1) // C
    return dot(wide, same.astype(jnp.bfloat16), precision=None)


def z_kernel(sizes, recv_ref, weights_hbm, part_hbm, send_ref, hat_ref, weights_ref, part_ref,
             each_ref, sems):
    C, zl, kxl, kyl, kz, groups, part_rows, scale = sizes
    copies = fetch(
        (part_hbm, weights_hbm.at[0], weights_hbm.at[1]),
        (part_ref, weights_ref.at[0], weights_ref.at[1]),
        sems,
    )
    forward = table_z(zl * groups, kz, 1, groups).T
    back_table = table_z(zl * groups, kz, 1, groups, SUB)
    kc = kxl * C
    rows = 2 * zl
    chunk = kyl * rows
    wide = send_ref.shape[1]
    cols = []
    for k in range(kyl):
        for f in range(2):
            cols.append(
                jnp.concatenate(
                    [
                        recv_ref[pl.ds((s * 2 + f) * chunk + k * rows, rows), :]
                        for s in range(groups)
                    ],
                    axis=0,
                )
            )
    hat = dot(forward, jnp.concatenate(cols, axis=1))
    for k in range(kyl):
        slope_hat = None
        for f in range(2):
            base = (k * 2 + f) * wide
            value = hat[:, base : base + wide]
            if f == 1:
                value = value * scale
                slope_hat = value[:, :kc]
            for r in range(2):
                hat_ref[pl.ds((f * 2 + r) * kyl + k, kz, stride=4 * kyl), :] = value[
                    r * kz : (r + 1) * kz
                ]
        each_ref[k] = spread(slope_hat, C).reshape(2, kz, C, kc)
    for copy in copies:
        copy.wait()
    duals = []
    for k in range(kyl):
        w_re, w_im = weights_ref[0, k], weights_ref[1, k]
        re = w_re * each_ref[k, 0] + w_im * each_ref[k, 1]
        im = w_re * each_ref[k, 1] - w_im * each_ref[k, 0]
        dual = jnp.stack([re, im]).reshape(2, kz, C // SUB, SUB, kc)
        duals.append(jnp.sum(dual, axis=2).reshape(2 * kz * SUB, kc))
    back = dot(back_table, jnp.concatenate(duals, axis=1))
    for g in range(groups):
        start = g * (chunk + part_rows)
        for k in range(kyl):
            piece = back[g * rows : (g + 1) * rows, k * kc : (k + 1) * kc]
            send_ref[pl.ds(start + k * rows, rows), :] = widen(piece, wide)
        send_ref[pl.ds(start + chunk, part_rows), :] = part_ref[...]


def grad_kernel(sizes, first, hat_ref, *refs):
    C, kxl, kyl, kz, steps = sizes
    out_hbm, out_ref, sems = refs[-3:]
    kc = kxl * C

    def copy(step):
        return pltpu.make_async_copy(
            out_ref.at[step], out_hbm.at[:, first + step], sems.at[step]
        )

    for step in range(steps):
        base = (first + step) * 4 * kyl
        in_re = hat_ref[pl.ds(base, kyl), :][:, :kc]
        in_im = hat_ref[pl.ds(base + kyl, kyl), :][:, :kc]
        wide = spread(hat_ref[pl.ds(base + 2 * kyl, 2 * kyl), :][:, :kc], C)
        wide = wide.reshape(2, kyl, C, kc)
        re, im = wide[0], wide[1]
        grad_re = re * in_re[:, None, :] + im * in_im[:, None, :]
        grad_im = im * in_re[:, None, :] - re * in_im[:, None, :]
        for kx in range(kxl):
            out_ref[step, 0, :, kx] = grad_re[:, :, kx * C : (kx + 1) * C]
            out_ref[step, 1, :, kx] = grad_im[:, :, kx * C : (kx + 1) * C]
        copy(step).start()
    for step in range(steps):
        copy(step).wait()


def y_back_kernel(sizes, recv_ref, *refs):
    send_ref = refs[-1]
    C, zl, kxl, ky, kyl, cells, yl, groups, dests, part_rows = sizes
    wide = recv_ref.shape[1]
    rows = 2 * zl
    kr = 2 * kxl
    chunk = kyl * rows + part_rows
    out_chunk = yl * kr + part_rows
    cols = []
    for z in range(zl):
        cols.append(
            jnp.concatenate(
                [
                    recv_ref[pl.ds(s * chunk + r * zl + z, kyl, stride=rows), :]
                    for r in range(2)
                    for s in range(groups)
                ],
                axis=0,
            )
        )
    out = dot(table_y(cells, ky, 1), jnp.concatenate(cols, axis=1))
    total = recv_ref[pl.ds(kyl * rows, part_rows), :]
    for s in range(1, groups):
        total = total + recv_ref[pl.ds(s * chunk + kyl * rows, part_rows), :]
    for kx in range(kxl):
        for r in range(2):
            block = out[r * cells : (r + 1) * cells]
            piece = jnp.concatenate(
                [block[:, z * wide + kx * C : z * wide + (kx + 1) * C] for z in range(zl)], axis=1
            )
            for d in range(dests):
                send_ref[pl.ds(d * out_chunk + kx * 2 + r, yl, stride=kr), :] = piece[
                    d * yl : (d + 1) * yl
                ]
    for d in range(dests):
        send_ref[pl.ds(d * out_chunk + yl * kr, part_rows), :] = total


def x_back_kernel(sizes, recv_ref, local_ref, fix_ref, out_ref, mix_ref, coef_ref, work_ref):
    C, zl, yl, kxl, sources, part_rows = sizes
    table = table_x(out_ref.shape[1], sources * kxl, 0)
    kr = 2 * kxl
    chunk = yl * kr + part_rows
    edge = 2 * C * yl
    for y in range(yl):
        column = jnp.concatenate(
            [recv_ref[pl.ds(s * chunk + y * kr, kr), :] for s in range(sources)], axis=0
        )
        value = dot(column.T, table)
        if y == 0:
            value = value + fix_ref[pl.ds(edge, zl * C), :]
        if y == yl - 1:
            value = value + fix_ref[pl.ds(edge + zl * C, zl * C), :]
        for z in range(zl):
            for half in range(value.shape[1] // LANES):
                work_ref[half, pl.ds(z * yl + y, C, stride=zl * yl), :] = value[
                    z * C : (z + 1) * C, half * LANES : (half + 1) * LANES
                ]
    for half in range(out_ref.shape[1] // LANES):
        cut = pl.ds(half * LANES, LANES)
        for c in range(C):
            for z in range(zl):
                row = pl.ds((c * zl + z) * yl, yl)
                value = work_ref[half, row, :] + local_ref[row, cut]
                if z == 0:
                    value = value + fix_ref[pl.ds(c * yl, yl), cut]
                if z == zl - 1:
                    value = value + fix_ref[pl.ds((C + c) * yl, yl), cut]
                out_ref[row, cut] = value
    total = recv_ref[pl.ds(yl * kr, part_rows), :]
    for s in range(1, sources):
        total = total + recv_ref[pl.ds(s * chunk + yl * kr, part_rows), :]
    total = total * (1.0 / 1024.0)
    high = C // kxl
    for b in range(kxl):
        mix_ref[pl.ds(b * high, high), :] = total[:high, b * C : (b + 1) * C]
    coef_ref[...] = total[high : high + 5, :C]


EXACT = PRECISION


def one_hot(rows, columns, times, major):
    if rows > columns:
        channel = iota((rows, columns), 0)
        channel = channel // times if major else jnp.remainder(channel, columns)
        return (channel == iota((rows, columns), 1)).astype(jnp.float32)
    channel = iota((rows, columns), 1)
    channel = channel // times if major else jnp.remainder(channel, rows)
    return (channel == iota((rows, columns), 0)).astype(jnp.float32)


def mixer(mix, C, times, major):
    n = C * times
    tall, flat = one_hot(n, C, times, major), one_hot(C, n, times, major)
    full = dot(dot(tall, mix, ((1,), (1,)), EXACT), flat, precision=EXACT)
    if major:
        place = [jnp.remainder(iota((n, n), axis), times) for axis in range(2)]
    else:
        place = [iota((n, n), axis) // C for axis in range(2)]
    return jnp.where(place[0] == place[1], full, 0.0)


def layer(ref, z, C, zl, yl):
    return jnp.concatenate([ref[pl.ds((c * zl + z) * yl, yl), :] for c in range(C)], axis=0)


def inner_kernel(sizes, in_hbm, slope_ref, mix_hbm, coefs_hbm, weights_hbm, out_ref, gram_ref,
                 sums_ref, kron_ref, packed_ref, in_ref, mix_ref, coefs_ref, raw_ref, sems):
    C, zl, yl, kxl, kyl, kz = sizes
    length = in_ref.shape[1]
    copies = fetch((mix_hbm, coefs_hbm, in_hbm), (mix_ref, coefs_ref, in_ref), sems)

    groups = math.gcd(4, kz)
    size = kz // groups

    def raw_copy(g):
        cut = pl.ds(g * size, size)
        return pltpu.make_async_copy(weights_hbm.at[:, cut], raw_ref.at[:, cut], sems.at[3 + g])

    for g in range(groups):
        raw_copy(g).start()

    def up(values):
        cube = values.reshape(C, yl, length)
        return jnp.concatenate(
            [jnp.zeros((C, 1, length), jnp.float32), cube[:, : yl - 1]], axis=1
        ).reshape(C * yl, length)

    def down(values):
        cube = values.reshape(C, yl, length)
        return jnp.concatenate(
            [cube[:, 1:], jnp.zeros((C, 1, length), jnp.float32)], axis=1
        ).reshape(C * yl, length)

    tall = one_hot(C * yl, C, yl, True)
    copies[0].wait()
    copies[1].wait()
    coef_rows = dot(tall, coefs_ref[...], ((1,), (1,)), EXACT)
    coef = [coef_rows[:, j : j + 1] for j in range(5)]
    kron = mixer(mix_ref[...], C, yl, True)
    kron_ref[...] = kron
    slopes = [layer(slope_ref, z, C, zl, yl) for z in range(zl)]
    hidden = [dot(kron, slopes[z]) for z in range(zl)]
    copies[2].wait()
    inputs = [layer(in_ref, z, C, zl, yl) for z in range(zl)]
    gram = None
    sums = [None] * 5
    for z in range(zl):
        shifted = {0: hidden[z], 1: up(hidden[z]), 2: down(hidden[z])}
        if z > 0:
            shifted[3] = hidden[z - 1]
        if z + 1 < zl:
            shifted[4] = hidden[z + 1]
        total = None
        for j, value in shifted.items():
            term = coef[j] * value
            total = term if total is None else total + term
            term = inputs[z] * value
            sums[j] = term if sums[j] is None else sums[j] + term
        for c in range(C):
            out_ref[pl.ds((c * zl + z) * yl, yl), :] = total[c * yl : (c + 1) * yl]
        stencil = coef[0] * inputs[z] + coef[1] * down(inputs[z]) + coef[2] * up(inputs[z])
        if z + 1 < zl:
            stencil = stencil + coef[3] * inputs[z + 1]
        if z > 0:
            stencil = stencil + coef[4] * inputs[z - 1]
        term = dot(slopes[z], stencil, ((1,), (1,)))
        gram = term if gram is None else gram + term
    gram_ref[...] = gram
    columns = []
    for term in sums:
        if term is None:
            columns.append(jnp.zeros((C * yl, 1), jnp.float32))
        else:
            columns.append(jnp.sum(term, axis=1, keepdims=True))
    columns.append(jnp.zeros((C * yl, SUB - 5), jnp.float32))
    sums_ref[...] = jnp.concatenate(columns, axis=1)
    for z in range(kz):
        if z % size == 0:
            raw_copy(z // size).wait()
        for part in range(2):
            for k in range(kyl):
                packed_ref[part, k, z] = jnp.concatenate(
                    [raw_ref[part, z, k, kx] for kx in range(kxl)], axis=1
                )


def edge_kernel(sizes, ybefore_ref, yafter_ref, zbefore_ref, zafter_ref, *refs):
    C, zl, yl, kxl = sizes
    hbms, (fix_ref, part_ref), refs, sems = refs[:6], refs[6:8], refs[8:-1], refs[-1]
    copies = fetch(hbms, refs, sems)
    mix_ref, coefs_ref, kron_ref, in_ref, gram_ref, sums_ref = refs

    def inside(ref, axis, place):
        return ref[...] * (lax.axis_index(axis) != place).astype(jnp.float32)

    last_y, last_z = lax.axis_size("gy") - 1, lax.axis_size("gz") - 1
    zbefore, zafter = inside(zbefore_ref, "gz", 0), inside(zafter_ref, "gz", last_z)
    ybefore, yafter = inside(ybefore_ref, "gy", 0), inside(yafter_ref, "gy", last_y)
    for copy in copies:
        copy.wait()
    kron_y = kron_ref[...]
    kron_z = mixer(mix_ref[...], C, zl, False)
    hidden_zb, hidden_za = dot(kron_y, zbefore), dot(kron_y, zafter)
    hidden_yb, hidden_ya = dot(kron_z, ybefore), dot(kron_z, yafter)
    length = in_ref.shape[1]
    first, last = layer(in_ref, 0, C, zl, yl), layer(in_ref, zl - 1, C, zl, yl)
    layers = [layer(in_ref, z, C, zl, yl) for z in range(zl)]

    def row_of(y):
        return jnp.concatenate([each.reshape(C, yl, length)[:, y] for each in layers], axis=0)

    low, high_row = row_of(0), row_of(yl - 1)
    flat_y, tall_y = one_hot(C, C * yl, yl, True), one_hot(C * yl, C, yl, True)
    flat_z, tall_z = one_hot(C, C * zl, zl, False), one_hot(C * zl, C, zl, False)
    coef_y = dot(tall_y, coefs_ref[...], ((1,), (1,)), EXACT)
    coef_z = dot(tall_z, coefs_ref[...], ((1,), (1,)), EXACT)
    n, m = C * yl, C * zl
    fix_ref[pl.ds(0, n), :] = coef_y[:, 3:4] * hidden_zb
    fix_ref[pl.ds(n, n), :] = coef_y[:, 4:5] * hidden_za
    fix_ref[pl.ds(2 * n, m), :] = coef_z[:, 1:2] * hidden_yb
    fix_ref[pl.ds(2 * n + m, m), :] = coef_z[:, 2:3] * hidden_ya
    gram = gram_ref[...]
    gram = gram + dot(zbefore, coef_y[:, 3:4] * first, ((1,), (1,)))
    gram = gram + dot(zafter, coef_y[:, 4:5] * last, ((1,), (1,)))
    edge = dot(ybefore, coef_z[:, 1:2] * low, ((1,), (1,)))
    edge = edge + dot(yafter, coef_z[:, 2:3] * high_row, ((1,), (1,)))
    same_y = jnp.remainder(iota((n, n), 0), yl) == jnp.remainder(iota((n, n), 1), yl)
    same_z = iota((m, m), 0) // C == iota((m, m), 1) // C
    mix = dot(dot(flat_y, jnp.where(same_y, gram, 0.0)), flat_y, ((1,), (1,)))
    mix = mix + dot(dot(flat_z, jnp.where(same_z, edge, 0.0)), flat_z, ((1,), (1,)))

    def column(values, place):
        total = jnp.sum(values, axis=1, keepdims=True)
        return jnp.where(iota((values.shape[0], SUB), 1) == place, total, 0.0)

    by_y = sums_ref[...] + column(first * hidden_zb, 3) + column(last * hidden_za, 4)
    by_z = column(low * hidden_yb, 1) + column(high_row * hidden_ya, 2)
    by_channel = dot(flat_y, by_y) + dot(flat_z, by_z)
    eye = (iota((SUB, SUB), 0) == iota((SUB, SUB), 1)).astype(jnp.float32)
    coefs = dot(eye, by_channel, ((1,), (1,)))
    high = C // kxl
    packed = jnp.concatenate([mix[b * high : (b + 1) * high] for b in range(kxl)], axis=1)
    part_ref[pl.ds(0, high), :] = widen(packed, part_ref.shape[1])
    part_ref[pl.ds(high, SUB), :] = widen(coefs, part_ref.shape[1])


def per_device(input_field, pre_activation, cotangent, spectral_weights, mix_weights, coefficients):
    C, zl, yl, length = input_field.shape
    groups_y = lax.axis_size("gy")
    groups_z = lax.axis_size("gz")
    cells_y, cells_z = yl * groups_y, zl * groups_z
    kz, kyl, kxl = spectral_weights.shape[1:4]
    modes_y, modes_x = kyl * groups_z, kxl * groups_y
    scale = 1.0 / (length * cells_y * cells_z)
    rows = C * zl * yl
    kr = 2 * kxl
    kc = kxl * C
    lanes = zl * C
    wide = max(kc, LANES)
    part_rows = C // kxl + SUB

    flat = lambda values: values.reshape(rows, length)
    exchange = functools.partial(lax.all_to_all, split_axis=0, concat_axis=0, tiled=True)
    far = pl.BlockSpec(memory_space=pl.ANY)
    near = pl.BlockSpec(memory_space=pltpu.VMEM)

    slope, send, ylast, yfirst, zlast, zfirst = call(
        functools.partial(x_kernel, (C, zl, yl, groups_y, kr)),
        (
            vmem(rows, length),
            f32(groups_y * 2 * yl * kr, lanes),
            far_out(C * zl, length),
            far_out(C * zl, length),
            far_out(C * yl, length),
            far_out(C * yl, length),
        ),
        (
            hbm(flat(input_field)),
            hbm(flat(pre_activation)),
            hbm(flat(cotangent)),
        ),
        24,
        flops=4 * rows * length * 2 * modes_x,
        bytes_accessed=6 * rows * length * 4,
        in_specs=[far] * 3,
        scratch=[
            pltpu.VMEM((rows, length), jnp.float32),
            pltpu.VMEM((rows, length), jnp.float32),
            pltpu.VMEM((rows, length), jnp.float32),
            pltpu.VMEM((2, rows, 4 * modes_x), jnp.float32),
            pltpu.VMEM((rows, LANES), jnp.float32),
            pltpu.SemaphoreType.DMA((3,)),
        ],
    )
    lines = exchange(send, "gy")

    def from_below(values, axis):
        size = lax.axis_size(axis)
        return lax.ppermute(values, axis, [(i, (i + 1) % size) for i in range(size)])

    def from_above(values, axis):
        size = lax.axis_size(axis)
        return lax.ppermute(values, axis, [((i + 1) % size, i) for i in range(size)])

    ybefore, yafter = from_below(ylast, "gy"), from_above(yfirst, "gy")
    zbefore, zafter = from_below(zlast, "gz"), from_above(zfirst, "gz")

    local, gram, sums, kron, weights = call(
        functools.partial(inner_kernel, (C, zl, yl, kxl, kyl, kz)),
        (
            vmem(rows, length),
            far_out(C * yl, C * yl),
            far_out(C * yl, SUB),
            far_out(C * yl, C * yl),
            far_out(2, kyl, kz, C, kc),
        ),
        (
            hbm(flat(input_field)),
            held(slope),
            hbm(mix_weights),
            hbm(coefficients),
            hbm(spectral_weights),
        ),
        44,
        flops=2 * 12 * (C * yl) ** 2 * length,
        bytes_accessed=2 * kz * kyl * kxl * C * 128 * 4 * 2,
        in_specs=[far, near, far, far, far],
        scratch=[
            pltpu.VMEM((rows, length), jnp.float32),
            pltpu.VMEM((C, C), jnp.float32),
            pltpu.VMEM(coefficients.shape, jnp.float32),
            pltpu.VMEM((2, kz, kyl, kxl, C, C), jnp.float32),
            pltpu.SemaphoreType.DMA((3 + math.gcd(4, kz),)),
        ],
    )

    send = call(
        functools.partial(y_kernel, (C, zl, kxl, modes_y, kyl, yl, groups_y)),
        f32(groups_z * 2 * kyl * 2 * zl, wide),
        (lines, held(ybefore), held(yafter), held(zbefore), held(zafter), hbm(weights)),
        16,
        flops=16 * modes_y * cells_y * kxl * lanes,
        bytes_accessed=4 * MIB,
        in_specs=[near] + [far] * 5,
    )
    owned = exchange(send, "gz")

    fix, part = call(
        functools.partial(edge_kernel, (C, zl, yl, kxl)),
        (vmem(2 * C * yl + 2 * C * zl, length), far_out(part_rows, wide)),
        (
            held(ybefore),
            held(yafter),
            held(zbefore),
            held(zafter),
            hbm(mix_weights),
            hbm(coefficients),
            hbm(kron),
            hbm(flat(input_field)),
            hbm(gram),
            hbm(sums),
        ),
        24,
        flops=2 * 6 * (C * yl) ** 2 * length,
        bytes_accessed=3 * MIB,
        in_specs=[near] * 4 + [far] * 6,
        scratch=[
            pltpu.VMEM((C, C), jnp.float32),
            pltpu.VMEM(coefficients.shape, jnp.float32),
            pltpu.VMEM(kron.shape, jnp.float32),
            pltpu.VMEM((rows, length), jnp.float32),
            pltpu.VMEM(gram.shape, jnp.float32),
            pltpu.VMEM(sums.shape, jnp.float32),
            pltpu.SemaphoreType.DMA((6,)),
        ],
    )

    chunk = kyl * 2 * zl + part_rows
    send, hats = call(
        functools.partial(z_kernel, (C, zl, kxl, kyl, kz, groups_z, part_rows, scale)),
        (f32(groups_z * chunk, wide), vmem(kz * 4 * kyl, wide)),
        (owned, hbm(weights), hbm(part)),
        24,
        flops=16 * kz * kyl * C * kc,
        bytes_accessed=6 * MIB,
        in_specs=[near, far, far],
        scratch=[
            pltpu.VMEM((2, kyl, kz, C, kc), jnp.float32),
            pltpu.VMEM((part_rows, wide), jnp.float32),
            pltpu.VMEM((kyl, 2, kz, C, kc), jnp.float32),
            pltpu.SemaphoreType.DMA((3,)),
        ],
    )
    returned = exchange(send, "gz")

    def gradient(first, steps, *before):
        return call(
            functools.partial(grad_kernel, (C, kxl, kyl, kz, steps), first),
            pltpu.HBM((2, kz, kyl, kxl, C, C), jnp.float32),
            (held(hats), *[hbm(each) for each in before]),
            16,
            flops=16 * steps * kyl * C * kc,
            bytes_accessed=2 * steps * kyl * kxl * C * 128 * 4,
            in_specs=[near] + [far] * len(before),
            out_specs=far,
            scratch=[
                pltpu.VMEM((steps, 2, kyl, kxl, C, C), jnp.float32),
                pltpu.SemaphoreType.DMA((steps,)),
            ],
            input_output_aliases={1: 0} if before else {},
        )

    few = max(1, kz * 7 // 16)
    grad_half = gradient(0, few)

    send = call(
        functools.partial(
            y_back_kernel,
            (C, zl, kxl, modes_y, kyl, cells_y, yl, groups_z, groups_y, part_rows),
        ),
        f32(groups_y * (yl * kr + part_rows), lanes),
        (returned, hbm(grad_half)),
        16,
        flops=8 * modes_y * cells_y * kxl * lanes,
        bytes_accessed=2 * MIB,
        in_specs=[near, far],
    )
    arrived = exchange(send, "gy")
    grad_spectral = gradient(few, kz - few, grad_half)

    grad_input, grad_mix, grad_coef = call(
        functools.partial(x_back_kernel, (C, zl, yl, kxl, groups_y, part_rows)),
        (f32(rows, length), f32(C, C), f32(5, C)),
        (arrived, held(local), held(fix)),
        16,
        flops=2 * rows * length * 2 * modes_x,
        bytes_accessed=3 * MIB,
        scratch=[pltpu.VMEM((length // LANES, rows, LANES), jnp.float32)],
    )
    return (grad_input.reshape(input_field.shape), grad_spectral, grad_mix, grad_coef)


def solution(mesh):
    in_specs = (
        P(None, "gz", "gy", None),
        P(None, "gz", "gy", None),
        P(None, "gz", "gy", None),
        P(None, None, "gz", "gy", None, None),
        P(),
        P(),
    )
    out_specs = (P(None, "gz", "gy", None), P(None, None, "gz", "gy", None, None), P(), P())
    return jax.shard_map(
        per_device, mesh=mesh, in_specs=in_specs, out_specs=out_specs, check_vma=False
    )
```
